32 devices in a mesh: dp: 8 (over z, x), mp: 4 (over y, core).
Axes of the slice: x: 2, y: 2, z: 4, core: 2. Of those that a mesh axis runs over, the one named last changes fastest.
Arguments:
- tokens: bfloat16 [4096, 1024], P(('dp', 'mp')), may hold values from -6 to 6
- gain_attn: float32 [1024], replicated, may hold values from 0.5 to 1.5
- w_query: bfloat16 [1024, 1024], P(None, 'mp'), may hold values from -0.0234375 to 0.0234375
- w_key: bfloat16 [1024, 1024], P(None, 'mp'), may hold values from -0.1875 to 0.1875
- w_value: bfloat16 [1024, 1024], P(None, 'mp'), may hold values from -0.1875 to 0.1875
- w_output: bfloat16 [1024, 1024], P('mp'), may hold values from -1 to 1
- rel_bias: float32 [32, 16], P(None, 'mp'), may hold values from -4 to 4
- bucket_table: int32 [512, 512], replicated, may hold values from 0 to 31
- gain_moe: float32 [1024], replicated, may hold values from 0.5 to 1.5
- router: float32 [1024, 16], replicated, may hold values from -0.09375 to 0.09375
- w_in: bfloat16 [16, 1024, 2816], P('dp', None, 'mp'), may hold values from -0.1875 to 0.1875
- w_out: bfloat16 [16, 2816, 1024], P('dp', 'mp'), may hold values from -1.75 to 1.75
- routes: int32 [4096], P(('dp', 'mp')), may hold values from 0 to 15
- slots: int32 [4096], P(('dp', 'mp')), may hold values from 0 to 10, as said below
- cotangent: bfloat16 [4096, 1024], P(('dp', 'mp')), may hold values from -6 to 6
Outputs:
- block_out: bfloat16 [4096, 1024], P(('dp', 'mp'))
- input_grad: bfloat16 [4096, 1024], P(('dp', 'mp'))
- grad_gain_attn: float32 [1024], replicated
- grad_w_query: float32 [1024, 1024], P(None, 'mp')
- grad_w_key: float32 [1024, 1024], P(None, 'mp')
- grad_w_value: float32 [1024, 1024], P(None, 'mp')
- grad_w_output: float32 [1024, 1024], P('mp')
- grad_rel_bias: float32 [32, 16], P(None, 'mp')
- grad_gain_moe: float32 [1024], replicated
- grad_router: float32 [1024, 16], replicated
- grad_w_in: float32 [16, 1024, 2816], P('dp', None, 'mp')
- grad_w_out: float32 [16, 2816, 1024], P('dp', 'mp')
The draws below stay inside these ranges and needn't reach their ends.
Inputs may be any that keep to these rules, and one draw needn't show every extreme that they name: slots[t] is the number of earlier tokens of the same device (aligned block of 128 tokens) with the same route, or 10 where that number is 10 or more (the token is dropped).
All inputs are finite; a program needn't handle non-finite values.
Results may differ from the reference program's by a relative error of at most 0.023.
Values may be sent and summed in bfloat16 or wider, within the bound.
No kernel may reach another device: no remote copies, remote signals or barrier semaphores. Data moves between devices by JAX's collectives and lax.ppermute only.
A program may use at most 128 MiB of HBM per device.

```python
import jax
import jax.numpy as jnp
from jax import lax

D = 1024
H = 16
HD = 64
FF = 2816
NB = 32
SEQ = 512
TOK_DEV = 128
SOURCES = 32
EXPERTS = 16
CAP = 10
TOKENS = 4096
N_MP = 4


def route_plan(key):
    base_key = jax.random.fold_in(key, 17)
    hot_key, pick_key, order_key = jax.random.split(base_key, 3)
    block_count = TOKENS // TOK_DEV
    hot_expert = jax.random.randint(hot_key, (), 0, EXPERTS)
    picked = jax.random.randint(pick_key, (block_count, TOK_DEV), 0, EXPERTS)

    def shuffle(sub_key):
        return jax.random.permutation(sub_key, TOK_DEV)
    orders = jax.vmap(shuffle)(jax.random.split(order_key, block_count))
    chosen = jnp.where(orders <= CAP, hot_expert, picked).astype(jnp.int32)
    labels = jnp.arange(EXPERTS, dtype=jnp.int32)
    matches = (chosen[:, :, None] == labels[None, None, :]).astype(jnp.int32)
    earlier = jnp.cumsum(matches, axis=1) - matches
    ranking = jnp.sum(earlier * matches, axis=2)
    placed = jnp.minimum(ranking, CAP).astype(jnp.int32)
    return (chosen.reshape(-1), placed.reshape(-1))


def draw_routes(key, part):
    return route_plan(key)[0]


def draw_slots(key, part):
    return route_plan(key)[1]


def plant(values, key, least, top_value):
    index_at = [jax.random.randint(jax.random.fold_in(key, axis), (), 0, length) for axis, length in enumerate(values.shape)]
    main_axis = values.shape.index(max(values.shape))
    neighbour = index_at[:main_axis] + [(index_at[main_axis] + 1) % values.shape[main_axis]] + index_at[main_axis + 1:]
    return values.at[tuple(index_at)].set(least).at[tuple(neighbour)].set(top_value)


def block_levels(stream_key, shape, cuts, least, high):
    level, own = 1.0, jax.random.fold_in(stream_key, 6)
    for dim, parts in cuts:
        draws = jnp.exp(jax.random.uniform(jax.random.fold_in(own, dim), (parts,), jnp.float32, least / len(cuts), high / len(cuts)))
        level = level * jnp.repeat(draws, shape[dim] // parts).reshape([-1 if axis == dim else 1 for axis in range(len(shape))])
    return level


def scatter_about(key, shape, deviation, limit, cuts=(), kind=jnp.bfloat16):
    values = jax.random.normal(key, shape, jnp.float32) * deviation
    if len(cuts) > 0:
        values = block_levels(key, shape, cuts, -0.22, 0.18) * values
    return jnp.clip(values, min=-limit, max=limit).astype(kind)


def setup_inputs(seed: int = 0) -> dict:
    streams_of = jax.random.split(jax.random.key(seed), 16)
    return {
        "tokens": scatter_about(streams_of[0], (TOKENS, D), 1.0, 6.0, ((0, 32),)),
        "gain_attn": jnp.clip(1.0 + 0.1 * jax.random.normal(streams_of[1], (D,), jnp.float32), 0.5, 1.5),
        "w_query": scatter_about(streams_of[2], (D, H * HD), (D * HD) ** -0.5, 0.0234375, ((1, 4),)),
        "w_key": scatter_about(streams_of[3], (D, H * HD), D ** -0.5, 0.1875, ((1, 4),)),
        "w_value": scatter_about(streams_of[4], (D, H * HD), D ** -0.5, 0.1875, ((1, 4),)),
        "w_output": scatter_about(streams_of[5], (H * HD, D), (H * HD // 32) ** -0.5, 1.0, ((0, 4),)),
        "rel_bias": scatter_about(streams_of[6], (NB, H), 1.0, 4.0, ((1, 4),), jnp.float32),
        "bucket_table": plant(jax.random.randint(streams_of[7], (SEQ, SEQ), 0, NB), jax.random.fold_in(streams_of[7], 1), 0, NB - 1).astype(jnp.int32),
        "gain_moe": jnp.clip(1.0 + 0.1 * jax.random.normal(streams_of[8], (D,), jnp.float32), 0.5, 1.5),
        "router": scatter_about(streams_of[9], (D, EXPERTS), (4 * D) ** -0.5, 0.09375, (), jnp.float32),
        "w_in": scatter_about(streams_of[10], (EXPERTS, D, FF), D ** -0.5, 0.1875, ((0, 8), (2, 4))),
        "w_out": scatter_about(streams_of[11], (EXPERTS, FF, D), (max(1, FF // (EXPERTS * EXPERTS))) ** -0.5, 1.75, ((0, 8), (1, 4))),
        "routes": draw_routes(jax.random.fold_in(streams_of[15], 71), 0),
        "slots": draw_slots(jax.random.fold_in(streams_of[15], 71), 0),
        "cotangent": scatter_about(streams_of[14], (TOKENS, D), 1.0, 6.0, ((0, 32),)),
    }


@jax.custom_vjp
def low(v):
    return lax.optimization_barrier(v.astype(jnp.bfloat16)).astype(jnp.float32)

@jax.custom_vjp
def low_back(v):
    return v

def low_keep(v):
    return (low(v), None)

def low_pass(kept, grad):
    return (grad,)

def back_keep(v):
    return (v, None)

def back_low(kept, grad):
    return (low(grad),)
low.defvjp(low_keep, low_pass)
low_back.defvjp(back_keep, back_low)
norm_eps = 1e-06
highest = lax.Precision.HIGHEST

def rms_norm(values, gain):
    return values * lax.rsqrt(lax.optimization_barrier(jnp.mean(values * values, axis=-1, keepdims=True)) + norm_eps) * gain

def matmul(left, right):
    return jnp.dot(left, right, precision=highest, preferred_element_type=jnp.float32)

def attend_block(queries, keys, values, bias):
    scores = low_back(jnp.einsum('nqhd,nkhd->nhqk', queries, keys, precision=highest) + bias)
    probs = jax.nn.softmax(scores, axis=-1)
    return jnp.einsum('nhqk,nkhd->nqhd', low(probs), values, precision=highest)

def reference(tokens, gain_attn, w_query, w_key, w_value, w_output, rel_bias, bucket_table, gain_moe, router, w_in, w_out, routes, slots, cotangent):
    anchor = (jnp.arange(TOKENS, dtype=jnp.int32) // TOK_DEV).astype(jnp.int32)
    kept = slots < CAP
    all_slots = EXPERTS * SOURCES * CAP
    target = jnp.where(kept, routes * (SOURCES * CAP) + anchor * CAP + slots, all_slots).astype(jnp.int32)
    safe_target = jnp.minimum(target, all_slots - 1).astype(jnp.int32)
    kept_f = kept.astype(jnp.float32)
    token_ids = jnp.arange(TOKENS, dtype=jnp.int32)
    owner_plus = jax.ops.segment_sum((token_ids + 1).astype(jnp.int32), target, num_segments=all_slots + 1).astype(jnp.int32)
    owner = owner_plus[:all_slots].astype(jnp.int32)
    has_owner = (owner > 0).astype(jnp.float32)
    owner_index = jnp.maximum(owner - 1, 0).astype(jnp.int32)
    per_block = N_MP * TOK_DEV // SEQ
    blocks = TOKENS // (per_block * SEQ)

    def forward(residual, gain_one, query_w, key_w, value_w, output_w, table_bias, gain_two, router_w, expert_in, expert_out):
        normed = low(rms_norm(residual, gain_one))
        queries = low_back(low(matmul(normed, query_w))).reshape(blocks, per_block, SEQ, H, HD)
        keys = low_back(low(matmul(normed, key_w))).reshape(blocks, per_block, SEQ, H, HD)
        values = low_back(low(matmul(normed, value_w))).reshape(blocks, per_block, SEQ, H, HD)
        bias = jnp.transpose(table_bias[bucket_table], (2, 0, 1))

        def one_block(item):
            return attend_block(item[0], item[1], item[2], bias)
        mixed = lax.map(jax.checkpoint(one_block), (queries, keys, values))
        mixed = low_back(low(mixed.reshape(TOKENS, H * HD)))
        attn = low_back(matmul(mixed, output_w))
        middle = residual + attn
        normed_two = low(rms_norm(middle, gain_two))
        probs = jax.nn.softmax(matmul(normed_two, router_w), axis=-1)
        gate_prob = jnp.take_along_axis(probs, routes[:, None], axis=1)[:, 0]
        buffer = normed_two[owner_index] * has_owner[:, None]
        rows_in = low_back(buffer).reshape(EXPERTS, SOURCES * CAP, D)
        pre = low_back(jnp.einsum('esd,edf->esf', rows_in, expert_in, precision=highest))
        hidden = low_back(low(jax.nn.gelu(pre, approximate=True)))
        produced = low_back(low(jnp.einsum('esf,efd->esd', hidden, expert_out, precision=highest))).reshape(all_slots, D)
        combined = produced[safe_target] * kept_f[:, None]
        return middle + gate_prob[:, None] * combined
    result, pullback = jax.vjp(forward, tokens.astype(jnp.float32), gain_attn.astype(jnp.float32), w_query.astype(jnp.float32), w_key.astype(jnp.float32), w_value.astype(jnp.float32), w_output.astype(jnp.float32), rel_bias.astype(jnp.float32), gain_moe.astype(jnp.float32), router.astype(jnp.float32), w_in.astype(jnp.float32), w_out.astype(jnp.float32))
    grads = pullback(cotangent.astype(jnp.float32))
    return (result.astype(jnp.bfloat16), grads[0].astype(jnp.bfloat16), grads[1], grads[2], grads[3], grads[4], grads[5], grads[6], grads[7], grads[8], grads[9], grads[10])
```

```python
import functools

import jax
import jax.numpy as jnp
import numpy as np
from jax import lax
from jax.experimental import pallas as pl
from jax.experimental.pallas import tpu as pltpu
from jax.sharding import PartitionSpec as P

norm_eps = 1e-06
highest = lax.Precision.HIGHEST
bf16 = jnp.bfloat16
f32 = jnp.float32
LANES = 128
MIB = 1 << 20


def swap(block, axis, offset):
    size = lax.axis_size(axis)
    return lax.ppermute(block, axis, [(i, i ^ offset) for i in range(size)])


def bit_count(axis):
    return lax.axis_size(axis).bit_length() - 1


def gather_members(block):
    held = block[None]
    for bit in reversed(range(bit_count("mp"))):
        other = swap(held, "mp", 1 << bit)
        held = jnp.stack([held, other], axis=1).reshape((-1,) + block.shape)
    return held


def scatter_pairs(keep, received, first_bit):
    held = keep.astype(f32) + received.astype(f32)
    for bit in range(first_bit, bit_count("mp")):
        halves = held.reshape((-1, 2) + held.shape[1:])
        got = swap(halves[:, 1].astype(bf16), "mp", 1 << bit)
        held = halves[:, 0] + got.astype(f32)
    return held[0]


def exchange_groups(chunks):
    got = [chunks[0]] + [swap(chunks[k], "dp", k) for k in range(1, len(chunks))]
    return jnp.concatenate(got, axis=0)


def sum_groups(part):
    me = lax.axis_index("dp")
    bits = bit_count("dp")
    held = part
    for bit in range(bits):
        halves = held.reshape((2, held.shape[0] // 2) + held.shape[1:])
        mine = (me >> bit) & 1
        send = lax.dynamic_index_in_dim(halves, 1 - mine, 0, keepdims=False)
        keep = lax.dynamic_index_in_dim(halves, mine, 0, keepdims=False)
        got = swap(send, "dp", 1 << bit)
        held = (keep.astype(f32) + got.astype(f32)).astype(bf16)
    held = held[None]
    for bit in reversed(range(bits)):
        other = swap(held, "dp", 1 << bit)
        held = jnp.concatenate([held, other], axis=0)
    size = 1 << bits
    offset_of = np.zeros(size, np.int64)
    for index in range(size):
        for step, bit in enumerate(reversed(range(bits))):
            if (index >> step) & 1:
                offset_of[index] |= 1 << bit
    index_of = np.argsort(offset_of)
    blocks = []
    my_block = jnp.int32(0)
    for bit in range(bits):
        my_block = my_block | (((me >> bit) & 1) << (bits - 1 - bit))
    reverse = np.array([sum(((q >> bit) & 1) << (bits - 1 - bit) for bit in range(bits)) for q in range(size)])
    place = jnp.asarray(index_of[reverse], jnp.int32)
    for q in range(size):
        blocks.append(lax.dynamic_index_in_dim(held, place[jnp.int32(q) ^ my_block], 0, keepdims=False))
    return jnp.concatenate(blocks, axis=0)


def sum_all(part, axes):
    held = part
    for axis in axes:
        for bit in range(bit_count(axis)):
            held = held + swap(held, axis, 1 << bit)
    return held


def bias_kernel(shift_ref, table_ref, bucket_ref, bias_ref, moved_ref):
    labels = table_ref[...]
    moved_ref[...] = labels
    for head in range(bucket_ref.shape[0]):
        row = jnp.broadcast_to(bucket_ref[head : head + 1, :], labels.shape)
        bias_ref[head] = jnp.take_along_axis(row, labels, axis=1, mode="promise_in_bounds")


def make_bias(table, bucket_rows, shift, block):
    seq_len = table.shape[0]
    heads = bucket_rows.shape[0]
    blocks = seq_len // block
    return pl.pallas_call(
        bias_kernel,
        grid_spec=pltpu.PrefetchScalarGridSpec(
            num_scalar_prefetch=1,
            grid=(blocks, blocks),
            in_specs=[
                pl.BlockSpec((block, block), lambda i, j, s: (i ^ s[0], j ^ s[0])),
                pl.BlockSpec((heads, LANES), lambda i, j, s: (0, 0)),
            ],
            out_specs=[
                pl.BlockSpec((heads, block, block), lambda i, j, s: (0, i, j)),
                pl.BlockSpec((block, block), lambda i, j, s: (i, j)),
            ],
        ),
        out_shape=[
            jax.ShapeDtypeStruct((heads, seq_len, seq_len), f32),
            jax.ShapeDtypeStruct((seq_len, seq_len), jnp.int32),
        ],
        cost_estimate=pl.CostEstimate(
            flops=seq_len * seq_len * heads, bytes_accessed=4 * seq_len * seq_len * (heads + 2), transcendentals=0
        ),
        name="bias_lookup",
    )(shift, table, bucket_rows)


def bucket_kernel(buckets, table_ref, grad_ref, out_ref):
    seqs, heads, rows, seq_len = grad_ref.shape

    @pl.when(pl.program_id(0) == 0)
    def _():
        out_ref[...] = jnp.zeros_like(out_ref)

    labels = lax.broadcasted_iota(jnp.int32, (rows, buckets, seq_len), 1)
    onehot = (table_ref[...][:, None, :] == labels).astype(f32).astype(bf16).reshape(rows * buckets, seq_len)
    total = jnp.zeros((rows * buckets, heads * rows), f32)
    for seq in range(seqs):
        grads = grad_ref[seq].reshape(heads * rows, seq_len)
        total += lax.dot_general(onehot, grads, (((1,), (1,)), ((), ())), preferred_element_type=f32)
    own_row = lax.broadcasted_iota(jnp.int32, (rows, buckets, heads * rows), 0)
    its_row = lax.broadcasted_iota(jnp.int32, (rows, buckets, heads * rows), 2) % rows
    kept = jnp.where(own_row == its_row, total.reshape(rows, buckets, heads * rows), 0.0)
    out_ref[...] += jnp.sum(kept, axis=0)


def bucket_grad(table, score_grad, buckets):
    seqs, heads, seq_len, _ = score_grad.shape
    rows = 32
    out = pl.pallas_call(
        functools.partial(bucket_kernel, buckets),
        grid=(seq_len // rows,),
        in_specs=[
            pl.BlockSpec((rows, seq_len), lambda i: (i, 0)),
            pl.BlockSpec((seqs, heads, rows, seq_len), lambda i: (0, 0, i, 0)),
        ],
        out_specs=pl.BlockSpec((buckets, heads * rows), lambda i: (0, 0)),
        out_shape=jax.ShapeDtypeStruct((buckets, heads * rows), f32),
        compiler_params=pltpu.CompilerParams(vmem_limit_bytes=32 * MIB),
        cost_estimate=pl.CostEstimate(
            flops=2 * seqs * seq_len * buckets * seq_len * heads * rows,
            bytes_accessed=2 * seqs * heads * seq_len * seq_len + 4 * seq_len * seq_len,
            transcendentals=0,
        ),
        name="bucket_grad",
    )(table, score_grad)
    return jnp.sum(out.reshape(buckets, heads, rows), axis=2)


def attend_kernel(head_size, joined_ref, bias_ref, mixed_ref, probs_ref):
    seq_len, width = joined_ref.shape
    head_cols = width // 3
    pair_heads = bias_ref.shape[0]
    pair_cols = pair_heads * head_size
    start = pl.program_id(1) * pair_cols
    columns = [
        joined_ref[:, pl.ds(pl.multiple_of(start + part * head_cols, pair_cols), pair_cols)] for part in range(3)
    ]
    rows = min(128, seq_len)
    for chunk in range(seq_len // rows):
        picked = slice(chunk * rows, (chunk + 1) * rows)
        outs = []
        for head in range(pair_heads):
            cols = slice(head * head_size, (head + 1) * head_size)
            scores = lax.dot_general(
                columns[0][picked, cols], columns[1][:, cols], (((1,), (1,)), ((), ())), preferred_element_type=f32
            )
            scores = scores + bias_ref[head, picked, :]
            expo = jnp.exp(scores - jnp.max(scores, axis=-1, keepdims=True))
            probs = expo / jnp.sum(expo, axis=-1, keepdims=True)
            probs_ref[0, head, picked, :] = probs
            outs.append(jnp.dot(probs.astype(bf16), columns[2][:, cols], preferred_element_type=f32))
        mixed_ref[picked, :] = jnp.concatenate(outs, axis=1).astype(bf16)


def attend(joined, bias, head_size):
    heads, seq_len, _ = bias.shape
    tokens, width = joined.shape
    seqs = tokens // seq_len
    head_cols = width // 3
    pair = min(heads, LANES // head_size)
    return pl.pallas_call(
        functools.partial(attend_kernel, head_size),
        grid=(seqs, heads // pair),
        in_specs=[
            pl.BlockSpec((seq_len, width), lambda s, h: (s, 0)),
            pl.BlockSpec((pair, seq_len, seq_len), lambda s, h: (h, 0, 0)),
        ],
        out_specs=[
            pl.BlockSpec((seq_len, pair * head_size), lambda s, h: (s, h)),
            pl.BlockSpec((1, pair, seq_len, seq_len), lambda s, h: (s, h, 0, 0)),
        ],
        out_shape=[
            jax.ShapeDtypeStruct((tokens, head_cols), bf16),
            jax.ShapeDtypeStruct((seqs, heads, seq_len, seq_len), f32),
        ],
        compiler_params=pltpu.CompilerParams(vmem_limit_bytes=32 * MIB),
        cost_estimate=pl.CostEstimate(
            flops=4 * seqs * heads * seq_len * seq_len * head_size,
            bytes_accessed=8 * seqs * heads * seq_len * seq_len,
            transcendentals=seqs * heads * seq_len * seq_len,
        ),
        name="attend",
    )(joined, bias)


def attend_back_kernel(head_size, joined_ref, grad_ref, probs_ref, out_ref, score_ref):
    seq_len, width = joined_ref.shape
    head_cols = width // 3
    pair_heads = probs_ref.shape[1]
    pair_cols = pair_heads * head_size
    start = pl.program_id(1) * pair_cols

    def place(part):
        return pl.ds(pl.multiple_of(start + part * head_cols, pair_cols), pair_cols)

    queries, keys, values = [joined_ref[:, place(part)] for part in range(3)]
    grads = grad_ref[...]
    queries_t, grads_t = queries.T, grads.T
    rows = min(128, seq_len)
    query_parts = []
    key_t = [jnp.zeros((head_size, seq_len), f32) for _ in range(pair_heads)]
    value_t = [jnp.zeros((head_size, seq_len), f32) for _ in range(pair_heads)]
    for chunk in range(seq_len // rows):
        picked = slice(chunk * rows, (chunk + 1) * rows)
        outs = []
        for head in range(pair_heads):
            cols = slice(head * head_size, (head + 1) * head_size)
            probs = probs_ref[0, head, picked, :]
            prob_grad = lax.dot_general(
                grads[picked, cols], values[:, cols], (((1,), (1,)), ((), ())), preferred_element_type=f32
            )
            weighted = jnp.sum(probs * prob_grad, axis=-1, keepdims=True)
            score_grad = (probs * (prob_grad - weighted)).astype(bf16)
            score_ref[0, head, picked, :] = score_grad
            outs.append(jnp.dot(score_grad, keys[:, cols], preferred_element_type=f32))
            key_t[head] += jnp.dot(queries_t[cols, picked], score_grad, preferred_element_type=f32)
            value_t[head] += jnp.dot(grads_t[cols, picked], probs.astype(bf16), preferred_element_type=f32)
        out_ref[picked, place(0)] = jnp.concatenate(outs, axis=1).astype(bf16)
    out_ref[:, place(1)] = jnp.concatenate(key_t, axis=0).T.astype(bf16)
    out_ref[:, place(2)] = jnp.concatenate(value_t, axis=0).T.astype(bf16)


def attend_back(joined, mixed_grad, probs, head_size):
    seqs, heads, seq_len, _ = probs.shape
    tokens, width = joined.shape
    pair = min(heads, LANES // head_size)
    return pl.pallas_call(
        functools.partial(attend_back_kernel, head_size),
        grid=(seqs, heads // pair),
        in_specs=[
            pl.BlockSpec((seq_len, width), lambda s, h: (s, 0)),
            pl.BlockSpec((seq_len, pair * head_size), lambda s, h: (s, h)),
            pl.BlockSpec((1, pair, seq_len, seq_len), lambda s, h: (s, h, 0, 0)),
        ],
        out_specs=[
            pl.BlockSpec((seq_len, width), lambda s, h: (s, 0)),
            pl.BlockSpec((1, pair, seq_len, seq_len), lambda s, h: (s, h, 0, 0)),
        ],
        out_shape=[
            jax.ShapeDtypeStruct((tokens, width), bf16),
            jax.ShapeDtypeStruct((seqs, heads, seq_len, seq_len), bf16),
        ],
        compiler_params=pltpu.CompilerParams(vmem_limit_bytes=32 * MIB),
        cost_estimate=pl.CostEstimate(
            flops=8 * seqs * heads * seq_len * seq_len * head_size,
            bytes_accessed=6 * seqs * heads * seq_len * seq_len,
            transcendentals=0,
        ),
        name="attend_back",
    )(joined, mixed_grad, probs)


def root_inverse(values):
    return lax.rsqrt(jnp.mean(values * values, axis=-1, keepdims=True) + norm_eps)


gelu_scale = float(np.sqrt(2.0 / np.pi))


def gelu_parts(pre):
    bent = jnp.tanh(gelu_scale * (pre + 0.044715 * pre * pre * pre))
    return 0.5 * pre * (1.0 + bent), bent


def gelu_slope(pre, bent):
    return 0.5 * (1.0 + bent) + 0.5 * pre * (1.0 - bent * bent) * gelu_scale * (1.0 + 0.134145 * pre * pre)


def shards(
    tokens,
    gain_attn,
    w_query,
    w_key,
    w_value,
    w_output,
    rel_bias,
    bucket_table,
    gain_moe,
    router,
    w_in,
    w_out,
    routes,
    slots,
    cotangent,
):
    group_count = lax.axis_size("dp")
    member_count = lax.axis_size("mp")
    group = lax.axis_index("dp")
    member = lax.axis_index("mp")
    tok_dev, width = tokens.shape
    expert_local = w_in.shape[0]
    expert_count = expert_local * group_count
    capacity = max(2, (5 * tok_dev + 4 * expert_count - 1) // (4 * expert_count))
    seq_len = bucket_table.shape[0]
    head_cols = w_query.shape[1]
    head_local = rel_bias.shape[1]
    head_size = head_cols // head_local
    group_tokens = tok_dev * member_count
    seq_members = seq_len // tok_dev

    all_tokens = gather_members(tokens).reshape(group_tokens, width).astype(f32)
    bucket_rows = jnp.pad(rel_bias.T, ((0, 0), (0, LANES - rel_bias.shape[0])))
    shift = (member % seq_members).astype(jnp.int32)[None]
    bias, moved_table = make_bias(bucket_table, bucket_rows, shift, tok_dev)
    w_joined = jnp.concatenate([w_query, w_key, w_value], axis=1)
    unit_attn = all_tokens * root_inverse(all_tokens)
    normed_low = (unit_attn * gain_attn).astype(bf16)
    joined = jnp.dot(normed_low, w_joined, preferred_element_type=f32).astype(bf16)
    mixed, probs = attend(joined, bias, head_size)
    mixed_pairs = mixed.reshape(member_count // 2, 2, tok_dev, head_cols)

    def project(rows):
        return jnp.einsum("stc,cd->std", rows, w_output, preferred_element_type=f32)

    attn_got = swap(project(mixed_pairs[:, 1]).astype(bf16), "mp", 1)
    attn = scatter_pairs(project(mixed_pairs[:, 0]), attn_got, 1)
    middle = tokens.astype(f32) + attn

    middle_root = root_inverse(middle)
    unit_moe = middle * middle_root
    moe_low = (unit_moe * gain_moe).astype(bf16)
    moe_rows = moe_low.astype(f32)
    router_t = router.T
    logits = lax.dot_general(
        moe_rows, router_t, (((1,), (1,)), ((), ())), precision=highest, preferred_element_type=f32
    )
    router_probs = jax.nn.softmax(logits, axis=-1)
    route_hot = (routes[:, None] == jnp.arange(expert_count, dtype=jnp.int32)[None, :]).astype(f32)
    gate_prob = jnp.sum(router_probs * route_hot, axis=-1, keepdims=True)

    chunk_slots = expert_local * capacity
    cuts = 1
    while cuts * chunk_slots % 8 != 0:
        cuts *= 2
    piece = width // cuts
    chunk_rows = cuts * chunk_slots
    all_rows = group_count * chunk_rows
    row_index = jnp.arange(all_rows, dtype=jnp.int32)
    row_chunk, row_cut, row_slot = (
        row_index // chunk_rows,
        (row_index // chunk_slots) % cuts,
        row_index % chunk_slots,
    )
    near = routes ^ (group * expert_local)
    target = jnp.where(slots < capacity, near * capacity + slots, -1)
    wanted = row_chunk * chunk_slots + row_slot
    hit = (wanted[:, None, None] == target[None, None, :]) & (
        row_cut[:, None, None] == jnp.arange(cuts, dtype=jnp.int32)[None, :, None]
    )
    placement = hit.astype(bf16).reshape(all_rows, cuts * tok_dev)

    def cut_rows(rows):
        return jnp.concatenate([rows[:, c * piece : (c + 1) * piece] for c in range(cuts)], axis=0)

    def join_rows(rows):
        return jnp.concatenate([rows[c * tok_dev : (c + 1) * tok_dev] for c in range(cuts)], axis=1)

    def dispatch(rows):
        buffer = jnp.dot(placement, cut_rows(rows), preferred_element_type=f32).astype(bf16)
        chunks = [buffer[k * chunk_rows : (k + 1) * chunk_rows] for k in range(group_count)]
        return gather_members(exchange_groups(chunks))

    def collect(blocks):
        pairs = blocks.reshape(member_count // 2, 2, all_rows, piece)
        got = swap(pairs[:, 1], "mp", 1)
        summed = scatter_pairs(pairs[:, 0], got, 1).astype(bf16)
        back = exchange_groups([summed[k * chunk_rows : (k + 1) * chunk_rows] for k in range(group_count)])
        rows = lax.dot_general(placement, back, (((0,), (0,)), ((), ())), preferred_element_type=f32)
        return join_rows(rows)

    order = np.arange(all_rows).reshape(group_count, cuts, expert_local, capacity).transpose(1, 2, 0, 3).reshape(-1)
    sorting = jnp.asarray(np.eye(all_rows, dtype=np.float32)[order], bf16)
    expert_rows = group_count * capacity

    def sort_rows(blocks):
        moved = jnp.einsum("rq,sqw->srw", sorting, blocks, preferred_element_type=f32).astype(bf16)
        moved = moved.reshape(member_count, cuts, expert_local, expert_rows, piece)
        return jnp.transpose(moved, (2, 0, 3, 1, 4)).reshape(expert_local, member_count * expert_rows, width)

    def unsort_rows(rows):
        moved = rows.reshape(expert_local, member_count, expert_rows, cuts, piece)
        moved = jnp.transpose(moved, (1, 3, 0, 2, 4)).reshape(member_count, all_rows, piece)
        return jnp.einsum("rq,srw->sqw", sorting, moved, preferred_element_type=f32).astype(bf16)

    upstream = cotangent.astype(f32)
    arrived = dispatch(moe_low)
    grad_arrived = dispatch((gate_prob * upstream).astype(bf16))

    expert_in = sort_rows(arrived)
    pre = jnp.einsum("jrd,jdf->jrf", expert_in, w_in, preferred_element_type=f32)
    activated, bent = gelu_parts(pre)
    hidden = activated.astype(bf16)
    partial_value = jnp.einsum("jrf,jfd->jrd", hidden, w_out, preferred_element_type=f32).astype(bf16)
    combined = collect(unsort_rows(partial_value))
    result_grad = sort_rows(grad_arrived)
    hidden_grad = jnp.einsum("jrd,jfd->jrf", result_grad, w_out, preferred_element_type=f32).astype(bf16)
    pre_grad = (hidden_grad.astype(f32) * gelu_slope(pre, bent)).astype(bf16)
    rows_partial = jnp.einsum("jrf,jdf->jrd", pre_grad, w_in, preferred_element_type=f32).astype(bf16)
    moe_grad = collect(unsort_rows(rows_partial))
    grad_w_out = jnp.einsum("jrf,jrd->jfd", hidden, result_grad, preferred_element_type=f32)
    grad_w_in = jnp.einsum("jrd,jrf->jdf", expert_in, pre_grad, preferred_element_type=f32)

    block_out = (middle + gate_prob * combined).astype(bf16)
    gate_grad = jnp.sum(upstream * combined, axis=-1, keepdims=True)
    logit_grad = router_probs * (route_hot * gate_grad - gate_prob * gate_grad)
    grad_router_t = lax.dot_general(
        logit_grad, moe_rows, (((0,), (0,)), ((), ())), precision=highest, preferred_element_type=f32
    )
    moe_grad = moe_grad + jnp.dot(logit_grad, router_t, precision=highest, preferred_element_type=f32)
    grad_gain_moe = jnp.sum(moe_grad * unit_moe, axis=0, keepdims=True)
    scaled = moe_grad * gain_moe
    middle_grad = upstream + middle_root * (
        scaled - unit_moe * jnp.mean(scaled * unit_moe, axis=-1, keepdims=True)
    )

    grad_rows = gather_members(middle_grad.astype(bf16)).reshape(group_tokens, width)
    mixed_grad = jnp.einsum("td,cd->tc", grad_rows, w_output, preferred_element_type=f32).astype(bf16)
    grad_w_output = sum_groups(
        jnp.einsum("tc,td->cd", mixed, grad_rows, preferred_element_type=f32).astype(bf16)
    ).astype(f32)
    joined_grad, score_grad = attend_back(joined, mixed_grad, probs, head_size)

    def weight_grad(part):
        columns = joined_grad[:, part * head_cols : (part + 1) * head_cols]
        local = jnp.einsum("td,tc->dc", normed_low, columns, preferred_element_type=f32).astype(bf16)
        return sum_groups(local).astype(f32)

    grad_w_value = weight_grad(2)
    grad_w_query = weight_grad(0)
    grad_w_key = weight_grad(1)
    attn_partial = jnp.einsum("tc,dc->td", joined_grad, w_joined, preferred_element_type=f32)
    attn_pairs = attn_partial.reshape(member_count // 2, 2, tok_dev, width)
    back_got = swap(attn_pairs[:, 1].astype(bf16), "mp", 1)
    attn_grad = scatter_pairs(attn_pairs[:, 0], back_got, 1)
    own_tokens = tokens.astype(f32)
    own_root = root_inverse(own_tokens)
    own_unit = own_tokens * own_root
    scaled = attn_grad * gain_attn
    input_grad = (
        middle_grad + own_root * (scaled - own_unit * jnp.mean(scaled * own_unit, axis=-1, keepdims=True))
    ).astype(bf16)
    grad_gain_attn = sum_all(jnp.sum(attn_grad * own_unit, axis=0, keepdims=True), ("mp", "dp"))[0]
    small = sum_all(jnp.concatenate([grad_gain_moe, grad_router_t], axis=0), ("mp", "dp"))
    grad_rel_bias = sum_all(bucket_grad(moved_table, score_grad, rel_bias.shape[0]), ("dp",))
    return (
        block_out,
        input_grad,
        grad_gain_attn,
        grad_w_query,
        grad_w_key,
        grad_w_value,
        grad_w_output,
        grad_rel_bias,
        small[0],
        small[1:].T,
        grad_w_in,
        grad_w_out,
    )


def solution(mesh):
    in_specs = (
        P(("dp", "mp"), None),
        P(),
        P(None, "mp"),
        P(None, "mp"),
        P(None, "mp"),
        P("mp", None),
        P(None, "mp"),
        P(),
        P(),
        P(),
        P("dp", None, "mp"),
        P("dp", "mp", None),
        P(("dp", "mp")),
        P(("dp", "mp")),
        P(("dp", "mp"), None),
    )
    out_specs = (
        P(("dp", "mp"), None),
        P(("dp", "mp"), None),
        P(),
        P(None, "mp"),
        P(None, "mp"),
        P(None, "mp"),
        P("mp", None),
        P(None, "mp"),
        P(),
        P(),
        P("dp", None, "mp"),
        P("dp", "mp", None),
    )
    return jax.shard_map(shards, mesh=mesh, in_specs=in_specs, out_specs=out_specs, check_vma=False)
```

```python
import functools

import jax
import jax.numpy as jnp
import numpy as np
from jax import lax
from jax.experimental import pallas as pl
from jax.experimental.pallas import tpu as pltpu
from jax.sharding import PartitionSpec as P

norm_eps = 1e-06
highest = lax.Precision.HIGHEST
bf16 = jnp.bfloat16
f32 = jnp.float32
LANES = 128
MIB = 1 << 20


def swap(block, axis, offset):
    size = lax.axis_size(axis)
    return lax.ppermute(block, axis, [(i, i ^ offset) for i in range(size)])


def bit_count(axis):
    return lax.axis_size(axis).bit_length() - 1


def gather_members(block, beside=None):
    held = block[None]
    for bit in reversed(range(bit_count("mp"))):
        other = swap(held, "mp", 1 << bit)
        if beside is not None and held.shape[0] == 1:
            other, beside = lax.optimization_barrier((other, beside))
        held = jnp.stack([held, other], axis=1).reshape((-1,) + block.shape)
    return held if beside is None else (held, beside)


def scatter_pairs(keep, received, first_bit):
    held = keep.astype(f32) + received.astype(f32)
    for bit in range(first_bit, bit_count("mp")):
        halves = held.reshape((-1, 2) + held.shape[1:])
        got = swap(halves[:, 1].astype(bf16), "mp", 1 << bit)
        held = halves[:, 0] + got.astype(f32)
    return held[0]


def exchange_groups(buffer):
    return lax.all_to_all(buffer, "dp", split_axis=0, concat_axis=0, tiled=True)


def near_step(part):
    mine = lax.axis_index("dp") & 1
    halves = part.reshape(2, part.shape[0] // 2, part.shape[1])
    got = swap(lax.dynamic_index_in_dim(halves, 1 - mine, 0, keepdims=False), "dp", 1)
    return lax.dynamic_index_in_dim(halves, mine, 0, keepdims=False), got


def far_steps(keep, got):
    rest = lax.axis_size("dp") // 2
    mine = lax.axis_index("dp") >> 1
    held = (keep.astype(f32) + got.astype(f32)).astype(bf16)
    blocks = held.reshape(rest, held.shape[0] // rest, held.shape[1])

    def block_of(offset):
        return lax.dynamic_index_in_dim(blocks, mine ^ offset, 0, keepdims=False)

    parts = [swap(block_of(offset), "dp", 2 * offset) for offset in range(1, rest)]
    total = block_of(0).astype(f32)
    for item in parts:
        total = total + item.astype(f32)
    own = total.astype(bf16)
    return jnp.stack([own] + [swap(own, "dp", 2 * offset) for offset in range(1, rest)])


def last_step(own_half):
    other = swap(own_half, "dp", 1)
    rest = lax.axis_size("dp") // 2
    me = lax.axis_index("dp")
    both = jnp.concatenate([own_half, other], axis=0)
    rows = []
    for half in range(2):
        for block in range(rest):
            at = (half ^ (me & 1)) * rest + (block ^ (me >> 1))
            rows.append(lax.dynamic_index_in_dim(both, at, 0, keepdims=False))
    return jnp.concatenate(rows, axis=0).astype(f32)


def sum_all(part, axes):
    held = part
    for axis in axes:
        for bit in range(bit_count(axis)):
            held = held + swap(held, axis, 1 << bit)
    return held


def bias_kernel(block, shift_ref, table_ref, bucket_ref, bias_ref, moved_ref):
    shift = shift_ref[0]
    for at in range(table_ref.shape[1] // block):
        source = pl.multiple_of((at ^ shift) * block, block)
        labels = table_ref[:, pl.ds(source, block)]
        columns = slice(at * block, (at + 1) * block)
        moved_ref[:, columns] = labels
        for head in range(bucket_ref.shape[0]):
            row = jnp.broadcast_to(bucket_ref[head : head + 1, :], labels.shape)
            bias_ref[head, :, columns] = jnp.take_along_axis(row, labels, axis=1, mode="promise_in_bounds")


def make_bias(table, bucket_rows, shift, block):
    seq_len = table.shape[0]
    heads = bucket_rows.shape[0]
    return pl.pallas_call(
        functools.partial(bias_kernel, block),
        grid_spec=pltpu.PrefetchScalarGridSpec(
            num_scalar_prefetch=1,
            grid=(seq_len // block,),
            in_specs=[
                pl.BlockSpec((block, seq_len), lambda i, s: (i ^ s[0], 0)),
                pl.BlockSpec((heads, LANES), lambda i, s: (0, 0)),
            ],
            out_specs=[
                pl.BlockSpec((heads, block, seq_len), lambda i, s: (0, i, 0)),
                pl.BlockSpec((block, seq_len), lambda i, s: (i, 0)),
            ],
        ),
        out_shape=[
            jax.ShapeDtypeStruct((heads, seq_len, seq_len), f32),
            jax.ShapeDtypeStruct((seq_len, seq_len), jnp.int32),
        ],
        compiler_params=pltpu.CompilerParams(vmem_limit_bytes=32 * MIB),
        cost_estimate=pl.CostEstimate(
            flops=seq_len * seq_len * heads, bytes_accessed=4 * seq_len * seq_len * (heads + 2), transcendentals=0
        ),
        name="bias_lookup",
    )(shift, table, bucket_rows)


def bucket_kernel(buckets, table_ref, grad_ref, out_ref):
    seqs, heads, rows, seq_len = grad_ref.shape

    @pl.when(pl.program_id(0) == 0)
    def _():
        out_ref[...] = jnp.zeros_like(out_ref)

    labels = lax.broadcasted_iota(jnp.int32, (rows, buckets, seq_len), 1)
    onehot = (table_ref[...][:, None, :] == labels).astype(f32).astype(bf16).reshape(rows * buckets, seq_len)
    total = jnp.zeros((rows * buckets, heads * rows), f32)
    for seq in range(seqs):
        grads = grad_ref[seq].reshape(heads * rows, seq_len)
        total += lax.dot_general(onehot, grads, (((1,), (1,)), ((), ())), preferred_element_type=f32)
    own_row = lax.broadcasted_iota(jnp.int32, (rows, buckets, heads * rows), 0)
    its_row = lax.broadcasted_iota(jnp.int32, (rows, buckets, heads * rows), 2) % rows
    kept = jnp.where(own_row == its_row, total.reshape(rows, buckets, heads * rows), 0.0)
    out_ref[...] += jnp.sum(kept, axis=0)


def bucket_grad(table, score_grad, buckets):
    seqs, heads, seq_len, _ = score_grad.shape
    rows = 32
    out = pl.pallas_call(
        functools.partial(bucket_kernel, buckets),
        grid=(seq_len // rows,),
        in_specs=[
            pl.BlockSpec((rows, seq_len), lambda i: (i, 0)),
            pl.BlockSpec((seqs, heads, rows, seq_len), lambda i: (0, 0, i, 0)),
        ],
        out_specs=pl.BlockSpec((buckets, heads * rows), lambda i: (0, 0)),
        out_shape=jax.ShapeDtypeStruct((buckets, heads * rows), f32),
        compiler_params=pltpu.CompilerParams(vmem_limit_bytes=32 * MIB),
        cost_estimate=pl.CostEstimate(
            flops=2 * seqs * seq_len * buckets * seq_len * heads * rows,
            bytes_accessed=2 * seqs * heads * seq_len * seq_len + 4 * seq_len * seq_len,
            transcendentals=0,
        ),
        name="bucket_grad",
    )(table, score_grad)
    return jnp.sum(out.reshape(buckets, heads, rows), axis=2)


def attend_kernel(head_size, joined_ref, bias_ref, mixed_ref, probs_ref):
    seq_len, width = joined_ref.shape
    head_cols = width // 3
    pair_heads = bias_ref.shape[0]
    pair_cols = pair_heads * head_size
    start = pl.program_id(1) * pair_cols
    columns = [
        joined_ref[:, pl.ds(pl.multiple_of(start + part * head_cols, pair_cols), pair_cols)] for part in range(3)
    ]
    rows = min(128, seq_len)
    for chunk in range(seq_len // rows):
        picked = slice(chunk * rows, (chunk + 1) * rows)
        outs = []
        for head in range(pair_heads):
            cols = slice(head * head_size, (head + 1) * head_size)
            scores = lax.dot_general(
                columns[0][picked, cols], columns[1][:, cols], (((1,), (1,)), ((), ())), preferred_element_type=f32
            )
            scores = scores + bias_ref[head, picked, :]
            expo = jnp.exp(scores - jnp.max(scores, axis=-1, keepdims=True))
            probs = expo / jnp.sum(expo, axis=-1, keepdims=True)
            probs_ref[0, head, picked, :] = probs
            outs.append(jnp.dot(probs.astype(bf16), columns[2][:, cols], preferred_element_type=f32))
        mixed_ref[picked, :] = jnp.concatenate(outs, axis=1).astype(bf16)


def attend(joined, bias, head_size):
    heads, seq_len, _ = bias.shape
    tokens, width = joined.shape
    seqs = tokens // seq_len
    head_cols = width // 3
    pair = min(heads, LANES // head_size)
    return pl.pallas_call(
        functools.partial(attend_kernel, head_size),
        grid=(seqs, heads // pair),
        in_specs=[
            pl.BlockSpec((seq_len, width), lambda s, h: (s, 0)),
            pl.BlockSpec((pair, seq_len, seq_len), lambda s, h: (h, 0, 0)),
        ],
        out_specs=[
            pl.BlockSpec((seq_len, pair * head_size), lambda s, h: (s, h)),
            pl.BlockSpec((1, pair, seq_len, seq_len), lambda s, h: (s, h, 0, 0)),
        ],
        out_shape=[
            jax.ShapeDtypeStruct((tokens, head_cols), bf16),
            jax.ShapeDtypeStruct((seqs, heads, seq_len, seq_len), f32),
        ],
        compiler_params=pltpu.CompilerParams(vmem_limit_bytes=32 * MIB),
        cost_estimate=pl.CostEstimate(
            flops=4 * seqs * heads * seq_len * seq_len * head_size,
            bytes_accessed=8 * seqs * heads * seq_len * seq_len,
            transcendentals=seqs * heads * seq_len * seq_len,
        ),
        name="attend",
    )(joined, bias)


def attend_back_kernel(head_size, joined_ref, grad_ref, probs_ref, out_ref, score_ref):
    seq_len, width = joined_ref.shape
    head_cols = width // 3
    pair_heads = probs_ref.shape[1]
    pair_cols = pair_heads * head_size
    start = pl.program_id(1) * pair_cols

    def place(part):
        return pl.ds(pl.multiple_of(start + part * head_cols, pair_cols), pair_cols)

    queries, keys, values = [joined_ref[:, place(part)] for part in range(3)]
    grads = grad_ref[...]
    queries_t, grads_t = queries.T, grads.T
    rows = min(128, seq_len)
    query_parts = []
    key_t = [jnp.zeros((head_size, seq_len), f32) for _ in range(pair_heads)]
    value_t = [jnp.zeros((head_size, seq_len), f32) for _ in range(pair_heads)]
    for chunk in range(seq_len // rows):
        picked = slice(chunk * rows, (chunk + 1) * rows)
        outs = []
        for head in range(pair_heads):
            cols = slice(head * head_size, (head + 1) * head_size)
            probs = probs_ref[0, head, picked, :]
            prob_grad = lax.dot_general(
                grads[picked, cols], values[:, cols], (((1,), (1,)), ((), ())), preferred_element_type=f32
            )
            weighted = jnp.sum(probs * prob_grad, axis=-1, keepdims=True)
            score_grad = (probs * (prob_grad - weighted)).astype(bf16)
            score_ref[0, head, picked, :] = score_grad
            outs.append(jnp.dot(score_grad, keys[:, cols], preferred_element_type=f32))
            key_t[head] += jnp.dot(queries_t[cols, picked], score_grad, preferred_element_type=f32)
            value_t[head] += jnp.dot(grads_t[cols, picked], probs.astype(bf16), preferred_element_type=f32)
        out_ref[picked, place(0)] = jnp.concatenate(outs, axis=1).astype(bf16)
    out_ref[:, place(1)] = jnp.concatenate(key_t, axis=0).T.astype(bf16)
    out_ref[:, place(2)] = jnp.concatenate(value_t, axis=0).T.astype(bf16)


def attend_back(joined, mixed_grad, probs, head_size):
    seqs, heads, seq_len, _ = probs.shape
    tokens, width = joined.shape
    pair = min(heads, LANES // head_size)
    return pl.pallas_call(
        functools.partial(attend_back_kernel, head_size),
        grid=(seqs, heads // pair),
        in_specs=[
            pl.BlockSpec((seq_len, width), lambda s, h: (s, 0)),
            pl.BlockSpec((seq_len, pair * head_size), lambda s, h: (s, h)),
            pl.BlockSpec((1, pair, seq_len, seq_len), lambda s, h: (s, h, 0, 0)),
        ],
        out_specs=[
            pl.BlockSpec((seq_len, width), lambda s, h: (s, 0)),
            pl.BlockSpec((1, pair, seq_len, seq_len), lambda s, h: (s, h, 0, 0)),
        ],
        out_shape=[
            jax.ShapeDtypeStruct((tokens, width), bf16),
            jax.ShapeDtypeStruct((seqs, heads, seq_len, seq_len), bf16),
        ],
        compiler_params=pltpu.CompilerParams(vmem_limit_bytes=32 * MIB),
        cost_estimate=pl.CostEstimate(
            flops=8 * seqs * heads * seq_len * seq_len * head_size,
            bytes_accessed=6 * seqs * heads * seq_len * seq_len,
            transcendentals=0,
        ),
        name="attend_back",
    )(joined, mixed_grad, probs)


gelu_scale = float(np.sqrt(2.0 / np.pi))


def gelu_parts(pre):
    bent = jnp.tanh(gelu_scale * (pre + 0.044715 * pre * pre * pre))
    return 0.5 * pre * (1.0 + bent), bent


def gelu_slope(pre):
    _, bent = gelu_parts(pre)
    return 0.5 * (1.0 + bent) + 0.5 * pre * (1.0 - bent * bent) * gelu_scale * (1.0 + 0.134145 * pre * pre)


def expert_kernel(cuts, middle_step, blocks_ref, sort_ref, unsort_ref, first_ref, second_ref, *refs):
    members, _, piece = blocks_ref.shape
    back_ref, rows_ref = refs[-1], refs[-2]
    expert_rows = sort_ref.shape[1] // cuts
    for member in range(members):
        moved = jnp.dot(sort_ref[0], blocks_ref[member], preferred_element_type=f32).astype(bf16)
        for cut in range(cuts):
            rows_ref[0, member * expert_rows : (member + 1) * expert_rows, cut * piece : (cut + 1) * piece] = moved[
                cut * expert_rows : (cut + 1) * expert_rows
            ]
    inner = lax.dot_general(rows_ref[0], first_ref[0], (((1,), (1,)), ((), ())), preferred_element_type=f32)
    inner = middle_step(inner, *refs[:-2])
    result = jnp.dot(inner, second_ref[0], preferred_element_type=f32).astype(bf16)
    for member in range(members):
        part = jnp.concatenate(
            [
                result[member * expert_rows : (member + 1) * expert_rows, cut * piece : (cut + 1) * piece]
                for cut in range(cuts)
            ],
            axis=0,
        )
        placed = jnp.dot(unsort_ref[0], part, preferred_element_type=f32).astype(bf16)

        @pl.when(pl.program_id(0) == 0)
        def _():
            back_ref[member] = placed

        @pl.when(pl.program_id(0) != 0)
        def _():
            back_ref[member] += placed


def forward_step(inner, pre_ref, hidden_ref):
    pre_ref[0] = inner
    hidden = gelu_parts(inner)[0].astype(bf16)
    hidden_ref[0] = hidden
    return hidden


def backward_step(inner, pre_ref, grad_ref):
    grad = (inner.astype(bf16).astype(f32) * gelu_slope(pre_ref[0])).astype(bf16)
    grad_ref[0] = grad
    return grad


def run_experts(blocks, sorting, unsorting, first, second, cuts, pre=None):
    members, all_rows, piece = blocks.shape
    experts, units, width = first.shape
    rows = members * (sorting.shape[1] // cuts)

    def per_expert(*shape):
        return pl.BlockSpec((1,) + shape, lambda j: (j, 0, 0))

    whole = pl.BlockSpec((members, all_rows, piece), lambda j: (0, 0, 0))
    inner = jax.ShapeDtypeStruct((experts, rows, units), bf16)
    in_specs = [
        whole,
        per_expert(*sorting.shape[1:]),
        per_expert(*unsorting.shape[1:]),
        per_expert(units, width),
        per_expert(units, width),
    ]
    operands = [blocks, sorting, unsorting, first, second]
    out_specs = [per_expert(rows, units), per_expert(rows, width), whole]
    out_shape = [inner, jax.ShapeDtypeStruct((experts, rows, width), bf16), jax.ShapeDtypeStruct(blocks.shape, bf16)]
    if pre is None:
        step, name = forward_step, "experts"
        out_specs.insert(0, per_expert(rows, units))
        out_shape.insert(0, jax.ShapeDtypeStruct(inner.shape, f32))
    else:
        step, name = backward_step, "experts_back"
        in_specs.append(per_expert(rows, units))
        operands.append(pre)
    return pl.pallas_call(
        functools.partial(expert_kernel, cuts, step),
        grid=(experts,),
        in_specs=in_specs,
        out_specs=out_specs,
        out_shape=out_shape,
        compiler_params=pltpu.CompilerParams(vmem_limit_bytes=40 * MIB),
        cost_estimate=pl.CostEstimate(
            flops=4 * experts * rows * units * width,
            bytes_accessed=4 * experts * units * width + 12 * experts * rows * width,
            transcendentals=experts * rows * units,
        ),
        name=name,
    )(*operands)


def root_inverse(values):
    return lax.rsqrt(jnp.mean(values * values, axis=-1, keepdims=True) + norm_eps)


def shards(
    tokens,
    gain_attn,
    w_query,
    w_key,
    w_value,
    w_output,
    rel_bias,
    bucket_table,
    gain_moe,
    router,
    w_in,
    w_out,
    routes,
    slots,
    cotangent,
):
    group_count = lax.axis_size("dp")
    member_count = lax.axis_size("mp")
    member = lax.axis_index("mp")
    tok_dev, width = tokens.shape
    expert_local = w_in.shape[0]
    expert_count = expert_local * group_count
    capacity = max(2, (5 * tok_dev + 4 * expert_count - 1) // (4 * expert_count))
    seq_len = bucket_table.shape[0]
    head_cols = w_query.shape[1]
    head_local = rel_bias.shape[1]
    head_size = head_cols // head_local
    group_tokens = tok_dev * member_count
    seq_members = seq_len // tok_dev

    bucket_rows = jnp.pad(rel_bias.T, ((0, 0), (0, LANES - rel_bias.shape[0])))
    shift = (member % seq_members).astype(jnp.int32)[None]
    bias, moved_table = make_bias(bucket_table, bucket_rows, shift, tok_dev)
    w_joined = jnp.concatenate([w_query, w_key, w_value], axis=1)
    all_tokens = gather_members(tokens, (bias, moved_table, w_joined))
    all_tokens, (bias, moved_table, w_joined) = all_tokens
    all_tokens = all_tokens.reshape(group_tokens, width).astype(f32)
    unit_attn = all_tokens * root_inverse(all_tokens)
    normed_low = (unit_attn * gain_attn).astype(bf16)
    joined = jnp.dot(normed_low, w_joined, preferred_element_type=f32).astype(bf16)
    mixed, probs = attend(joined, bias, head_size)
    mixed_pairs = mixed.reshape(member_count // 2, 2, tok_dev, head_cols)

    def project(rows):
        return jnp.einsum("stc,cd->std", rows, w_output, preferred_element_type=f32)

    attn_got = swap(project(mixed_pairs[:, 1]).astype(bf16), "mp", 1)
    attn = scatter_pairs(project(mixed_pairs[:, 0]), attn_got, 1)
    middle = tokens.astype(f32) + attn

    middle_root = root_inverse(middle)
    unit_moe = middle * middle_root
    moe_low = (unit_moe * gain_moe).astype(bf16)
    moe_rows = moe_low.astype(f32)
    router_t = router.T
    logits = lax.dot_general(
        moe_rows, router_t, (((1,), (1,)), ((), ())), precision=highest, preferred_element_type=f32
    )
    router_probs = jax.nn.softmax(logits, axis=-1)
    route_hot = (routes[:, None] == jnp.arange(expert_count, dtype=jnp.int32)[None, :]).astype(f32)
    gate_prob = jnp.sum(router_probs * route_hot, axis=-1, keepdims=True)

    chunk_slots = expert_local * capacity
    cuts = 1
    while cuts * chunk_slots % 8 != 0:
        cuts *= 2
    piece = width // cuts
    chunk_rows = cuts * chunk_slots
    all_rows = group_count * chunk_rows
    row_index = jnp.arange(all_rows, dtype=jnp.int32)
    row_chunk, row_cut, row_slot = (
        row_index // chunk_rows,
        (row_index // chunk_slots) % cuts,
        row_index % chunk_slots,
    )
    target = jnp.where(slots < capacity, routes * capacity + slots, -1)
    wanted = row_chunk * chunk_slots + row_slot
    hit = (wanted[:, None, None] == target[None, None, :]) & (
        row_cut[:, None, None] == jnp.arange(cuts, dtype=jnp.int32)[None, :, None]
    )
    placement = hit.astype(bf16).reshape(all_rows, cuts * tok_dev)

    def cut_rows(rows):
        return jnp.concatenate([rows[:, c * piece : (c + 1) * piece] for c in range(cuts)], axis=0)

    def join_rows(rows):
        return jnp.concatenate([rows[c * tok_dev : (c + 1) * tok_dev] for c in range(cuts)], axis=1)

    def send_rows(rows):
        return exchange_groups(jnp.dot(placement, cut_rows(rows), preferred_element_type=f32).astype(bf16))

    def collect(blocks):
        pairs = blocks.reshape(member_count // 2, 2, all_rows, piece)
        got = swap(pairs[:, 1], "mp", 1)
        back = exchange_groups(scatter_pairs(pairs[:, 0], got, 1).astype(bf16))
        rows = lax.dot_general(placement, back, (((0,), (0,)), ((), ())), preferred_element_type=f32)
        return join_rows(rows)

    order = np.arange(all_rows).reshape(group_count, cuts, expert_local, capacity).transpose(2, 1, 0, 3)
    picks = np.eye(all_rows, dtype=np.float32)[order.reshape(expert_local, -1)]
    sorting = jnp.asarray(picks, bf16)
    unsorting = jnp.asarray(picks.transpose(0, 2, 1), bf16)
    w_in_t = jnp.swapaxes(w_in, 1, 2)

    upstream = cotangent.astype(f32)
    sent = send_rows(moe_low)
    grad_sent = send_rows((gate_prob * upstream).astype(bf16))
    arrived = gather_members(sent)

    arrived, grad_sent = lax.optimization_barrier((arrived, grad_sent))
    grad_arrived = gather_members(grad_sent)
    pre, hidden, expert_in, value_blocks = run_experts(arrived, sorting, unsorting, w_in_t, w_out, cuts)
    pre_grad, result_grad, rows_blocks = run_experts(grad_arrived, sorting, unsorting, w_out, w_in_t, cuts, pre)
    combined = collect(value_blocks)
    moe_grad = collect(rows_blocks)
    grad_w_out = jnp.einsum("jrf,jrd->jfd", hidden, result_grad, preferred_element_type=f32)
    grad_w_in = jnp.swapaxes(
        jnp.einsum("jrf,jrd->jfd", pre_grad, expert_in, preferred_element_type=f32), 1, 2
    )

    block_out = (middle + gate_prob * combined).astype(bf16)
    gate_grad = jnp.sum(upstream * combined, axis=-1, keepdims=True)
    logit_grad = router_probs * (route_hot * gate_grad - gate_prob * gate_grad)
    grad_router_t = lax.dot_general(
        logit_grad, moe_rows, (((0,), (0,)), ((), ())), precision=highest, preferred_element_type=f32
    )
    moe_grad = moe_grad + jnp.dot(logit_grad, router_t, precision=highest, preferred_element_type=f32)
    grad_gain_moe = jnp.sum(moe_grad * unit_moe, axis=0, keepdims=True)
    scaled = moe_grad * gain_moe
    middle_grad = upstream + middle_root * (
        scaled - unit_moe * jnp.mean(scaled * unit_moe, axis=-1, keepdims=True)
    )

    grad_rows = gather_members(middle_grad.astype(bf16)).reshape(group_tokens, width)
    mixed_grad = jnp.einsum("td,cd->tc", grad_rows, w_output, preferred_element_type=f32).astype(bf16)
    output_part = jnp.einsum("tc,td->cd", mixed, grad_rows, preferred_element_type=f32).astype(bf16)
    output_near = near_step(output_part)
    joined_grad, score_grad = attend_back(joined, mixed_grad, probs, head_size)
    output_near, joined_grad = lax.optimization_barrier((output_near, joined_grad))
    joined_near = []
    for half in range(2):
        columns = normed_low[:, half * (width // 2) : (half + 1) * (width // 2)]
        local = jnp.einsum("td,tc->dc", columns, joined_grad, preferred_element_type=f32).astype(bf16)
        joined_near.append(near_step(local))
    grad_w_output = last_step(far_steps(*output_near))
    grad_joined = jnp.concatenate([last_step(far_steps(*near)) for near in joined_near], axis=0)
    grad_w_query, grad_w_key, grad_w_value = [
        grad_joined[:, part * head_cols : (part + 1) * head_cols] for part in range(3)
    ]
    attn_partial = jnp.einsum("tc,dc->td", joined_grad, w_joined, preferred_element_type=f32)
    attn_pairs = attn_partial.reshape(member_count // 2, 2, tok_dev, width)
    back_got = swap(attn_pairs[:, 1].astype(bf16), "mp", 1)
    attn_grad = scatter_pairs(attn_pairs[:, 0], back_got, 1)
    own_tokens = tokens.astype(f32)
    own_root = root_inverse(own_tokens)
    own_unit = own_tokens * own_root
    scaled = attn_grad * gain_attn
    input_grad = (
        middle_grad + own_root * (scaled - own_unit * jnp.mean(scaled * own_unit, axis=-1, keepdims=True))
    ).astype(bf16)
    grad_gain_attn = sum_all(jnp.sum(attn_grad * own_unit, axis=0, keepdims=True), ("mp", "dp"))[0]
    small = sum_all(jnp.concatenate([grad_gain_moe, grad_router_t], axis=0), ("mp", "dp"))
    grad_rel_bias = sum_all(bucket_grad(moved_table, score_grad, rel_bias.shape[0]), ("dp",))
    return (
        block_out,
        input_grad,
        grad_gain_attn,
        grad_w_query,
        grad_w_key,
        grad_w_value,
        grad_w_output,
        grad_rel_bias,
        small[0],
        small[1:].T,
        grad_w_in,
        grad_w_out,
    )


def solution(mesh):
    in_specs = (
        P(("dp", "mp"), None),
        P(),
        P(None, "mp"),
        P(None, "mp"),
        P(None, "mp"),
        P("mp", None),
        P(None, "mp"),
        P(),
        P(),
        P(),
        P("dp", None, "mp"),
        P("dp", "mp", None),
        P(("dp", "mp")),
        P(("dp", "mp")),
        P(("dp", "mp"), None),
    )
    out_specs = (
        P(("dp", "mp"), None),
        P(("dp", "mp"), None),
        P(),
        P(None, "mp"),
        P(None, "mp"),
        P(None, "mp"),
        P("mp", None),
        P(None, "mp"),
        P(),
        P(),
        P("dp", None, "mp"),
        P("dp", "mp", None),
    )
    return jax.shard_map(shards, mesh=mesh, in_specs=in_specs, out_specs=out_specs, check_vma=False)
```

```python
import functools

import jax
import jax.numpy as jnp
import numpy as np
from jax import lax
from jax.experimental import pallas as pl
from jax.experimental.pallas import tpu as pltpu
from jax.sharding import PartitionSpec as P

norm_eps = 1e-06
highest = lax.Precision.HIGHEST
bf16 = jnp.bfloat16
f32 = jnp.float32
LANES = 128
MIB = 1 << 20


def swap(block, axis, offset):
    size = lax.axis_size(axis)
    return lax.ppermute(block, axis, [(i, i ^ offset) for i in range(size)])


def bit_count(axis):
    return lax.axis_size(axis).bit_length() - 1


def gather_members(block, beside=None):
    held = block[None]
    for bit in reversed(range(bit_count("mp"))):
        other = swap(held, "mp", 1 << bit)
        if beside is not None and held.shape[0] == 1:
            other, beside = lax.optimization_barrier((other, beside))
        held = jnp.stack([held, other], axis=1).reshape((-1,) + block.shape)
    return held if beside is None else (held, beside)


def core_hop(blocks):
    pairs = blocks.reshape((-1, 2) + blocks.shape[1:])
    return pairs[:, 0], swap(pairs[:, 1].astype(bf16), "mp", 1)


def scatter_rest(keep, received, beside=None):
    held = keep.astype(f32) + received.astype(f32)
    for bit in range(1, bit_count("mp")):
        halves = held.reshape((-1, 2) + held.shape[1:])
        got = swap(halves[:, 1].astype(bf16), "mp", 1 << bit)
        if beside is not None and bit == 1:
            got, beside = lax.optimization_barrier((got, beside))
        held = halves[:, 0] + got.astype(f32)
    return held[0] if beside is None else (held[0], beside)


def exchange_groups(buffer):
    return lax.all_to_all(buffer, "dp", split_axis=0, concat_axis=0, tiled=True)


def near_step(part):
    mine = lax.axis_index("dp") & 1
    halves = part.reshape(2, part.shape[0] // 2, part.shape[1])
    got = swap(lax.dynamic_index_in_dim(halves, 1 - mine, 0, keepdims=False), "dp", 1)
    return lax.dynamic_index_in_dim(halves, mine, 0, keepdims=False), got


def far_sums(keep, got):
    rest = lax.axis_size("dp") // 2
    mine = lax.axis_index("dp") >> 1
    held = (keep.astype(f32) + got.astype(f32)).astype(bf16)
    blocks = held.reshape(rest, held.shape[0] // rest, held.shape[1])

    def block_of(offset):
        return lax.dynamic_index_in_dim(blocks, mine ^ offset, 0, keepdims=False)

    return [block_of(0)] + [swap(block_of(offset), "dp", 2 * offset) for offset in range(1, rest)]


def far_gather(parts):
    total = parts[0].astype(f32)
    for item in parts[1:]:
        total = total + item.astype(f32)
    own = total.astype(bf16)
    return [own] + [swap(own, "dp", 2 * offset) for offset in range(1, len(parts))]


def last_step(parts):
    own_half = jnp.stack(parts)
    other = swap(own_half, "dp", 1)
    rest = lax.axis_size("dp") // 2
    me = lax.axis_index("dp")
    both = jnp.concatenate([own_half, other], axis=0)
    rows = []
    for half in range(2):
        for block in range(rest):
            at = (half ^ (me & 1)) * rest + (block ^ (me >> 1))
            rows.append(lax.dynamic_index_in_dim(both, at, 0, keepdims=False))
    return jnp.concatenate(rows, axis=0).astype(f32)


def sum_all(part, axes):
    held = part
    for axis in axes:
        for bit in range(bit_count(axis)):
            held = held + swap(held, axis, 1 << bit)
    return held


def bias_kernel(block, shift_ref, table_ref, bucket_ref, bias_ref, moved_ref):
    shift = shift_ref[0]
    for at in range(table_ref.shape[1] // block):
        source = pl.multiple_of((at ^ shift) * block, block)
        labels = table_ref[:, pl.ds(source, block)]
        columns = slice(at * block, (at + 1) * block)
        moved_ref[:, columns] = labels
        for head in range(bucket_ref.shape[0]):
            row = jnp.broadcast_to(bucket_ref[head : head + 1, :], labels.shape)
            bias_ref[head, :, columns] = jnp.take_along_axis(row, labels, axis=1, mode="promise_in_bounds")


def make_bias(table, bucket_rows, shift, block):
    seq_len = table.shape[0]
    heads = bucket_rows.shape[0]
    return pl.pallas_call(
        functools.partial(bias_kernel, block),
        grid_spec=pltpu.PrefetchScalarGridSpec(
            num_scalar_prefetch=1,
            grid=(seq_len // block,),
            in_specs=[
                pl.BlockSpec((block, seq_len), lambda i, s: (i ^ s[0], 0)),
                pl.BlockSpec((heads, LANES), lambda i, s: (0, 0)),
            ],
            out_specs=[
                pl.BlockSpec((heads, block, seq_len), lambda i, s: (0, i, 0)),
                pl.BlockSpec((block, seq_len), lambda i, s: (i, 0)),
            ],
        ),
        out_shape=[
            jax.ShapeDtypeStruct((heads, seq_len, seq_len), f32),
            jax.ShapeDtypeStruct((seq_len, seq_len), jnp.int32),
        ],
        compiler_params=pltpu.CompilerParams(vmem_limit_bytes=8 * MIB),
        cost_estimate=pl.CostEstimate(
            flops=seq_len * seq_len * heads, bytes_accessed=4 * seq_len * seq_len * (heads + 2), transcendentals=0
        ),
        name="bias_lookup",
    )(shift, table, bucket_rows)


def bucket_kernel(buckets, table_ref, grad_ref, out_ref):
    seqs, heads, rows, seq_len = grad_ref.shape

    @pl.when(pl.program_id(0) == 0)
    def _():
        out_ref[...] = jnp.zeros_like(out_ref)

    labels = lax.broadcasted_iota(jnp.int32, (rows, buckets, seq_len), 1)
    onehot = (table_ref[...][:, None, :] == labels).astype(f32).astype(bf16).reshape(rows * buckets, seq_len)
    total = jnp.zeros((rows * buckets, heads * rows), f32)
    for seq in range(seqs):
        grads = grad_ref[seq].reshape(heads * rows, seq_len)
        total += lax.dot_general(onehot, grads, (((1,), (1,)), ((), ())), preferred_element_type=f32)
    own_row = lax.broadcasted_iota(jnp.int32, (rows, buckets, heads * rows), 0)
    its_row = lax.broadcasted_iota(jnp.int32, (rows, buckets, heads * rows), 2) % rows
    kept = jnp.where(own_row == its_row, total.reshape(rows, buckets, heads * rows), 0.0)
    out_ref[...] += jnp.sum(kept, axis=0)


def bucket_grad(table, score_grad, buckets):
    seqs, heads, seq_len, _ = score_grad.shape
    rows = 32
    out = pl.pallas_call(
        functools.partial(bucket_kernel, buckets),
        grid=(seq_len // rows,),
        in_specs=[
            pl.BlockSpec((rows, seq_len), lambda i: (i, 0)),
            pl.BlockSpec((seqs, heads, rows, seq_len), lambda i: (0, 0, i, 0)),
        ],
        out_specs=pl.BlockSpec((buckets, heads * rows), lambda i: (0, 0)),
        out_shape=jax.ShapeDtypeStruct((buckets, heads * rows), f32),
        compiler_params=pltpu.CompilerParams(vmem_limit_bytes=16 * MIB),
        cost_estimate=pl.CostEstimate(
            flops=2 * seqs * seq_len * buckets * seq_len * heads * rows,
            bytes_accessed=2 * seqs * heads * seq_len * seq_len + 4 * seq_len * seq_len,
            transcendentals=0,
        ),
        name="bucket_grad",
    )(table, score_grad)
    return jnp.sum(out.reshape(buckets, heads, rows), axis=2)


def attend_kernel(head_size, joined_ref, bias_ref, mixed_ref, probs_ref):
    seq_len, width = joined_ref.shape
    head_cols = width // 3
    pair_heads = bias_ref.shape[0]
    pair_cols = pair_heads * head_size
    start = pl.program_id(1) * pair_cols
    columns = [
        joined_ref[:, pl.ds(pl.multiple_of(start + part * head_cols, pair_cols), pair_cols)] for part in range(3)
    ]
    rows = min(128, seq_len)
    for chunk in range(seq_len // rows):
        picked = slice(chunk * rows, (chunk + 1) * rows)
        outs = []
        for head in range(pair_heads):
            cols = slice(head * head_size, (head + 1) * head_size)
            scores = lax.dot_general(
                columns[0][picked, cols], columns[1][:, cols], (((1,), (1,)), ((), ())), preferred_element_type=f32
            )
            scores = scores + bias_ref[head, picked, :]
            expo = jnp.exp(scores - jnp.max(scores, axis=-1, keepdims=True))
            probs = expo / jnp.sum(expo, axis=-1, keepdims=True)
            probs_ref[0, head, picked, :] = probs
            outs.append(jnp.dot(probs.astype(bf16), columns[2][:, cols], preferred_element_type=f32))
        mixed_ref[picked, :] = jnp.concatenate(outs, axis=1).astype(bf16)


def attend(joined, bias, head_size):
    heads, seq_len, _ = bias.shape
    tokens, width = joined.shape
    seqs = tokens // seq_len
    head_cols = width // 3
    pair = min(heads, LANES // head_size)
    return pl.pallas_call(
        functools.partial(attend_kernel, head_size),
        grid=(seqs, heads // pair),
        in_specs=[
            pl.BlockSpec((seq_len, width), lambda s, h: (s, 0)),
            pl.BlockSpec((pair, seq_len, seq_len), lambda s, h: (h, 0, 0)),
        ],
        out_specs=[
            pl.BlockSpec((seq_len, pair * head_size), lambda s, h: (s, h)),
            pl.BlockSpec((1, pair, seq_len, seq_len), lambda s, h: (s, h, 0, 0)),
        ],
        out_shape=[
            jax.ShapeDtypeStruct((tokens, head_cols), bf16),
            jax.ShapeDtypeStruct((seqs, heads, seq_len, seq_len), f32),
        ],
        compiler_params=pltpu.CompilerParams(vmem_limit_bytes=20 * MIB),
        cost_estimate=pl.CostEstimate(
            flops=4 * seqs * heads * seq_len * seq_len * head_size,
            bytes_accessed=8 * seqs * heads * seq_len * seq_len,
            transcendentals=seqs * heads * seq_len * seq_len,
        ),
        name="attend",
    )(joined, bias)


def attend_back_kernel(head_size, joined_ref, grad_ref, probs_ref, out_ref, score_ref):
    seq_len, width = joined_ref.shape
    head_cols = width // 3
    pair_heads = probs_ref.shape[1]
    pair_cols = pair_heads * head_size
    start = pl.program_id(1) * pair_cols

    def place(part):
        return pl.ds(pl.multiple_of(start + part * head_cols, pair_cols), pair_cols)

    queries, keys, values = [joined_ref[:, place(part)] for part in range(3)]
    grads = grad_ref[...]
    queries_t, grads_t = queries.T, grads.T
    rows = min(128, seq_len)
    query_parts = []
    key_t = [jnp.zeros((head_size, seq_len), f32) for _ in range(pair_heads)]
    value_t = [jnp.zeros((head_size, seq_len), f32) for _ in range(pair_heads)]
    for chunk in range(seq_len // rows):
        picked = slice(chunk * rows, (chunk + 1) * rows)
        outs = []
        for head in range(pair_heads):
            cols = slice(head * head_size, (head + 1) * head_size)
            probs = probs_ref[0, head, picked, :]
            prob_grad = lax.dot_general(
                grads[picked, cols], values[:, cols], (((1,), (1,)), ((), ())), preferred_element_type=f32
            )
            weighted = jnp.sum(probs * prob_grad, axis=-1, keepdims=True)
            score_grad = (probs * (prob_grad - weighted)).astype(bf16)
            score_ref[0, head, picked, :] = score_grad
            outs.append(jnp.dot(score_grad, keys[:, cols], preferred_element_type=f32))
            key_t[head] += jnp.dot(queries_t[cols, picked], score_grad, preferred_element_type=f32)
            value_t[head] += jnp.dot(grads_t[cols, picked], probs.astype(bf16), preferred_element_type=f32)
        out_ref[picked, place(0)] = jnp.concatenate(outs, axis=1).astype(bf16)
    out_ref[:, place(1)] = jnp.concatenate(key_t, axis=0).T.astype(bf16)
    out_ref[:, place(2)] = jnp.concatenate(value_t, axis=0).T.astype(bf16)


def attend_back(joined, mixed_grad, probs, head_size):
    seqs, heads, seq_len, _ = probs.shape
    tokens, width = joined.shape
    pair = min(heads, LANES // head_size)
    return pl.pallas_call(
        functools.partial(attend_back_kernel, head_size),
        grid=(seqs, heads // pair),
        in_specs=[
            pl.BlockSpec((seq_len, width), lambda s, h: (s, 0)),
            pl.BlockSpec((seq_len, pair * head_size), lambda s, h: (s, h)),
            pl.BlockSpec((1, pair, seq_len, seq_len), lambda s, h: (s, h, 0, 0)),
        ],
        out_specs=[
            pl.BlockSpec((seq_len, width), lambda s, h: (s, 0)),
            pl.BlockSpec((1, pair, seq_len, seq_len), lambda s, h: (s, h, 0, 0)),
        ],
        out_shape=[
            jax.ShapeDtypeStruct((tokens, width), bf16),
            jax.ShapeDtypeStruct((seqs, heads, seq_len, seq_len), bf16),
        ],
        compiler_params=pltpu.CompilerParams(vmem_limit_bytes=20 * MIB),
        cost_estimate=pl.CostEstimate(
            flops=8 * seqs * heads * seq_len * seq_len * head_size,
            bytes_accessed=6 * seqs * heads * seq_len * seq_len,
            transcendentals=0,
        ),
        name="attend_back",
    )(joined, mixed_grad, probs)


gelu_scale = float(np.sqrt(2.0 / np.pi))


def gelu_parts(pre):
    bent = jnp.tanh(gelu_scale * (pre + 0.044715 * pre * pre * pre))
    return 0.5 * pre * (1.0 + bent), bent


def gelu_slope(pre):
    _, bent = gelu_parts(pre)
    return 0.5 * (1.0 + bent) + 0.5 * pre * (1.0 - bent * bent) * gelu_scale * (1.0 + 0.134145 * pre * pre)


def expert_kernel(cuts, middle_step, blocks_ref, sort_ref, unsort_ref, first_ref, second_ref, *refs):
    members, _, piece = blocks_ref.shape
    back_ref, rows_ref = refs[-1], refs[-2]
    expert_rows = sort_ref.shape[1] // cuts
    for member in range(members):
        moved = jnp.dot(sort_ref[0], blocks_ref[member], preferred_element_type=f32).astype(bf16)
        for cut in range(cuts):
            rows_ref[0, member * expert_rows : (member + 1) * expert_rows, cut * piece : (cut + 1) * piece] = moved[
                cut * expert_rows : (cut + 1) * expert_rows
            ]
    inner = lax.dot_general(rows_ref[0], first_ref[0], (((1,), (1,)), ((), ())), preferred_element_type=f32)
    inner = middle_step(inner, *refs[:-2])
    result = jnp.dot(inner, second_ref[0], preferred_element_type=f32).astype(bf16)
    for member in range(members):
        part = jnp.concatenate(
            [
                result[member * expert_rows : (member + 1) * expert_rows, cut * piece : (cut + 1) * piece]
                for cut in range(cuts)
            ],
            axis=0,
        )
        placed = jnp.dot(unsort_ref[0], part, preferred_element_type=f32).astype(bf16)

        @pl.when(pl.program_id(0) == 0)
        def _():
            back_ref[member] = placed

        @pl.when(pl.program_id(0) != 0)
        def _():
            back_ref[member] += placed


def forward_step(inner, pre_ref, hidden_ref):
    pre_ref[0] = inner
    hidden = gelu_parts(inner)[0].astype(bf16)
    hidden_ref[0] = hidden
    return hidden


def backward_step(inner, pre_ref, grad_ref):
    grad = (inner.astype(bf16).astype(f32) * gelu_slope(pre_ref[0])).astype(bf16)
    grad_ref[0] = grad
    return grad


def run_experts(blocks, sorting, unsorting, first, second, cuts, pre=None):
    members, all_rows, piece = blocks.shape
    experts, units, width = first.shape
    rows = members * (sorting.shape[1] // cuts)

    def per_expert(*shape):
        return pl.BlockSpec((1,) + shape, lambda j: (j, 0, 0))

    whole = pl.BlockSpec((members, all_rows, piece), lambda j: (0, 0, 0))
    inner = jax.ShapeDtypeStruct((experts, rows, units), bf16)
    in_specs = [
        whole,
        per_expert(*sorting.shape[1:]),
        per_expert(*unsorting.shape[1:]),
        per_expert(units, width),
        per_expert(units, width),
    ]
    operands = [blocks, sorting, unsorting, first, second]
    out_specs = [per_expert(rows, units), per_expert(rows, width), whole]
    out_shape = [inner, jax.ShapeDtypeStruct((experts, rows, width), bf16), jax.ShapeDtypeStruct(blocks.shape, bf16)]
    if pre is None:
        step, name = forward_step, "experts"
        out_specs.insert(0, per_expert(rows, units))
        out_shape.insert(0, jax.ShapeDtypeStruct(inner.shape, f32))
    else:
        step, name = backward_step, "experts_back"
        in_specs.append(per_expert(rows, units))
        operands.append(pre)
    return pl.pallas_call(
        functools.partial(expert_kernel, cuts, step),
        grid=(experts,),
        in_specs=in_specs,
        out_specs=out_specs,
        out_shape=out_shape,
        compiler_params=pltpu.CompilerParams(vmem_limit_bytes=24 * MIB),
        cost_estimate=pl.CostEstimate(
            flops=4 * experts * rows * units * width,
            bytes_accessed=4 * experts * units * width + 12 * experts * rows * width,
            transcendentals=experts * rows * units,
        ),
        name=name,
    )(*operands)


def root_inverse(values):
    return lax.rsqrt(jnp.mean(values * values, axis=-1, keepdims=True) + norm_eps)


def shards(
    tokens,
    gain_attn,
    w_query,
    w_key,
    w_value,
    w_output,
    rel_bias,
    bucket_table,
    gain_moe,
    router,
    w_in,
    w_out,
    routes,
    slots,
    cotangent,
):
    group_count = lax.axis_size("dp")
    member_count = lax.axis_size("mp")
    member = lax.axis_index("mp")
    tok_dev, width = tokens.shape
    expert_local = w_in.shape[0]
    expert_count = expert_local * group_count
    capacity = max(2, (5 * tok_dev + 4 * expert_count - 1) // (4 * expert_count))
    seq_len = bucket_table.shape[0]
    head_cols = w_query.shape[1]
    head_local = rel_bias.shape[1]
    head_size = head_cols // head_local
    group_tokens = tok_dev * member_count
    seq_members = seq_len // tok_dev

    bucket_rows = jnp.pad(rel_bias.T, ((0, 0), (0, LANES - rel_bias.shape[0])))
    shift = (member % seq_members).astype(jnp.int32)[None]
    bias, moved_table = make_bias(bucket_table, bucket_rows, shift, tok_dev)
    w_joined = jnp.concatenate([w_query, w_key, w_value], axis=1)
    all_tokens = gather_members(tokens, (bias, moved_table, w_joined))
    all_tokens, (bias, moved_table, w_joined) = all_tokens
    all_tokens = all_tokens.reshape(group_tokens, width).astype(f32)
    unit_attn = all_tokens * root_inverse(all_tokens)
    normed_low = (unit_attn * gain_attn).astype(bf16)
    joined = jnp.dot(normed_low, w_joined, preferred_element_type=f32).astype(bf16)
    mixed, probs = attend(joined, bias, head_size)
    mixed_pairs = mixed.reshape(member_count // 2, 2, tok_dev, head_cols)

    def project(rows):
        return jnp.einsum("stc,cd->std", rows, w_output, preferred_element_type=f32)

    attn_got = swap(project(mixed_pairs[:, 1]).astype(bf16), "mp", 1)
    attn = scatter_rest(project(mixed_pairs[:, 0]), attn_got)
    middle = tokens.astype(f32) + attn

    middle_root = root_inverse(middle)
    unit_moe = middle * middle_root
    moe_low = (unit_moe * gain_moe).astype(bf16)
    moe_rows = moe_low.astype(f32)
    router_t = router.T
    logits = lax.dot_general(
        moe_rows, router_t, (((1,), (1,)), ((), ())), precision=highest, preferred_element_type=f32
    )
    router_probs = jax.nn.softmax(logits, axis=-1)
    route_hot = (routes[:, None] == jnp.arange(expert_count, dtype=jnp.int32)[None, :]).astype(f32)
    gate_prob = jnp.sum(router_probs * route_hot, axis=-1, keepdims=True)

    chunk_slots = expert_local * capacity
    cuts = 1
    while cuts * chunk_slots % 8 != 0:
        cuts *= 2
    piece = width // cuts
    chunk_rows = cuts * chunk_slots
    all_rows = group_count * chunk_rows
    row_index = jnp.arange(all_rows, dtype=jnp.int32)
    row_chunk, row_cut, row_slot = (
        row_index // chunk_rows,
        (row_index // chunk_slots) % cuts,
        row_index % chunk_slots,
    )
    target = jnp.where(slots < capacity, routes * capacity + slots, -1)
    wanted = row_chunk * chunk_slots + row_slot
    hit = (wanted[:, None, None] == target[None, None, :]) & (
        row_cut[:, None, None] == jnp.arange(cuts, dtype=jnp.int32)[None, :, None]
    )
    placement = hit.astype(bf16).reshape(all_rows, cuts * tok_dev)

    def cut_rows(rows):
        return jnp.concatenate([rows[:, c * piece : (c + 1) * piece] for c in range(cuts)], axis=0)

    def join_rows(rows):
        return jnp.concatenate([rows[c * tok_dev : (c + 1) * tok_dev] for c in range(cuts)], axis=1)

    def send_rows(rows):
        return exchange_groups(jnp.dot(placement, cut_rows(rows), preferred_element_type=f32).astype(bf16))

    def place_back(back):
        rows = lax.dot_general(placement, back, (((0,), (0,)), ((), ())), preferred_element_type=f32)
        return join_rows(rows)

    order = np.arange(all_rows).reshape(group_count, cuts, expert_local, capacity).transpose(2, 1, 0, 3)
    picks = np.eye(all_rows, dtype=np.float32)[order.reshape(expert_local, -1)]
    sorting = jnp.asarray(picks, bf16)
    unsorting = jnp.asarray(picks.transpose(0, 2, 1), bf16)
    w_in_t = jnp.swapaxes(w_in, 1, 2)

    upstream = cotangent.astype(f32)
    sent = send_rows(moe_low)
    grad_sent = send_rows((gate_prob * upstream).astype(bf16))
    arrived, grad_sent = gather_members(sent, grad_sent)

    pre, hidden, expert_in, value_blocks = run_experts(arrived, sorting, unsorting, w_in_t, w_out, cuts)
    grad_arrived, value_blocks = gather_members(grad_sent, value_blocks)
    value_hop = core_hop(value_blocks)
    pre_grad, result_grad, rows_blocks = run_experts(grad_arrived, sorting, unsorting, w_out, w_in_t, cuts, pre)
    value_sum, rows_blocks = scatter_rest(*value_hop, beside=rows_blocks)
    rows_hop = core_hop(rows_blocks)
    value_back = exchange_groups(value_sum.astype(bf16))
    rows_sum, value_back = scatter_rest(*rows_hop, beside=value_back)
    rows_back = exchange_groups(rows_sum.astype(bf16))
    grad_w_out = jnp.einsum("jrf,jrd->jfd", hidden, result_grad, preferred_element_type=f32)
    rows_back, grad_w_out = lax.optimization_barrier((rows_back, grad_w_out))
    grad_w_in_t = jnp.einsum("jrf,jrd->jfd", pre_grad, expert_in, preferred_element_type=f32)
    combined = place_back(value_back)
    moe_grad = place_back(rows_back)

    block_out = (middle + gate_prob * combined).astype(bf16)
    gate_grad = jnp.sum(upstream * combined, axis=-1, keepdims=True)
    logit_grad = router_probs * (route_hot * gate_grad - gate_prob * gate_grad)
    grad_router_t = lax.dot_general(
        logit_grad, moe_rows, (((0,), (0,)), ((), ())), precision=highest, preferred_element_type=f32
    )
    moe_grad = moe_grad + jnp.dot(logit_grad, router_t, precision=highest, preferred_element_type=f32)
    grad_gain_moe = jnp.sum(moe_grad * unit_moe, axis=0, keepdims=True)
    scaled = moe_grad * gain_moe
    middle_grad = upstream + middle_root * (
        scaled - unit_moe * jnp.mean(scaled * unit_moe, axis=-1, keepdims=True)
    )

    grad_rows, grad_w_in_t = gather_members(middle_grad.astype(bf16), grad_w_in_t)
    grad_rows = grad_rows.reshape(group_tokens, width)
    grad_w_in = jnp.swapaxes(grad_w_in_t, 1, 2)
    mixed_grad = jnp.einsum("td,cd->tc", grad_rows, w_output, preferred_element_type=f32).astype(bf16)
    output_part = jnp.einsum("tc,td->cd", mixed, grad_rows, preferred_element_type=f32).astype(bf16)
    output_near = near_step(output_part)
    joined_grad, score_grad = attend_back(joined, mixed_grad, probs, head_size)
    output_near, joined_grad = lax.optimization_barrier((output_near, joined_grad))
    locals_ = []
    for half in range(2):
        columns = normed_low[:, half * (width // 2) : (half + 1) * (width // 2)]
        locals_.append(jnp.einsum("td,tc->dc", columns, joined_grad, preferred_element_type=f32).astype(bf16))
    locals_, joined_grad, score_grad = lax.optimization_barrier((locals_, joined_grad, score_grad))
    first_near = near_step(locals_[0])
    second_near = near_step(locals_[1])
    output_sums = far_sums(*output_near)
    attn_partial = jnp.einsum("tc,dc->td", joined_grad, w_joined, preferred_element_type=f32)
    attn_hop = core_hop(attn_partial.reshape(member_count, tok_dev, width))
    gain_partial = jnp.sum(attn_partial * unit_attn, axis=0, keepdims=True)
    first_near, output_sums, attn_hop, score_grad = lax.optimization_barrier(
        (first_near, output_sums, attn_hop, score_grad)
    )
    first_sums = far_sums(*first_near)
    output_parts = far_gather(output_sums)
    bucket_part = bucket_grad(moved_table, score_grad, rel_bias.shape[0])
    first_sums, second_near, bucket_part, output_parts = lax.optimization_barrier(
        (first_sums, second_near, bucket_part, output_parts)
    )
    second_sums = far_sums(*second_near)
    first_parts = far_gather(first_sums)
    attn_grad = scatter_rest(*attn_hop)
    grad_w_output = last_step(output_parts)
    second_parts = far_gather(second_sums)
    grad_joined = jnp.concatenate([last_step(first_parts), last_step(second_parts)], axis=0)
    grad_w_query, grad_w_key, grad_w_value = [
        grad_joined[:, part * head_cols : (part + 1) * head_cols] for part in range(3)
    ]
    own_tokens = tokens.astype(f32)
    own_root = root_inverse(own_tokens)
    own_unit = own_tokens * own_root
    scaled = attn_grad * gain_attn
    input_grad = (
        middle_grad + own_root * (scaled - own_unit * jnp.mean(scaled * own_unit, axis=-1, keepdims=True))
    ).astype(bf16)
    bucket_row = lax.dynamic_update_slice(
        jnp.zeros((1, width), f32), bucket_part.reshape(1, -1), (0, member * bucket_part.size)
    )
    small = sum_all(jnp.concatenate([grad_gain_moe, gain_partial, bucket_row, grad_router_t], axis=0), ("mp", "dp"))
    grad_rel_bias = lax.dynamic_slice(small[2:3], (0, member * bucket_part.size), (1, bucket_part.size))
    grad_rel_bias = grad_rel_bias.reshape(bucket_part.shape)
    return (
        block_out,
        input_grad,
        small[1],
        grad_w_query,
        grad_w_key,
        grad_w_value,
        grad_w_output,
        grad_rel_bias,
        small[0],
        small[3:].T,
        grad_w_in,
        grad_w_out,
    )


def solution(mesh):
    in_specs = (
        P(("dp", "mp"), None),
        P(),
        P(None, "mp"),
        P(None, "mp"),
        P(None, "mp"),
        P("mp", None),
        P(None, "mp"),
        P(),
        P(),
        P(),
        P("dp", None, "mp"),
        P("dp", "mp", None),
        P(("dp", "mp")),
        P(("dp", "mp")),
        P(("dp", "mp"), None),
    )
    out_specs = (
        P(("dp", "mp"), None),
        P(("dp", "mp"), None),
        P(),
        P(None, "mp"),
        P(None, "mp"),
        P(None, "mp"),
        P("mp", None),
        P(None, "mp"),
        P(),
        P(),
        P("dp", None, "mp"),
        P("dp", "mp", None),
    )
    return jax.shard_map(shards, mesh=mesh, in_specs=in_specs, out_specs=out_specs, check_vma=False)
```

```python
import functools

import jax
import jax.numpy as jnp
import numpy as np
from jax import lax
from jax.experimental import pallas as pl
from jax.experimental.pallas import tpu as pltpu
from jax.sharding import PartitionSpec as P

norm_eps = 1e-06
highest = lax.Precision.HIGHEST
bf16 = jnp.bfloat16
f32 = jnp.float32
LANES = 128
MIB = 1 << 20


def swap(block, axis, offset):
    size = lax.axis_size(axis)
    return lax.ppermute(block, axis, [(i, i ^ offset) for i in range(size)])


def bit_count(axis):
    return lax.axis_size(axis).bit_length() - 1


def gather_members(block, beside):
    held = [block]
    mirrored = [swap(block, "mp", 1)]
    bits = bit_count("mp")
    for bit in reversed(range(1, bits)):
        others = [swap(item, "mp", 1 << bit) for item in held]
        if bit == bits - 1:
            others, beside = lax.optimization_barrier((others, beside))
        held = [item for pair in zip(held, others) for item in pair]
    return held, mirrored + [swap(item, "mp", 1) for item in held[1:]], beside


def core_hop(keep, send):
    return keep, swap(send.astype(bf16), "mp", 1)


def scatter_rest(keep, received, beside=None):
    held = keep.astype(f32) + received.astype(f32)
    for bit in range(1, bit_count("mp")):
        halves = held.reshape((-1, 2) + held.shape[1:])
        got = swap(halves[:, 1].astype(bf16), "mp", 1 << bit)
        if beside is not None and bit == 1:
            got, beside = lax.optimization_barrier((got, beside))
        held = halves[:, 0] + got.astype(f32)
    return held[0] if beside is None else (held[0], beside)


def exchange_groups(buffer):
    return lax.all_to_all(buffer, "dp", split_axis=0, concat_axis=0, tiled=True)


def halve(held, bit):
    mine = (lax.axis_index("dp") >> bit) & 1
    halves = held.reshape(2, held.shape[0] // 2, held.shape[1])
    got = swap(lax.dynamic_index_in_dim(halves, 1 - mine, 0, keepdims=False), "dp", 1 << bit)
    return lax.dynamic_index_in_dim(halves, mine, 0, keepdims=False), got


def joined_halves(keep, got):
    return (keep.astype(f32) + got.astype(f32)).astype(bf16)


def sum_rest(near):
    held = joined_halves(*near)
    for bit in range(1, bit_count("dp")):
        held = joined_halves(*halve(held, bit))
    held = held[None]
    for bit in reversed(range(1, bit_count("dp"))):
        held = jnp.concatenate([held, swap(held, "dp", 1 << bit)], axis=0)
    return held


def last_step(own_half):
    other = swap(own_half, "dp", 1)
    both = jnp.stack([own_half, other])
    bits = bit_count("dp")
    me = lax.axis_index("dp")
    rows = []
    for half in range(2):
        for block in range(1 << (bits - 1)):
            at = jnp.int32(0)
            for bit in range(1, bits):
                differs = ((block >> (bits - 1 - bit)) & 1) ^ ((me >> bit) & 1)
                at = at + (differs << (bits - 1 - bit))
            rows.append(both[half ^ (me & 1), at])
    return jnp.concatenate(rows, axis=0).astype(f32)


def bias_kernel(block, shift_ref, table_ref, bucket_ref, bias_ref, moved_ref):
    shift = shift_ref[0]
    for at in range(table_ref.shape[1] // block):
        source = pl.multiple_of((at ^ shift) * block, block)
        labels = table_ref[:, pl.ds(source, block)]
        columns = slice(at * block, (at + 1) * block)
        moved_ref[:, columns] = labels
        for head in range(bucket_ref.shape[0]):
            row = jnp.broadcast_to(bucket_ref[head : head + 1, :], labels.shape)
            bias_ref[head, :, columns] = jnp.take_along_axis(row, labels, axis=1, mode="promise_in_bounds")


def make_bias(table, bucket_rows, shift, block):
    seq_len = table.shape[0]
    heads = bucket_rows.shape[0]
    return pl.pallas_call(
        functools.partial(bias_kernel, block),
        grid_spec=pltpu.PrefetchScalarGridSpec(
            num_scalar_prefetch=1,
            grid=(seq_len // block,),
            in_specs=[
                pl.BlockSpec((block, seq_len), lambda i, s: (i ^ s[0], 0)),
                pl.BlockSpec((heads, LANES), lambda i, s: (0, 0)),
            ],
            out_specs=[
                pl.BlockSpec((heads, block, seq_len), lambda i, s: (0, i, 0)),
                pl.BlockSpec((block, seq_len), lambda i, s: (i, 0)),
            ],
        ),
        out_shape=[
            jax.ShapeDtypeStruct((heads, seq_len, seq_len), f32),
            pltpu.HBM((seq_len, seq_len), jnp.int32),
        ],
        compiler_params=pltpu.CompilerParams(vmem_limit_bytes=8 * MIB),
        cost_estimate=pl.CostEstimate(
            flops=seq_len * seq_len * heads, bytes_accessed=4 * seq_len * seq_len * (heads + 2), transcendentals=0
        ),
        name="bias_lookup",
    )(shift, table, bucket_rows)


def bucket_kernel(buckets, table_ref, grad_ref, out_ref):
    seqs, heads, rows, seq_len = grad_ref.shape

    @pl.when(pl.program_id(0) == 0)
    def _():
        out_ref[...] = jnp.zeros_like(out_ref)

    labels = lax.broadcasted_iota(jnp.int32, (buckets, seq_len), 0).astype(f32).astype(bf16)
    table = table_ref[...].astype(f32).astype(bf16)
    one, zero = jnp.ones((), bf16), jnp.zeros((), bf16)
    onehot = jnp.concatenate([jnp.where(table[row : row + 1, :] == labels, one, zero) for row in range(rows)], axis=0)
    total = jnp.zeros((rows * buckets, heads * rows), f32)
    for seq in range(seqs):
        grads = grad_ref[seq].reshape(heads * rows, seq_len)
        total += lax.dot_general(onehot, grads, (((1,), (1,)), ((), ())), preferred_element_type=f32)
    own_row = lax.broadcasted_iota(jnp.int32, (rows, buckets, heads * rows), 0)
    its_row = lax.broadcasted_iota(jnp.int32, (rows, buckets, heads * rows), 2) % rows
    kept = jnp.where(own_row == its_row, total.reshape(rows, buckets, heads * rows), 0.0)
    out_ref[...] += jnp.sum(kept, axis=0)


def bucket_grad(table, score_grad, buckets):
    seqs, heads, seq_len, _ = score_grad.shape
    rows = 32
    out = pl.pallas_call(
        functools.partial(bucket_kernel, buckets),
        grid=(seq_len // rows,),
        in_specs=[
            pl.BlockSpec((rows, seq_len), lambda i: (i, 0)),
            pl.BlockSpec((seqs, heads, rows, seq_len), lambda i: (0, 0, i, 0)),
        ],
        out_specs=pl.BlockSpec((buckets, heads * rows), lambda i: (0, 0)),
        out_shape=jax.ShapeDtypeStruct((buckets, heads * rows), f32),
        compiler_params=pltpu.CompilerParams(vmem_limit_bytes=16 * MIB),
        cost_estimate=pl.CostEstimate(flops=0, bytes_accessed=4 * seq_len, transcendentals=0),
        name="bucket_grad",
    )(table, score_grad)
    return jnp.sum(out.reshape(buckets, heads, rows), axis=2)


def attend_kernel(
    head_size,
    *refs,
):
    *token_refs, gain_ref, query_ref, key_ref, value_ref, bias_ref, normed_ref, joined_ref, mixed_ref, probs_ref = refs
    seq_len, width = joined_ref.shape
    head_cols = width // 3
    pair_heads = bias_ref.shape[0]
    pair_cols = pair_heads * head_size
    block = token_refs[0].shape[0]

    @pl.when(pl.program_id(0) == 0)
    def _():
        for at, token_ref in enumerate(token_refs):
            values = token_ref[...].astype(f32)
            root = lax.rsqrt(jnp.mean(values * values, axis=-1, keepdims=True) + norm_eps)
            normed_ref[at * block : (at + 1) * block, :] = (values * root * gain_ref[...]).astype(bf16)
        for part, weight_ref in enumerate((query_ref, key_ref, value_ref)):
            joined_ref[:, part * head_cols : (part + 1) * head_cols] = jnp.dot(
                normed_ref[...], weight_ref[...], preferred_element_type=f32
            ).astype(bf16)

    start = pl.program_id(0) * pair_cols
    columns = [
        joined_ref[:, pl.ds(pl.multiple_of(start + part * head_cols, pair_cols), pair_cols)] for part in range(3)
    ]
    rows = min(128, seq_len)
    for chunk in range(seq_len // rows):
        picked = slice(chunk * rows, (chunk + 1) * rows)
        outs = []
        for head in range(pair_heads):
            cols = slice(head * head_size, (head + 1) * head_size)
            scores = lax.dot_general(
                columns[0][picked, cols], columns[1][:, cols], (((1,), (1,)), ((), ())), preferred_element_type=f32
            )
            scores = scores + bias_ref[head, picked, :]
            expo = jnp.exp(scores - jnp.max(scores, axis=-1, keepdims=True))
            probs = (expo * (1.0 / jnp.sum(expo, axis=-1, keepdims=True))).astype(bf16)
            probs_ref[0, head, picked, :] = probs
            outs.append(jnp.dot(probs, columns[2][:, cols], preferred_element_type=f32))
        mixed_ref[picked, :] = jnp.concatenate(outs, axis=1).astype(bf16)


def attend(blocks, gain, w_query, w_key, w_value, bias, head_size):
    heads, seq_len, _ = bias.shape
    block, width = blocks[0].shape
    head_cols = w_query.shape[1]
    pair = min(heads, LANES // head_size)
    weight = pl.BlockSpec((width, head_cols), lambda h: (0, 0))
    weights = [pltpu.with_memory_space_constraint(item, pltpu.HBM) for item in (w_query, w_key, w_value)]
    return pl.pallas_call(
        functools.partial(attend_kernel, head_size),
        grid=(heads // pair,),
        in_specs=[pl.BlockSpec((block, width), lambda h: (0, 0))] * len(blocks)
        + [
            pl.BlockSpec((1, width), lambda h: (0, 0)),
            weight,
            weight,
            weight,
            pl.BlockSpec((pair, seq_len, seq_len), lambda h: (h, 0, 0)),
        ],
        out_specs=[
            pl.BlockSpec((seq_len, width), lambda h: (0, 0)),
            pl.BlockSpec((seq_len, 3 * head_cols), lambda h: (0, 0)),
            pl.BlockSpec((seq_len, pair * head_size), lambda h: (0, h)),
            pl.BlockSpec((1, pair, seq_len, seq_len), lambda h: (0, h, 0, 0)),
        ],
        out_shape=[
            pltpu.HBM((seq_len, width), bf16),
            pltpu.HBM((seq_len, 3 * head_cols), bf16),
            jax.ShapeDtypeStruct((seq_len, head_cols), bf16),
            pltpu.HBM((1, heads, seq_len, seq_len), bf16),
        ],
        compiler_params=pltpu.CompilerParams(vmem_limit_bytes=24 * MIB),
        cost_estimate=pl.CostEstimate(
            flops=4 * heads * seq_len * seq_len * head_size + 6 * seq_len * width * head_cols,
            bytes_accessed=6 * heads * seq_len * seq_len,
            transcendentals=heads * seq_len * seq_len,
        ),
        name="attend",
    )(*blocks, gain, *weights, bias)


def output_back_kernel(*refs):
    *block_refs, mixed_ref, weight_ref, mixed_grad_ref, part_ref = refs
    rows = jnp.concatenate([block_ref[...] for block_ref in block_refs], axis=0)
    part_ref[...] = lax.dot_general(
        mixed_ref[...], rows, (((0,), (0,)), ((), ())), preferred_element_type=f32
    ).astype(bf16)
    mixed_grad_ref[...] = lax.dot_general(
        rows, weight_ref[...], (((1,), (1,)), ((), ())), preferred_element_type=f32
    ).astype(bf16)


def output_back(blocks, mixed, weight):
    tokens, head_cols = mixed.shape
    width = weight.shape[1]
    return pl.pallas_call(
        output_back_kernel,
        out_shape=[
            jax.ShapeDtypeStruct((tokens, head_cols), bf16),
            jax.ShapeDtypeStruct((head_cols, width), bf16),
        ],
        compiler_params=pltpu.CompilerParams(vmem_limit_bytes=16 * MIB),
        cost_estimate=pl.CostEstimate(
            flops=4 * tokens * head_cols * width, bytes_accessed=4 * tokens * width, transcendentals=0
        ),
        name="output_back",
    )(*blocks, mixed, weight)


def attend_back_kernel(head_size, joined_ref, grad_ref, probs_ref, out_ref, score_ref):
    seq_len, width = joined_ref.shape
    head_cols = width // 3
    pair_heads = probs_ref.shape[1]
    pair_cols = pair_heads * head_size
    start = pl.program_id(1) * pair_cols

    def place(part):
        return pl.ds(pl.multiple_of(start + part * head_cols, pair_cols), pair_cols)

    queries, keys, values = [joined_ref[:, place(part)] for part in range(3)]
    grads = grad_ref[...]
    queries_t, grads_t = queries.T, grads.T
    rows = min(128, seq_len)
    query_parts = []
    key_t = [jnp.zeros((head_size, seq_len), f32) for _ in range(pair_heads)]
    value_t = [jnp.zeros((head_size, seq_len), f32) for _ in range(pair_heads)]
    for chunk in range(seq_len // rows):
        picked = slice(chunk * rows, (chunk + 1) * rows)
        outs = []
        for head in range(pair_heads):
            cols = slice(head * head_size, (head + 1) * head_size)
            probs_low = probs_ref[0, head, picked, :]
            probs = probs_low.astype(f32)
            prob_grad = lax.dot_general(
                grads[picked, cols], values[:, cols], (((1,), (1,)), ((), ())), preferred_element_type=f32
            )
            weighted = jnp.sum(probs * prob_grad, axis=-1, keepdims=True)
            score_grad = (probs * (prob_grad - weighted)).astype(bf16)
            score_ref[0, head, picked, :] = score_grad
            outs.append(jnp.dot(score_grad, keys[:, cols], preferred_element_type=f32))
            key_t[head] += jnp.dot(queries_t[cols, picked], score_grad, preferred_element_type=f32)
            value_t[head] += jnp.dot(grads_t[cols, picked], probs_low, preferred_element_type=f32)
        out_ref[picked, place(0)] = jnp.concatenate(outs, axis=1).astype(bf16)
    out_ref[:, place(1)] = jnp.concatenate(key_t, axis=0).T.astype(bf16)
    out_ref[:, place(2)] = jnp.concatenate(value_t, axis=0).T.astype(bf16)


def attend_back(joined, mixed_grad, probs, head_size):
    seqs, heads, seq_len, _ = probs.shape
    tokens, width = joined.shape
    pair = min(heads, LANES // head_size)
    return pl.pallas_call(
        functools.partial(attend_back_kernel, head_size),
        grid=(seqs, heads // pair),
        in_specs=[
            pl.BlockSpec((seq_len, width), lambda s, h: (s, 0)),
            pl.BlockSpec((seq_len, pair * head_size), lambda s, h: (s, h)),
            pl.BlockSpec((1, pair, seq_len, seq_len), lambda s, h: (s, h, 0, 0)),
        ],
        out_specs=[
            pl.BlockSpec((seq_len, width), lambda s, h: (s, 0)),
            pl.BlockSpec((1, pair, seq_len, seq_len), lambda s, h: (s, h, 0, 0)),
        ],
        out_shape=[
            jax.ShapeDtypeStruct((tokens, width), bf16),
            pltpu.HBM((seqs, heads, seq_len, seq_len), bf16),
        ],
        compiler_params=pltpu.CompilerParams(vmem_limit_bytes=20 * MIB),
        cost_estimate=pl.CostEstimate(
            flops=8 * seqs * heads * seq_len * seq_len * head_size,
            bytes_accessed=6 * seqs * heads * seq_len * seq_len,
            transcendentals=0,
        ),
        name="attend_back",
    )(joined, mixed_grad, probs)


gelu_scale = float(np.sqrt(2.0 / np.pi))


def gelu_parts(pre):
    bent = jnp.tanh(gelu_scale * (pre + 0.044715 * pre * pre * pre))
    return 0.5 * pre * (1.0 + bent), bent


def gelu_slope(pre):
    _, bent = gelu_parts(pre)
    return 0.5 * (1.0 + bent) + 0.5 * pre * (1.0 - bent * bent) * gelu_scale * (1.0 + 0.134145 * pre * pre)


def expert_kernel(cuts, middle_step, members, *refs):
    block_refs = refs[:members]
    order_ref, first_ref, second_ref, *middle_refs, inner_ref, rows_out, keep_ref, send_ref = refs[members:-6]
    first_held, second_held, inner_held, rows_ref, arrived, left = refs[-6:]
    half = members // 2
    all_rows, piece = block_refs[0].shape
    experts, _, picked = order_ref.shape
    expert_rows = picked // cuts
    loads = []
    for expert in range(experts):
        for at, (source, held) in enumerate(((first_ref, first_held), (second_ref, second_held))):
            load = pltpu.make_async_copy(source.at[expert], held.at[expert], arrived.at[2 * expert + at])
            load.start()
            loads.append(load)
    places = [
        (order_ref[expert] == lax.broadcasted_iota(jnp.int32, (all_rows, picked), 0)).astype(f32)
        for expert in range(experts)
    ]
    for expert in range(experts):
        sorting = places[expert].T.astype(bf16)
        for member in range(members):
            moved = jnp.dot(sorting, block_refs[member][...], preferred_element_type=f32).astype(bf16)
            for cut in range(cuts):
                rows_ref[
                    expert, member * expert_rows : (member + 1) * expert_rows, cut * piece : (cut + 1) * piece
                ] = moved[cut * expert_rows : (cut + 1) * expert_rows]
    stores = [pltpu.make_async_copy(rows_ref, rows_out, left.at[experts])]
    stores[0].start()
    results = []
    for expert in range(experts):
        loads[2 * expert].wait()
        inner = lax.dot_general(
            rows_ref[expert], first_held[expert], (((1,), (1,)), ((), ())), preferred_element_type=f32
        )
        inner = middle_step(expert, inner, *middle_refs)
        inner_held[expert] = inner
        stores.append(pltpu.make_async_copy(inner_held.at[expert], inner_ref.at[expert], left.at[expert]))
        stores[-1].start()
        loads[2 * expert + 1].wait()
        results.append(jnp.dot(inner, second_held[expert], preferred_element_type=f32).astype(bf16))
    for member in range(members):
        parts = [
            result[member * expert_rows : (member + 1) * expert_rows, cut * piece : (cut + 1) * piece]
            for result in results
            for cut in range(cuts)
        ]
        unsorting = jnp.concatenate([place.astype(bf16) for place in places], axis=1)
        placed = jnp.dot(unsorting, jnp.concatenate(parts, axis=0), preferred_element_type=f32).astype(bf16)
        target, at = (keep_ref, member) if member < half else (send_ref, member - half)
        target[at] = placed
    for store in stores:
        store.wait()


def forward_step(expert, inner, pre_ref):
    pre_ref[expert] = inner
    return gelu_parts(inner)[0].astype(bf16)


def backward_step(expert, inner, pre_ref):
    return (inner.astype(bf16).astype(f32) * gelu_slope(pre_ref[expert])).astype(bf16)


def run_experts(blocks, order, first, second, cuts, pre=None):
    members = len(blocks)
    experts, units, width = first.shape
    picked = order.shape[1]
    rows = members * (picked // cuts)
    part = jax.ShapeDtypeStruct((members // 2,) + blocks[0].shape, bf16)
    inside = pl.BlockSpec(memory_space=pltpu.VMEM)
    outside = pl.BlockSpec(memory_space=pltpu.HBM)
    first, second = [pltpu.with_memory_space_constraint(item, pltpu.HBM) for item in (first, second)]
    out_specs = [outside, outside, inside, inside]
    in_specs = [inside] * (members + 1) + [outside, outside]
    operands = [*blocks, order[:, None, :], first, second]
    out_shape = [pltpu.HBM((experts, rows, units), bf16), pltpu.HBM((experts, rows, width), bf16), part, part]
    if pre is None:
        step, name = forward_step, "experts"
        out_shape.insert(0, jax.ShapeDtypeStruct((experts, rows, units), f32))
        out_specs.insert(0, inside)
    else:
        step, name = backward_step, "experts_back"
        in_specs.append(inside)
        operands.append(pre)
    return pl.pallas_call(
        functools.partial(expert_kernel, cuts, step, members),
        in_specs=in_specs,
        out_specs=out_specs,
        out_shape=out_shape,
        scratch_shapes=[
            pltpu.VMEM((experts, units, width), bf16),
            pltpu.VMEM((experts, units, width), bf16),
            pltpu.VMEM((experts, rows, units), bf16),
            pltpu.VMEM((experts, rows, width), bf16),
            pltpu.SemaphoreType.DMA((2 * experts,)),
            pltpu.SemaphoreType.DMA((experts + 1,)),
        ],
        compiler_params=pltpu.CompilerParams(vmem_limit_bytes=26 * MIB),
        cost_estimate=pl.CostEstimate(
            flops=4 * experts * rows * units * width,
            bytes_accessed=4 * experts * units * width + 12 * experts * rows * width,
            transcendentals=experts * rows * units,
        ),
        name=name,
    )(*operands)


def root_inverse(values):
    return lax.rsqrt(jnp.mean(values * values, axis=-1, keepdims=True) + norm_eps)


def shards(
    tokens,
    gain_attn,
    w_query,
    w_key,
    w_value,
    w_output,
    rel_bias,
    bucket_table,
    gain_moe,
    router,
    w_in,
    w_out,
    routes,
    slots,
    cotangent,
):
    group_count = lax.axis_size("dp")
    member_count = lax.axis_size("mp")
    member = lax.axis_index("mp")
    tok_dev, width = tokens.shape
    expert_local = w_in.shape[0]
    expert_count = expert_local * group_count
    capacity = max(2, (5 * tok_dev + 4 * expert_count - 1) // (4 * expert_count))
    seq_len = bucket_table.shape[0]
    head_cols = w_query.shape[1]
    head_local = rel_bias.shape[1]
    head_size = head_cols // head_local
    group_tokens = tok_dev * member_count
    seq_members = seq_len // tok_dev

    bucket_rows = jnp.pad(rel_bias.T, ((0, 0), (0, LANES - rel_bias.shape[0])))
    shift = (member % seq_members).astype(jnp.int32)[None]
    bias, moved_table = make_bias(bucket_table, bucket_rows, shift, tok_dev)
    near_tokens, far_tokens, (bias, moved_table) = gather_members(tokens, (bias, moved_table))
    token_blocks = [item for pair in zip(near_tokens, far_tokens) for item in pair]
    sequences = [
        attend(token_blocks[at : at + seq_members], gain_attn[None], w_query, w_key, w_value, bias, head_size)
        for at in range(0, member_count, seq_members)
    ]
    normed_low, joined, mixed, probs = [
        parts[0] if len(parts) == 1 else jnp.concatenate(parts, axis=0) for parts in zip(*sequences)
    ]
    mixed_pairs = mixed.reshape(member_count // 2, 2, tok_dev, head_cols)

    def project(rows):
        return jnp.einsum("stc,cd->std", rows, w_output, preferred_element_type=f32)

    attn_got = swap(project(mixed_pairs[:, 1]).astype(bf16), "mp", 1)
    attn = scatter_rest(project(mixed_pairs[:, 0]), attn_got)
    middle = tokens.astype(f32) + attn

    middle_root = root_inverse(middle)
    unit_moe = middle * middle_root
    moe_low = (unit_moe * gain_moe).astype(bf16)
    moe_rows = moe_low.astype(f32)
    router_t = router.T
    logits = lax.dot_general(
        moe_rows, router_t, (((1,), (1,)), ((), ())), precision=highest, preferred_element_type=f32
    )
    router_probs = jax.nn.softmax(logits, axis=-1)
    route_hot = (routes[:, None] == jnp.arange(expert_count, dtype=jnp.int32)[None, :]).astype(f32)
    gate_prob = jnp.sum(router_probs * route_hot, axis=-1, keepdims=True)

    chunk_slots = expert_local * capacity
    cuts = 1
    while cuts * chunk_slots % 8 != 0:
        cuts *= 2
    piece = width // cuts
    chunk_rows = cuts * chunk_slots
    all_rows = group_count * chunk_rows
    row_index = jnp.arange(all_rows, dtype=jnp.int32)
    row_chunk, row_cut, row_slot = (
        row_index // chunk_rows,
        (row_index // chunk_slots) % cuts,
        row_index % chunk_slots,
    )
    target = jnp.where(slots < capacity, routes * capacity + slots, -1)
    wanted = row_chunk * chunk_slots + row_slot
    hit = (wanted[:, None, None] == target[None, None, :]) & (
        row_cut[:, None, None] == jnp.arange(cuts, dtype=jnp.int32)[None, :, None]
    )
    placement = hit.astype(bf16).reshape(all_rows, cuts * tok_dev)

    def cut_rows(rows):
        return jnp.concatenate([rows[:, c * piece : (c + 1) * piece] for c in range(cuts)], axis=0)

    def join_rows(rows):
        return jnp.concatenate([rows[c * tok_dev : (c + 1) * tok_dev] for c in range(cuts)], axis=1)

    def send_rows(rows):
        return exchange_groups(jnp.dot(placement, cut_rows(rows), preferred_element_type=f32).astype(bf16))

    def place_back(back):
        rows = lax.dot_general(placement, back, (((0,), (0,)), ((), ())), preferred_element_type=f32)
        return join_rows(rows)

    order = np.arange(all_rows).reshape(group_count, cuts, expert_local, capacity).transpose(2, 1, 0, 3)
    order = jnp.asarray(order.reshape(expert_local, -1), jnp.int32)
    w_in_t = jnp.swapaxes(w_in, 1, 2)

    upstream = cotangent.astype(f32)
    sent = send_rows(moe_low)
    grad_sent = send_rows((gate_prob * upstream).astype(bf16))
    w_joined = jnp.concatenate([w_query, w_key, w_value], axis=1)
    near_rows, far_rows, (grad_sent, w_joined) = gather_members(sent, (grad_sent, w_joined))

    pre, hidden, expert_in, value_keep, value_send = run_experts(near_rows + far_rows, order, w_in_t, w_out, cuts)
    near_rows, far_rows, (value_keep, value_send) = gather_members(grad_sent, (value_keep, value_send))
    value_hop = core_hop(value_keep, value_send)
    pre_grad, result_grad, *rows_blocks = run_experts(near_rows + far_rows, order, w_out, w_in_t, cuts, pre)
    value_sum, rows_blocks = scatter_rest(*value_hop, beside=rows_blocks)
    rows_hop = core_hop(*rows_blocks)
    value_back = exchange_groups(value_sum.astype(bf16))
    rows_sum, value_back = scatter_rest(*rows_hop, beside=value_back)
    rows_back = exchange_groups(rows_sum.astype(bf16))
    grad_w_out = jnp.einsum("jrf,jrd->jfd", hidden, result_grad, preferred_element_type=f32)
    rows_back, grad_w_out = lax.optimization_barrier((rows_back, grad_w_out))
    grad_w_in_t = jnp.einsum("jrf,jrd->jfd", pre_grad, expert_in, preferred_element_type=f32)
    combined = place_back(value_back)
    moe_grad = place_back(rows_back)

    block_out = (middle + gate_prob * combined).astype(bf16)
    gate_grad = jnp.sum(upstream * combined, axis=-1, keepdims=True)
    logit_grad = router_probs * (route_hot * gate_grad - gate_prob * gate_grad)
    grad_router_t = lax.dot_general(
        logit_grad, moe_rows, (((0,), (0,)), ((), ())), precision=highest, preferred_element_type=f32
    )
    moe_grad = moe_grad + jnp.dot(logit_grad, router_t, precision=highest, preferred_element_type=f32)
    grad_gain_moe = jnp.sum(moe_grad * unit_moe, axis=0, keepdims=True)
    scaled = moe_grad * gain_moe
    middle_grad = upstream + middle_root * (
        scaled - unit_moe * jnp.mean(scaled * unit_moe, axis=-1, keepdims=True)
    )

    near_grads, far_grads, grad_w_in_t = gather_members(middle_grad.astype(bf16), grad_w_in_t)
    grad_w_in = jnp.swapaxes(grad_w_in_t, 1, 2)
    grad_blocks = [item for pair in zip(near_grads, far_grads) for item in pair]
    mixed_grad, output_part = output_back(grad_blocks, mixed, w_output)
    output_near = halve(output_part, 0)
    joined_grad, score_grad = attend_back(joined, mixed_grad, probs, head_size)
    output_near, joined_grad, token_blocks = lax.optimization_barrier((output_near, joined_grad, token_blocks))
    locals_ = []
    for half in range(2):
        columns = normed_low[:, half * (width // 2) : (half + 1) * (width // 2)]
        locals_.append(jnp.einsum("td,tc->dc", columns, joined_grad, preferred_element_type=f32).astype(bf16))
    locals_, joined_grad, score_grad = lax.optimization_barrier((locals_, joined_grad, score_grad))
    first_near = halve(locals_[0], 0)
    second_near = halve(locals_[1], 0)
    attn_partial = jnp.einsum("tc,dc->td", joined_grad, w_joined, preferred_element_type=f32)
    attn_pairs = attn_partial.reshape(member_count // 2, 2, tok_dev, width)
    attn_hop = core_hop(attn_pairs[:, 0], attn_pairs[:, 1])
    all_tokens = jnp.concatenate(token_blocks, axis=0).astype(f32)
    gain_partial = jnp.sum(attn_partial * (all_tokens * root_inverse(all_tokens)), axis=0, keepdims=True)
    bucket_part = bucket_grad(moved_table, score_grad, rel_bias.shape[0])
    first_near, attn_hop, bucket_part, gain_partial, output_near = lax.optimization_barrier(
        (first_near, attn_hop, bucket_part, gain_partial, output_near)
    )
    bucket_row = lax.dynamic_update_slice(
        jnp.zeros((1, width), f32), bucket_part.reshape(1, -1), (0, member * bucket_part.size)
    )
    small = jnp.concatenate([grad_gain_moe, gain_partial, bucket_row, grad_router_t], axis=0)
    for axis in ("mp", "dp"):
        for bit in range(bit_count(axis)):
            small = small + swap(small, axis, 1 << bit)
    attn_grad = scatter_rest(*attn_hop)
    grad_w_output = last_step(sum_rest(output_near))
    grad_joined = jnp.concatenate([last_step(sum_rest(first_near)), last_step(sum_rest(second_near))], axis=0)
    grad_w_query, grad_w_key, grad_w_value = [
        grad_joined[:, part * head_cols : (part + 1) * head_cols] for part in range(3)
    ]
    own_tokens = tokens.astype(f32)
    own_root = root_inverse(own_tokens)
    own_unit = own_tokens * own_root
    scaled = attn_grad * gain_attn
    input_grad = (
        middle_grad + own_root * (scaled - own_unit * jnp.mean(scaled * own_unit, axis=-1, keepdims=True))
    ).astype(bf16)
    grad_rel_bias = lax.dynamic_slice(small[2:3], (0, member * bucket_part.size), (1, bucket_part.size))
    grad_rel_bias = grad_rel_bias.reshape(bucket_part.shape)
    return (
        block_out,
        input_grad,
        small[1],
        grad_w_query,
        grad_w_key,
        grad_w_value,
        grad_w_output,
        grad_rel_bias,
        small[0],
        small[3:].T,
        grad_w_in,
        grad_w_out,
    )


def solution(mesh):
    in_specs = (
        P(("dp", "mp"), None),
        P(),
        P(None, "mp"),
        P(None, "mp"),
        P(None, "mp"),
        P("mp", None),
        P(None, "mp"),
        P(),
        P(),
        P(),
        P("dp", None, "mp"),
        P("dp", "mp", None),
        P(("dp", "mp")),
        P(("dp", "mp")),
        P(("dp", "mp"), None),
    )
    out_specs = (
        P(("dp", "mp"), None),
        P(("dp", "mp"), None),
        P(),
        P(None, "mp"),
        P(None, "mp"),
        P(None, "mp"),
        P("mp", None),
        P(None, "mp"),
        P(),
        P(),
        P("dp", None, "mp"),
        P("dp", "mp", None),
    )
    return jax.shard_map(shards, mesh=mesh, in_specs=in_specs, out_specs=out_specs, check_vma=False)
```

```python
import functools

import jax
import jax.numpy as jnp
import numpy as np
from jax import lax
from jax.experimental import pallas as pl
from jax.experimental.pallas import tpu as pltpu
from jax.sharding import PartitionSpec as P

norm_eps = 1e-06
highest = lax.Precision.HIGHEST
bf16 = jnp.bfloat16
f32 = jnp.float32
LANES = 128
MIB = 1 << 20
small_cost = pl.CostEstimate(flops=0, bytes_accessed=2048, transcendentals=0)


def swap(block, axis, offset):
    size = lax.axis_size(axis)
    return lax.ppermute(block, axis, [(i, i ^ offset) for i in range(size)])


def bit_count(axis):
    return lax.axis_size(axis).bit_length() - 1


def gather_members(block, beside):
    held = [block]
    mirrored = [swap(block, "mp", 1)]
    bits = bit_count("mp")
    for bit in reversed(range(1, bits)):
        others = [swap(item, "mp", 1 << bit) for item in held]
        if bit == bits - 1:
            others, beside = lax.optimization_barrier((others, beside))
        held = [item for pair in zip(held, others) for item in pair]
    return held, mirrored + [swap(item, "mp", 1) for item in held[1:]], beside


def core_hop(keep, send):
    return keep, swap(send.astype(bf16), "mp", 1)


def scatter_rest(keep, received, beside=None):
    held = keep.astype(f32) + received.astype(f32)
    for bit in range(1, bit_count("mp")):
        halves = held.reshape((-1, 2) + held.shape[1:])
        got = swap(halves[:, 1].astype(bf16), "mp", 1 << bit)
        if beside is not None and bit == 1:
            got, beside = lax.optimization_barrier((got, beside))
        held = halves[:, 0] + got.astype(f32)
    return held[0] if beside is None else (held[0], beside)


def exchange_groups(buffer):
    return lax.all_to_all(buffer, "dp", split_axis=0, concat_axis=0, tiled=True)


def halve(held, bit):
    mine = (lax.axis_index("dp") >> bit) & 1
    halves = held.reshape(2, held.shape[0] // 2, held.shape[1])
    got = swap(lax.dynamic_index_in_dim(halves, 1 - mine, 0, keepdims=False), "dp", 1 << bit)
    return lax.dynamic_index_in_dim(halves, mine, 0, keepdims=False), got


def joined_halves(keep, got):
    return (keep.astype(f32) + got.astype(f32)).astype(bf16)


def sum_rest(near):
    held = joined_halves(*near)
    for bit in range(1, bit_count("dp")):
        held = joined_halves(*halve(held, bit))
    held = held[None]
    for bit in reversed(range(1, bit_count("dp"))):
        held = jnp.concatenate([held, swap(held, "dp", 1 << bit)], axis=0)
    return held


def sum_rest_direct(near):
    rest = lax.axis_size("dp") // 2
    bits = bit_count("dp")
    mine = lax.axis_index("dp") >> 1
    held = joined_halves(*near)
    blocks = held.reshape(rest, held.shape[0] // rest, held.shape[1])
    reverse = [sum(((q >> bit) & 1) << (bits - 2 - bit) for bit in range(bits - 1)) for q in range(rest)]
    place = jnp.int32(0)
    for bit in range(bits - 1):
        place = place | (((mine >> bit) & 1) << (bits - 2 - bit))
    total = lax.dynamic_index_in_dim(blocks, place, 0, keepdims=False).astype(f32)
    got = [
        swap(lax.dynamic_index_in_dim(blocks, place ^ reverse[offset], 0, keepdims=False), "dp", 2 * offset)
        for offset in range(1, rest)
    ]
    for item in got:
        total = total + item.astype(f32)
    own = total.astype(bf16)
    gathered = {0: own}
    for offset in range(1, rest):
        gathered[reverse[offset]] = swap(own, "dp", 2 * offset)
    return jnp.stack([gathered[at] for at in range(rest)])


def last_step(own_half):
    other = swap(own_half, "dp", 1)
    both = jnp.stack([own_half, other])
    bits = bit_count("dp")
    me = lax.axis_index("dp")
    rows = []
    for half in range(2):
        for block in range(1 << (bits - 1)):
            at = jnp.int32(0)
            for bit in range(1, bits):
                differs = ((block >> (bits - 1 - bit)) & 1) ^ ((me >> bit) & 1)
                at = at + (differs << (bits - 1 - bit))
            rows.append(both[half ^ (me & 1), at])
    return jnp.concatenate(rows, axis=0).astype(f32)


def bias_kernel(block, shift_ref, table_ref, bucket_ref, bias_ref, moved_ref):
    shift = shift_ref[0]
    for at in range(table_ref.shape[1] // block):
        source = pl.multiple_of((at ^ shift) * block, block)
        labels = table_ref[:, pl.ds(source, block)]
        columns = slice(at * block, (at + 1) * block)
        moved_ref[:, columns] = labels
        for head in range(bucket_ref.shape[0]):
            row = jnp.broadcast_to(bucket_ref[head : head + 1, :], labels.shape)
            bias_ref[head, :, columns] = jnp.take_along_axis(row, labels, axis=1, mode="promise_in_bounds")


def make_bias(table, bucket_rows, shift, block):
    seq_len = table.shape[0]
    heads = bucket_rows.shape[0]
    return pl.pallas_call(
        functools.partial(bias_kernel, block),
        grid_spec=pltpu.PrefetchScalarGridSpec(
            num_scalar_prefetch=1,
            grid=(seq_len // block,),
            in_specs=[
                pl.BlockSpec((block, seq_len), lambda i, s: (i ^ s[0], 0)),
                pl.BlockSpec((heads, LANES), lambda i, s: (0, 0)),
            ],
            out_specs=[
                pl.BlockSpec((heads, block, seq_len), lambda i, s: (0, i, 0)),
                pl.BlockSpec((block, seq_len), lambda i, s: (i, 0)),
            ],
        ),
        out_shape=[
            jax.ShapeDtypeStruct((heads, seq_len, seq_len), f32),
            pltpu.HBM((seq_len, seq_len), jnp.int32),
        ],
        compiler_params=pltpu.CompilerParams(vmem_limit_bytes=8 * MIB),
        cost_estimate=small_cost,
        name="bias_lookup",
    )(shift, table, bucket_rows)


def bucket_kernel(buckets, table_ref, grad_ref, out_ref):
    seqs, heads, rows, seq_len = grad_ref.shape

    @pl.when(pl.program_id(0) == 0)
    def _():
        out_ref[...] = jnp.zeros_like(out_ref)

    labels = lax.broadcasted_iota(jnp.int32, (buckets, seq_len), 0).astype(f32).astype(bf16)
    table = table_ref[...].astype(f32).astype(bf16)
    one, zero = jnp.ones((), bf16), jnp.zeros((), bf16)
    onehot = jnp.concatenate([jnp.where(table[row : row + 1, :] == labels, one, zero) for row in range(rows)], axis=0)
    total = jnp.zeros((rows * buckets, heads * rows), f32)
    for seq in range(seqs):
        grads = grad_ref[seq].reshape(heads * rows, seq_len)
        total += lax.dot_general(onehot, grads, (((1,), (1,)), ((), ())), preferred_element_type=f32)
    own_row = lax.broadcasted_iota(jnp.int32, (rows, buckets, heads * rows), 0)
    its_row = lax.broadcasted_iota(jnp.int32, (rows, buckets, heads * rows), 2) % rows
    kept = jnp.where(own_row == its_row, total.reshape(rows, buckets, heads * rows), 0.0)
    out_ref[...] += jnp.sum(kept, axis=0)


def bucket_grad(table, score_grad, buckets):
    seqs, heads, seq_len, _ = score_grad.shape
    rows = 32
    out = pl.pallas_call(
        functools.partial(bucket_kernel, buckets),
        grid=(seq_len // rows,),
        in_specs=[
            pl.BlockSpec((rows, seq_len), lambda i: (i, 0)),
            pl.BlockSpec((seqs, heads, rows, seq_len), lambda i: (0, 0, i, 0)),
        ],
        out_specs=pl.BlockSpec((buckets, heads * rows), lambda i: (0, 0)),
        out_shape=jax.ShapeDtypeStruct((buckets, heads * rows), f32),
        compiler_params=pltpu.CompilerParams(vmem_limit_bytes=16 * MIB),
        cost_estimate=small_cost,
        name="bucket_grad",
    )(table, score_grad)
    return jnp.sum(out.reshape(buckets, heads, rows), axis=2)


def attend_kernel(
    head_size,
    *refs,
):
    *token_refs, gain_ref, query_ref, key_ref, value_ref, bias_ref, normed_ref, joined_ref, mixed_ref, probs_ref = refs
    seq_len, width = joined_ref.shape
    head_cols = width // 3
    pair_heads = bias_ref.shape[0]
    pair_cols = pair_heads * head_size
    block = token_refs[0].shape[0]

    @pl.when(pl.program_id(0) == 0)
    def _():
        for at, token_ref in enumerate(token_refs):
            values = token_ref[...].astype(f32)
            root = lax.rsqrt(jnp.mean(values * values, axis=-1, keepdims=True) + norm_eps)
            normed_ref[at * block : (at + 1) * block, :] = (values * root * gain_ref[...]).astype(bf16)
        for part, weight_ref in enumerate((query_ref, key_ref, value_ref)):
            joined_ref[:, part * head_cols : (part + 1) * head_cols] = jnp.dot(
                normed_ref[...], weight_ref[...], preferred_element_type=f32
            ).astype(bf16)

    start = pl.program_id(0) * pair_cols
    columns = [
        joined_ref[:, pl.ds(pl.multiple_of(start + part * head_cols, pair_cols), pair_cols)] for part in range(3)
    ]
    rows = min(512, seq_len)
    for chunk in range(seq_len // rows):
        picked = slice(chunk * rows, (chunk + 1) * rows)
        outs = []
        for head in range(pair_heads):
            cols = slice(head * head_size, (head + 1) * head_size)
            scores = lax.dot_general(
                columns[0][picked, cols], columns[1][:, cols], (((1,), (1,)), ((), ())), preferred_element_type=f32
            )
            scores = scores + bias_ref[head, picked, :]
            expo = jnp.exp(scores - jnp.max(scores, axis=-1, keepdims=True))
            probs = (expo * (1.0 / jnp.sum(expo, axis=-1, keepdims=True))).astype(bf16)
            probs_ref[0, head, picked, :] = probs
            outs.append(jnp.dot(probs, columns[2][:, cols], preferred_element_type=f32))
        mixed_ref[picked, :] = jnp.concatenate(outs, axis=1).astype(bf16)


def attend(blocks, gain, w_query, w_key, w_value, bias, head_size):
    heads, seq_len, _ = bias.shape
    block, width = blocks[0].shape
    head_cols = w_query.shape[1]
    pair = min(heads, LANES // head_size)
    weight = pl.BlockSpec((width, head_cols), lambda h: (0, 0))
    weights = [pltpu.with_memory_space_constraint(item, pltpu.HBM) for item in (w_query, w_key, w_value)]
    return pl.pallas_call(
        functools.partial(attend_kernel, head_size),
        grid=(heads // pair,),
        in_specs=[pl.BlockSpec((block, width), lambda h: (0, 0))] * len(blocks)
        + [
            pl.BlockSpec((1, width), lambda h: (0, 0)),
            weight,
            weight,
            weight,
            pl.BlockSpec((pair, seq_len, seq_len), lambda h: (h, 0, 0)),
        ],
        out_specs=[
            pl.BlockSpec((seq_len, width), lambda h: (0, 0)),
            pl.BlockSpec((seq_len, 3 * head_cols), lambda h: (0, 0)),
            pl.BlockSpec((seq_len, pair * head_size), lambda h: (0, h)),
            pl.BlockSpec((1, pair, seq_len, seq_len), lambda h: (0, h, 0, 0)),
        ],
        out_shape=[
            pltpu.HBM((seq_len, width), bf16),
            pltpu.HBM((seq_len, 3 * head_cols), bf16),
            jax.ShapeDtypeStruct((seq_len, head_cols), bf16),
            pltpu.HBM((1, heads, seq_len, seq_len), bf16),
        ],
        compiler_params=pltpu.CompilerParams(vmem_limit_bytes=24 * MIB),
        cost_estimate=small_cost,
        name="attend",
    )(*blocks, gain, *weights, bias)


def output_back_kernel(*refs):
    *block_refs, mixed_ref, weight_ref, mixed_grad_ref, part_ref = refs
    rows = jnp.concatenate([block_ref[...] for block_ref in block_refs], axis=0)
    part_ref[...] = lax.dot_general(
        mixed_ref[...], rows, (((0,), (0,)), ((), ())), preferred_element_type=f32
    ).astype(bf16)
    mixed_grad_ref[...] = lax.dot_general(
        rows, weight_ref[...], (((1,), (1,)), ((), ())), preferred_element_type=f32
    ).astype(bf16)


def output_back(blocks, mixed, weight):
    tokens, head_cols = mixed.shape
    width = weight.shape[1]
    return pl.pallas_call(
        output_back_kernel,
        out_shape=[
            jax.ShapeDtypeStruct((tokens, head_cols), bf16),
            jax.ShapeDtypeStruct((head_cols, width), bf16),
        ],
        compiler_params=pltpu.CompilerParams(vmem_limit_bytes=16 * MIB),
        cost_estimate=small_cost,
        name="output_back",
    )(*blocks, mixed, weight)


def attend_back_kernel(head_size, joined_ref, grad_ref, probs_ref, out_ref, score_ref):
    seq_len, width = joined_ref.shape
    head_cols = width // 3
    pair_heads = probs_ref.shape[1]
    pair_cols = pair_heads * head_size
    start = pl.program_id(1) * pair_cols

    def place(part):
        return pl.ds(pl.multiple_of(start + part * head_cols, pair_cols), pair_cols)

    queries, keys, values = [joined_ref[:, place(part)] for part in range(3)]
    grads = grad_ref[...]
    queries_t, grads_t = queries.T, grads.T
    rows = min(512, seq_len)
    query_parts = []
    key_t = [jnp.zeros((head_size, seq_len), f32) for _ in range(pair_heads)]
    value_t = [jnp.zeros((head_size, seq_len), f32) for _ in range(pair_heads)]
    for chunk in range(seq_len // rows):
        picked = slice(chunk * rows, (chunk + 1) * rows)
        outs = []
        for head in range(pair_heads):
            cols = slice(head * head_size, (head + 1) * head_size)
            probs_low = probs_ref[0, head, picked, :]
            probs = probs_low.astype(f32)
            prob_grad = lax.dot_general(
                grads[picked, cols], values[:, cols], (((1,), (1,)), ((), ())), preferred_element_type=f32
            )
            weighted = jnp.sum(probs * prob_grad, axis=-1, keepdims=True)
            score_grad = (probs * (prob_grad - weighted)).astype(bf16)
            score_ref[0, head, picked, :] = score_grad
            outs.append(jnp.dot(score_grad, keys[:, cols], preferred_element_type=f32))
            key_t[head] += jnp.dot(queries_t[cols, picked], score_grad, preferred_element_type=f32)
            value_t[head] += jnp.dot(grads_t[cols, picked], probs_low, preferred_element_type=f32)
        out_ref[picked, place(0)] = jnp.concatenate(outs, axis=1).astype(bf16)
    out_ref[:, place(1)] = jnp.concatenate(key_t, axis=0).T.astype(bf16)
    out_ref[:, place(2)] = jnp.concatenate(value_t, axis=0).T.astype(bf16)


def attend_back(joined, mixed_grad, probs, head_size):
    seqs, heads, seq_len, _ = probs.shape
    tokens, width = joined.shape
    pair = min(heads, LANES // head_size)
    return pl.pallas_call(
        functools.partial(attend_back_kernel, head_size),
        grid=(seqs, heads // pair),
        in_specs=[
            pl.BlockSpec((seq_len, width), lambda s, h: (s, 0)),
            pl.BlockSpec((seq_len, pair * head_size), lambda s, h: (s, h)),
            pl.BlockSpec((1, pair, seq_len, seq_len), lambda s, h: (s, h, 0, 0)),
        ],
        out_specs=[
            pl.BlockSpec((seq_len, width), lambda s, h: (s, 0)),
            pl.BlockSpec((1, pair, seq_len, seq_len), lambda s, h: (s, h, 0, 0)),
        ],
        out_shape=[
            jax.ShapeDtypeStruct((tokens, width), bf16),
            pltpu.HBM((seqs, heads, seq_len, seq_len), bf16),
        ],
        compiler_params=pltpu.CompilerParams(vmem_limit_bytes=20 * MIB),
        cost_estimate=small_cost,
        name="attend_back",
    )(joined, mixed_grad, probs)


gelu_scale = float(np.sqrt(2.0 / np.pi))


def gelu_parts(pre):
    bent = jnp.tanh(gelu_scale * (pre + 0.044715 * pre * pre * pre))
    return 0.5 * pre * (1.0 + bent), bent


def gelu_slope(pre):
    _, bent = gelu_parts(pre)
    return 0.5 * (1.0 + bent) + 0.5 * pre * (1.0 - bent * bent) * gelu_scale * (1.0 + 0.134145 * pre * pre)


def expert_kernel(cuts, middle_step, members, *refs):
    block_refs = refs[:members]
    order_ref, first_ref, second_ref, *middle_refs, inner_ref, rows_out, keep_ref, send_ref = refs[members:-6]
    first_held, second_held, inner_held, rows_ref, arrived, left = refs[-6:]
    half = members // 2
    all_rows, piece = block_refs[0].shape
    experts, _, picked = order_ref.shape
    expert_rows = picked // cuts
    loads = []
    for expert in range(experts):
        for at, (source, held) in enumerate(((first_ref, first_held), (second_ref, second_held))):
            load = pltpu.make_async_copy(source.at[expert], held.at[expert], arrived.at[2 * expert + at])
            load.start()
            loads.append(load)
    places = [
        (order_ref[expert] == lax.broadcasted_iota(jnp.int32, (all_rows, picked), 0)).astype(f32)
        for expert in range(experts)
    ]
    sorting = jnp.concatenate([place.T for place in places], axis=0).astype(bf16)
    for member in range(members):
        moved = jnp.dot(sorting, block_refs[member][...], preferred_element_type=f32).astype(bf16)
        for expert in range(experts):
            for cut in range(cuts):
                source = expert * picked + cut * expert_rows
                rows_ref[
                    expert, member * expert_rows : (member + 1) * expert_rows, cut * piece : (cut + 1) * piece
                ] = moved[source : source + expert_rows]
    stores = [pltpu.make_async_copy(rows_ref, rows_out, left.at[experts])]
    stores[0].start()
    results = []
    for expert in range(experts):
        loads[2 * expert].wait()
        inner = lax.dot_general(
            rows_ref[expert], first_held[expert], (((1,), (1,)), ((), ())), preferred_element_type=f32
        )
        inner = middle_step(expert, inner, *middle_refs)
        inner_held[expert] = inner
        stores.append(pltpu.make_async_copy(inner_held.at[expert], inner_ref.at[expert], left.at[expert]))
        stores[-1].start()
        loads[2 * expert + 1].wait()
        results.append(jnp.dot(inner, second_held[expert], preferred_element_type=f32).astype(bf16))
    unsorting = jnp.concatenate([place.astype(bf16) for place in places], axis=1)
    for member in range(members):
        parts = [
            result[member * expert_rows : (member + 1) * expert_rows, cut * piece : (cut + 1) * piece]
            for result in results
            for cut in range(cuts)
        ]
        placed = jnp.dot(unsorting, jnp.concatenate(parts, axis=0), preferred_element_type=f32).astype(bf16)
        target, at = (keep_ref, member) if member < half else (send_ref, member - half)
        target[at] = placed
    for store in stores:
        store.wait()


def forward_step(expert, inner, pre_ref):
    pre_ref[expert] = inner
    return gelu_parts(inner)[0].astype(bf16)


def backward_step(expert, inner, pre_ref):
    return (inner.astype(bf16).astype(f32) * gelu_slope(pre_ref[expert])).astype(bf16)


def run_experts(blocks, order, first, second, cuts, pre=None):
    members = len(blocks)
    experts, units, width = first.shape
    picked = order.shape[1]
    rows = members * (picked // cuts)
    part = jax.ShapeDtypeStruct((members // 2,) + blocks[0].shape, bf16)
    inside = pl.BlockSpec(memory_space=pltpu.VMEM)
    outside = pl.BlockSpec(memory_space=pltpu.HBM)
    first, second = [pltpu.with_memory_space_constraint(item, pltpu.HBM) for item in (first, second)]
    out_specs = [outside, outside, inside, inside]
    in_specs = [inside] * (members + 1) + [outside, outside]
    operands = [*blocks, order[:, None, :], first, second]
    out_shape = [pltpu.HBM((experts, rows, units), bf16), pltpu.HBM((experts, rows, width), bf16), part, part]
    if pre is None:
        step, name = forward_step, "experts"
        out_shape.insert(0, jax.ShapeDtypeStruct((experts, rows, units), f32))
        out_specs.insert(0, inside)
    else:
        step, name = backward_step, "experts_back"
        in_specs.append(inside)
        operands.append(pre)
    return pl.pallas_call(
        functools.partial(expert_kernel, cuts, step, members),
        in_specs=in_specs,
        out_specs=out_specs,
        out_shape=out_shape,
        scratch_shapes=[
            pltpu.VMEM((experts, units, width), bf16),
            pltpu.VMEM((experts, units, width), bf16),
            pltpu.VMEM((experts, rows, units), bf16),
            pltpu.VMEM((experts, rows, width), bf16),
            pltpu.SemaphoreType.DMA((2 * experts,)),
            pltpu.SemaphoreType.DMA((experts + 1,)),
        ],
        compiler_params=pltpu.CompilerParams(vmem_limit_bytes=26 * MIB),
        cost_estimate=small_cost,
        name=name,
    )(*operands)


def root_inverse(values):
    return lax.rsqrt(jnp.mean(values * values, axis=-1, keepdims=True) + norm_eps)


def shards(
    tokens,
    gain_attn,
    w_query,
    w_key,
    w_value,
    w_output,
    rel_bias,
    bucket_table,
    gain_moe,
    router,
    w_in,
    w_out,
    routes,
    slots,
    cotangent,
):
    group_count = lax.axis_size("dp")
    member_count = lax.axis_size("mp")
    member = lax.axis_index("mp")
    tok_dev, width = tokens.shape
    expert_local = w_in.shape[0]
    expert_count = expert_local * group_count
    capacity = max(2, (5 * tok_dev + 4 * expert_count - 1) // (4 * expert_count))
    seq_len = bucket_table.shape[0]
    head_cols = w_query.shape[1]
    head_local = rel_bias.shape[1]
    head_size = head_cols // head_local
    group_tokens = tok_dev * member_count
    seq_members = seq_len // tok_dev

    bucket_rows = jnp.pad(rel_bias.T, ((0, 0), (0, LANES - rel_bias.shape[0])))
    shift = (member % seq_members).astype(jnp.int32)[None]
    bias, moved_table = make_bias(bucket_table, bucket_rows, shift, tok_dev)
    near_tokens, far_tokens, (bias, moved_table) = gather_members(tokens, (bias, moved_table))
    token_blocks = [item for pair in zip(near_tokens, far_tokens) for item in pair]
    sequences = [
        attend(token_blocks[at : at + seq_members], gain_attn[None], w_query, w_key, w_value, bias, head_size)
        for at in range(0, member_count, seq_members)
    ]
    normed_low, joined, mixed, probs = [
        parts[0] if len(parts) == 1 else jnp.concatenate(parts, axis=0) for parts in zip(*sequences)
    ]
    mixed_pairs = mixed.reshape(member_count // 2, 2, tok_dev, head_cols)

    def project(rows):
        return jnp.einsum("stc,cd->std", rows, w_output, preferred_element_type=f32)

    attn_got = swap(project(mixed_pairs[:, 1]).astype(bf16), "mp", 1)
    attn = scatter_rest(project(mixed_pairs[:, 0]), attn_got)
    middle = tokens.astype(f32) + attn

    middle_root = root_inverse(middle)
    unit_moe = middle * middle_root
    moe_low = (unit_moe * gain_moe).astype(bf16)
    moe_rows = moe_low.astype(f32)
    router_t = router.T
    logits = lax.dot_general(
        moe_rows, router_t, (((1,), (1,)), ((), ())), precision=highest, preferred_element_type=f32
    )
    router_probs = jax.nn.softmax(logits, axis=-1)
    route_hot = (routes[:, None] == jnp.arange(expert_count, dtype=jnp.int32)[None, :]).astype(f32)
    gate_prob = jnp.sum(router_probs * route_hot, axis=-1, keepdims=True)

    chunk_slots = expert_local * capacity
    cuts = 1
    while cuts * chunk_slots % 8 != 0:
        cuts *= 2
    piece = width // cuts
    chunk_rows = cuts * chunk_slots
    all_rows = group_count * chunk_rows
    row_index = jnp.arange(all_rows, dtype=jnp.int32)
    row_chunk, row_cut, row_slot = (
        row_index // chunk_rows,
        (row_index // chunk_slots) % cuts,
        row_index % chunk_slots,
    )
    target = jnp.where(slots < capacity, routes * capacity + slots, -1)
    wanted = row_chunk * chunk_slots + row_slot
    hit = (wanted[:, None, None] == target[None, None, :]) & (
        row_cut[:, None, None] == jnp.arange(cuts, dtype=jnp.int32)[None, :, None]
    )
    placement = hit.astype(bf16).reshape(all_rows, cuts * tok_dev)

    def cut_rows(rows):
        return jnp.concatenate([rows[:, c * piece : (c + 1) * piece] for c in range(cuts)], axis=0)

    def join_rows(rows):
        return jnp.concatenate([rows[c * tok_dev : (c + 1) * tok_dev] for c in range(cuts)], axis=1)

    def send_rows(rows):
        return exchange_groups(jnp.dot(placement, cut_rows(rows), preferred_element_type=f32).astype(bf16))

    def place_back(back):
        rows = lax.dot_general(placement, back, (((0,), (0,)), ((), ())), preferred_element_type=f32)
        return join_rows(rows)

    order = np.arange(all_rows).reshape(group_count, cuts, expert_local, capacity).transpose(2, 1, 0, 3)
    order = jnp.asarray(order.reshape(expert_local, -1), jnp.int32)
    w_in_t = jnp.swapaxes(w_in, 1, 2)

    upstream = cotangent.astype(f32)
    sent = send_rows(moe_low)
    grad_sent = send_rows((gate_prob * upstream).astype(bf16))
    w_joined = jnp.concatenate([w_query, w_key, w_value], axis=1)
    near_rows, far_rows, (grad_sent, w_joined) = gather_members(sent, (grad_sent, w_joined))

    pre, hidden, expert_in, value_keep, value_send = run_experts(near_rows + far_rows, order, w_in_t, w_out, cuts)
    near_rows, far_rows, (value_keep, value_send) = gather_members(grad_sent, (value_keep, value_send))
    value_hop = core_hop(value_keep, value_send)
    pre_grad, result_grad, *rows_blocks = run_experts(near_rows + far_rows, order, w_out, w_in_t, cuts, pre)
    value_sum, rows_blocks = scatter_rest(*value_hop, beside=rows_blocks)
    rows_hop = core_hop(*rows_blocks)
    value_back = exchange_groups(value_sum.astype(bf16))
    rows_sum, value_back = scatter_rest(*rows_hop, beside=value_back)
    rows_back = exchange_groups(rows_sum.astype(bf16))
    grad_w_out = jnp.einsum("jrf,jrd->jfd", hidden, result_grad, preferred_element_type=f32)
    rows_back, grad_w_out = lax.optimization_barrier((rows_back, grad_w_out))
    grad_w_in_t = jnp.einsum("jrf,jrd->jfd", pre_grad, expert_in, preferred_element_type=f32)
    combined = place_back(value_back)
    moe_grad = place_back(rows_back)

    block_out = (middle + gate_prob * combined).astype(bf16)
    gate_grad = jnp.sum(upstream * combined, axis=-1, keepdims=True)
    logit_grad = router_probs * (route_hot * gate_grad - gate_prob * gate_grad)
    grad_router_t = lax.dot_general(
        logit_grad, moe_rows, (((0,), (0,)), ((), ())), precision=highest, preferred_element_type=f32
    )
    moe_grad = moe_grad + jnp.dot(logit_grad, router_t, precision=highest, preferred_element_type=f32)
    grad_gain_moe = jnp.sum(moe_grad * unit_moe, axis=0, keepdims=True)
    scaled = moe_grad * gain_moe
    middle_grad = upstream + middle_root * (
        scaled - unit_moe * jnp.mean(scaled * unit_moe, axis=-1, keepdims=True)
    )

    near_grads, far_grads, grad_w_in_t = gather_members(middle_grad.astype(bf16), grad_w_in_t)
    grad_w_in = jnp.swapaxes(grad_w_in_t, 1, 2)
    grad_blocks = [item for pair in zip(near_grads, far_grads) for item in pair]
    mixed_grad, output_part = output_back(grad_blocks, mixed, w_output)
    output_near = halve(output_part, 0)
    joined_grad, score_grad = attend_back(joined, mixed_grad, probs, head_size)
    output_near, joined_grad, token_blocks = lax.optimization_barrier((output_near, joined_grad, token_blocks))
    locals_ = []
    for half in range(2):
        columns = normed_low[:, half * (width // 2) : (half + 1) * (width // 2)]
        locals_.append(jnp.einsum("td,tc->dc", columns, joined_grad, preferred_element_type=f32).astype(bf16))
    locals_, joined_grad, score_grad = lax.optimization_barrier((locals_, joined_grad, score_grad))
    first_near = halve(locals_[0], 0)
    second_near = halve(locals_[1], 0)
    attn_partial = jnp.einsum("tc,dc->td", joined_grad, w_joined, preferred_element_type=f32)
    attn_pairs = attn_partial.reshape(member_count // 2, 2, tok_dev, width)
    attn_hop = core_hop(attn_pairs[:, 0], attn_pairs[:, 1])
    all_tokens = jnp.concatenate(token_blocks, axis=0).astype(f32)
    gain_partial = jnp.sum(attn_partial * (all_tokens * root_inverse(all_tokens)), axis=0, keepdims=True)
    bucket_part = bucket_grad(moved_table, score_grad, rel_bias.shape[0])
    first_near, attn_hop, bucket_part, gain_partial, output_near = lax.optimization_barrier(
        (first_near, attn_hop, bucket_part, gain_partial, output_near)
    )
    bucket_row = lax.dynamic_update_slice(
        jnp.zeros((1, width), f32), bucket_part.reshape(1, -1), (0, member * bucket_part.size)
    )
    small = jnp.concatenate([grad_gain_moe, gain_partial, bucket_row, grad_router_t], axis=0)
    for axis in ("mp", "dp"):
        for bit in range(bit_count(axis)):
            small = small + swap(small, axis, 1 << bit)
    attn_grad = scatter_rest(*attn_hop)
    grad_w_output = last_step(sum_rest(output_near))
    grad_joined = jnp.concatenate([last_step(sum_rest_direct(first_near)), last_step(sum_rest_direct(second_near))], axis=0)
    grad_w_query, grad_w_key, grad_w_value = [
        grad_joined[:, part * head_cols : (part + 1) * head_cols] for part in range(3)
    ]
    own_tokens = tokens.astype(f32)
    own_root = root_inverse(own_tokens)
    own_unit = own_tokens * own_root
    scaled = attn_grad * gain_attn
    input_grad = (
        middle_grad + own_root * (scaled - own_unit * jnp.mean(scaled * own_unit, axis=-1, keepdims=True))
    ).astype(bf16)
    grad_rel_bias = lax.dynamic_slice(small[2:3], (0, member * bucket_part.size), (1, bucket_part.size))
    grad_rel_bias = grad_rel_bias.reshape(bucket_part.shape)
    return (
        block_out,
        input_grad,
        small[1],
        grad_w_query,
        grad_w_key,
        grad_w_value,
        grad_w_output,
        grad_rel_bias,
        small[0],
        small[3:].T,
        grad_w_in,
        grad_w_out,
    )


def solution(mesh):
    in_specs = (
        P(("dp", "mp"), None),
        P(),
        P(None, "mp"),
        P(None, "mp"),
        P(None, "mp"),
        P("mp", None),
        P(None, "mp"),
        P(),
        P(),
        P(),
        P("dp", None, "mp"),
        P("dp", "mp", None),
        P(("dp", "mp")),
        P(("dp", "mp")),
        P(("dp", "mp"), None),
    )
    out_specs = (
        P(("dp", "mp"), None),
        P(("dp", "mp"), None),
        P(),
        P(None, "mp"),
        P(None, "mp"),
        P(None, "mp"),
        P("mp", None),
        P(None, "mp"),
        P(),
        P(),
        P("dp", None, "mp"),
        P("dp", "mp", None),
    )
    return jax.shard_map(shards, mesh=mesh, in_specs=in_specs, out_specs=out_specs, check_vma=False)
```

```python
import functools

import jax
import jax.numpy as jnp
import numpy as np
from jax import lax
from jax.experimental import pallas as pl
from jax.experimental.pallas import tpu as pltpu
from jax.sharding import PartitionSpec as P

norm_eps = 1e-06
highest = lax.Precision.HIGHEST
bf16 = jnp.bfloat16
f32 = jnp.float32
LANES = 128
MIB = 1 << 20
small_cost = pl.CostEstimate(flops=0, bytes_accessed=2048, transcendentals=0)


def swap(block, axis, offset):
    size = lax.axis_size(axis)
    return lax.ppermute(block, axis, [(i, i ^ offset) for i in range(size)])


def bit_count(axis):
    return lax.axis_size(axis).bit_length() - 1


def gather_members(block, beside):
    held = [block]
    mirrored = [swap(block, "mp", 1)]
    bits = bit_count("mp")
    for bit in reversed(range(1, bits)):
        others = [swap(item, "mp", 1 << bit) for item in held]
        if bit == bits - 1:
            others, beside = lax.optimization_barrier((others, beside))
        held = [item for pair in zip(held, others) for item in pair]
    return held, mirrored + [swap(item, "mp", 1) for item in held[1:]], beside


def core_hop(keep, send):
    return keep, swap(send.astype(bf16), "mp", 1)


def scatter_rest(keep, received, beside=None):
    held = keep.astype(f32) + received.astype(f32)
    for bit in range(1, bit_count("mp")):
        halves = held.reshape((-1, 2) + held.shape[1:])
        got = swap(halves[:, 1].astype(bf16), "mp", 1 << bit)
        if beside is not None and bit == 1:
            got, beside = lax.optimization_barrier((got, beside))
        held = halves[:, 0] + got.astype(f32)
    return held[0] if beside is None else (held[0], beside)


def exchange_groups(buffer):
    return lax.all_to_all(buffer, "dp", split_axis=0, concat_axis=0, tiled=True)


def halve(held, bit):
    mine = (lax.axis_index("dp") >> bit) & 1
    halves = held.reshape(2, held.shape[0] // 2, held.shape[1])
    got = swap(lax.dynamic_index_in_dim(halves, 1 - mine, 0, keepdims=False), "dp", 1 << bit)
    return lax.dynamic_index_in_dim(halves, mine, 0, keepdims=False), got


def joined_halves(keep, got):
    return (keep.astype(f32) + got.astype(f32)).astype(bf16)


def sum_rest(near):
    held = joined_halves(*near)
    for bit in range(1, bit_count("dp")):
        held = joined_halves(*halve(held, bit))
    held = held[None]
    for bit in reversed(range(1, bit_count("dp"))):
        held = jnp.concatenate([held, swap(held, "dp", 1 << bit)], axis=0)
    return held


def sum_rest_direct(near):
    rest = lax.axis_size("dp") // 2
    bits = bit_count("dp")
    mine = lax.axis_index("dp") >> 1
    held = joined_halves(*near)
    blocks = held.reshape(rest, held.shape[0] // rest, held.shape[1])
    reverse = [sum(((q >> bit) & 1) << (bits - 2 - bit) for bit in range(bits - 1)) for q in range(rest)]
    place = jnp.int32(0)
    for bit in range(bits - 1):
        place = place | (((mine >> bit) & 1) << (bits - 2 - bit))
    total = lax.dynamic_index_in_dim(blocks, place, 0, keepdims=False).astype(f32)
    got = [
        swap(lax.dynamic_index_in_dim(blocks, place ^ reverse[offset], 0, keepdims=False), "dp", 2 * offset)
        for offset in range(1, rest)
    ]
    for item in got:
        total = total + item.astype(f32)
    own = total.astype(bf16)
    gathered = {0: own}
    for offset in range(1, rest):
        gathered[reverse[offset]] = swap(own, "dp", 2 * offset)
    return jnp.stack([gathered[at] for at in range(rest)])


def last_step(own_half):
    other = swap(own_half, "dp", 1)
    both = jnp.stack([own_half, other])
    bits = bit_count("dp")
    me = lax.axis_index("dp")
    rows = []
    for half in range(2):
        for block in range(1 << (bits - 1)):
            at = jnp.int32(0)
            for bit in range(1, bits):
                differs = ((block >> (bits - 1 - bit)) & 1) ^ ((me >> bit) & 1)
                at = at + (differs << (bits - 1 - bit))
            rows.append(both[half ^ (me & 1), at])
    return jnp.concatenate(rows, axis=0).astype(f32)


def bias_kernel(block, shift_ref, table_ref, bucket_ref, bias_ref, moved_ref):
    shift = shift_ref[0]
    for at in range(table_ref.shape[1] // block):
        source = pl.multiple_of((at ^ shift) * block, block)
        labels = table_ref[:, pl.ds(source, block)]
        columns = slice(at * block, (at + 1) * block)
        moved_ref[:, columns] = labels
        for head in range(bucket_ref.shape[0]):
            row = jnp.broadcast_to(bucket_ref[head : head + 1, :], labels.shape)
            bias_ref[head, :, columns] = jnp.take_along_axis(row, labels, axis=1, mode="promise_in_bounds")


def make_bias(table, bucket_rows, shift, block):
    seq_len = table.shape[0]
    heads = bucket_rows.shape[0]
    return pl.pallas_call(
        functools.partial(bias_kernel, block),
        grid_spec=pltpu.PrefetchScalarGridSpec(
            num_scalar_prefetch=1,
            grid=(seq_len // block,),
            in_specs=[
                pl.BlockSpec((block, seq_len), lambda i, s: (i ^ s[0], 0)),
                pl.BlockSpec((heads, LANES), lambda i, s: (0, 0)),
            ],
            out_specs=[
                pl.BlockSpec((heads, block, seq_len), lambda i, s: (0, i, 0)),
                pl.BlockSpec((block, seq_len), lambda i, s: (i, 0)),
            ],
        ),
        out_shape=[
            jax.ShapeDtypeStruct((heads, seq_len, seq_len), f32),
            pltpu.HBM((seq_len, seq_len), jnp.int32),
        ],
        compiler_params=pltpu.CompilerParams(vmem_limit_bytes=8 * MIB),
        cost_estimate=small_cost,
        name="bias_lookup",
    )(shift, table, bucket_rows)


def bucket_kernel(buckets, table_ref, grad_ref, out_ref):
    seqs, heads, rows, seq_len = grad_ref.shape

    @pl.when(pl.program_id(0) == 0)
    def _():
        out_ref[...] = jnp.zeros_like(out_ref)

    labels = lax.broadcasted_iota(jnp.int32, (buckets, seq_len), 0).astype(f32).astype(bf16)
    table = table_ref[...].astype(f32).astype(bf16)
    one, zero = jnp.ones((), bf16), jnp.zeros((), bf16)
    onehot = jnp.concatenate([jnp.where(table[row : row + 1, :] == labels, one, zero) for row in range(rows)], axis=0)
    total = jnp.zeros((rows * buckets, heads * rows), f32)
    for seq in range(seqs):
        grads = grad_ref[seq].reshape(heads * rows, seq_len)
        total += lax.dot_general(onehot, grads, (((1,), (1,)), ((), ())), preferred_element_type=f32)
    own_row = lax.broadcasted_iota(jnp.int32, (rows, buckets, heads * rows), 0)
    its_row = lax.broadcasted_iota(jnp.int32, (rows, buckets, heads * rows), 2) % rows
    kept = jnp.where(own_row == its_row, total.reshape(rows, buckets, heads * rows), 0.0)
    out_ref[...] += jnp.sum(kept, axis=0)


def bucket_grad(table, score_grad, buckets):
    seqs, heads, seq_len, _ = score_grad.shape
    rows = 32
    out = pl.pallas_call(
        functools.partial(bucket_kernel, buckets),
        grid=(seq_len // rows,),
        in_specs=[
            pl.BlockSpec((rows, seq_len), lambda i: (i, 0)),
            pl.BlockSpec((seqs, heads, rows, seq_len), lambda i: (0, 0, i, 0)),
        ],
        out_specs=pl.BlockSpec((buckets, heads * rows), lambda i: (0, 0)),
        out_shape=jax.ShapeDtypeStruct((buckets, heads * rows), f32),
        compiler_params=pltpu.CompilerParams(vmem_limit_bytes=16 * MIB),
        cost_estimate=small_cost,
        name="bucket_grad",
    )(table, score_grad)
    return jnp.sum(out.reshape(buckets, heads, rows), axis=2)


def attend_kernel(
    head_size,
    *refs,
):
    *token_refs, gain_ref, query_ref, key_ref, value_ref, bias_ref, normed_ref, joined_ref, mixed_ref, probs_ref = refs
    seq_len, width = joined_ref.shape
    head_cols = width // 3
    pair_heads = bias_ref.shape[0]
    pair_cols = pair_heads * head_size
    block = token_refs[0].shape[0]

    @pl.when(pl.program_id(0) == 0)
    def _():
        for at, token_ref in enumerate(token_refs):
            values = token_ref[...].astype(f32)
            root = lax.rsqrt(jnp.mean(values * values, axis=-1, keepdims=True) + norm_eps)
            normed_ref[at * block : (at + 1) * block, :] = (values * root * gain_ref[...]).astype(bf16)
        for part, weight_ref in enumerate((query_ref, key_ref, value_ref)):
            joined_ref[:, part * head_cols : (part + 1) * head_cols] = jnp.dot(
                normed_ref[...], weight_ref[...], preferred_element_type=f32
            ).astype(bf16)

    start = pl.program_id(0) * pair_cols
    columns = [
        joined_ref[:, pl.ds(pl.multiple_of(start + part * head_cols, pair_cols), pair_cols)] for part in range(3)
    ]
    rows = min(512, seq_len)
    for chunk in range(seq_len // rows):
        picked = slice(chunk * rows, (chunk + 1) * rows)
        outs = []
        for head in range(pair_heads):
            cols = slice(head * head_size, (head + 1) * head_size)
            scores = lax.dot_general(
                columns[0][picked, cols], columns[1][:, cols], (((1,), (1,)), ((), ())), preferred_element_type=f32
            )
            scores = scores + bias_ref[head, picked, :]
            expo = jnp.exp(scores - jnp.max(scores, axis=-1, keepdims=True))
            probs = (expo * (1.0 / jnp.sum(expo, axis=-1, keepdims=True))).astype(bf16)
            probs_ref[0, head, picked, :] = probs
            outs.append(jnp.dot(probs, columns[2][:, cols], preferred_element_type=f32))
        mixed_ref[picked, :] = jnp.concatenate(outs, axis=1).astype(bf16)


def attend(blocks, gain, w_query, w_key, w_value, bias, head_size):
    heads, seq_len, _ = bias.shape
    block, width = blocks[0].shape
    head_cols = w_query.shape[1]
    pair = min(heads, LANES // head_size)
    weight = pl.BlockSpec((width, head_cols), lambda h: (0, 0))
    gain, *weights = [pltpu.with_memory_space_constraint(item, pltpu.HBM) for item in (gain, w_query, w_key, w_value)]
    blocks = [pltpu.with_memory_space_constraint(blocks[0], pltpu.HBM)] + blocks[1:]
    return pl.pallas_call(
        functools.partial(attend_kernel, head_size),
        grid=(heads // pair,),
        in_specs=[pl.BlockSpec((block, width), lambda h: (0, 0))] * len(blocks)
        + [
            pl.BlockSpec((1, width), lambda h: (0, 0)),
            weight,
            weight,
            weight,
            pl.BlockSpec((pair, seq_len, seq_len), lambda h: (h, 0, 0)),
        ],
        out_specs=[
            pl.BlockSpec((seq_len, width), lambda h: (0, 0)),
            pl.BlockSpec((seq_len, 3 * head_cols), lambda h: (0, 0)),
            pl.BlockSpec((seq_len, pair * head_size), lambda h: (0, h)),
            pl.BlockSpec((1, pair, seq_len, seq_len), lambda h: (0, h, 0, 0)),
        ],
        out_shape=[
            pltpu.HBM((seq_len, width), bf16),
            pltpu.HBM((seq_len, 3 * head_cols), bf16),
            jax.ShapeDtypeStruct((seq_len, head_cols), bf16),
            pltpu.HBM((1, heads, seq_len, seq_len), bf16),
        ],
        compiler_params=pltpu.CompilerParams(vmem_limit_bytes=24 * MIB),
        cost_estimate=small_cost,
        name="attend",
    )(*blocks, gain, *weights, bias)


def output_back_kernel(*refs):
    *block_refs, mixed_ref, weight_ref, mixed_grad_ref, part_ref = refs
    rows = jnp.concatenate([block_ref[...] for block_ref in block_refs], axis=0)
    part_ref[...] = lax.dot_general(
        mixed_ref[...], rows, (((0,), (0,)), ((), ())), preferred_element_type=f32
    ).astype(bf16)
    mixed_grad_ref[...] = lax.dot_general(
        rows, weight_ref[...], (((1,), (1,)), ((), ())), preferred_element_type=f32
    ).astype(bf16)


def output_back(blocks, mixed, weight):
    tokens, head_cols = mixed.shape
    width = weight.shape[1]
    return pl.pallas_call(
        output_back_kernel,
        out_shape=[
            jax.ShapeDtypeStruct((tokens, head_cols), bf16),
            jax.ShapeDtypeStruct((head_cols, width), bf16),
        ],
        compiler_params=pltpu.CompilerParams(vmem_limit_bytes=16 * MIB),
        cost_estimate=small_cost,
        name="output_back",
    )(*blocks, mixed, weight)


def attend_back_kernel(head_size, joined_ref, grad_ref, probs_ref, out_ref, score_ref):
    seq_len, width = joined_ref.shape
    head_cols = width // 3
    pair_heads = probs_ref.shape[1]
    pair_cols = pair_heads * head_size
    start = pl.program_id(1) * pair_cols

    def place(part):
        return pl.ds(pl.multiple_of(start + part * head_cols, pair_cols), pair_cols)

    queries, keys, values = [joined_ref[:, place(part)] for part in range(3)]
    grads = grad_ref[...]
    queries_t, grads_t = queries.T, grads.T
    rows = min(512, seq_len)
    query_parts = []
    key_t = [jnp.zeros((head_size, seq_len), f32) for _ in range(pair_heads)]
    value_t = [jnp.zeros((head_size, seq_len), f32) for _ in range(pair_heads)]
    for chunk in range(seq_len // rows):
        picked = slice(chunk * rows, (chunk + 1) * rows)
        outs = []
        for head in range(pair_heads):
            cols = slice(head * head_size, (head + 1) * head_size)
            probs_low = probs_ref[0, head, picked, :]
            probs = probs_low.astype(f32)
            prob_grad = lax.dot_general(
                grads[picked, cols], values[:, cols], (((1,), (1,)), ((), ())), preferred_element_type=f32
            )
            weighted = jnp.sum(probs * prob_grad, axis=-1, keepdims=True)
            score_grad = (probs * (prob_grad - weighted)).astype(bf16)
            score_ref[0, head, picked, :] = score_grad
            outs.append(jnp.dot(score_grad, keys[:, cols], preferred_element_type=f32))
            key_t[head] += jnp.dot(queries_t[cols, picked], score_grad, preferred_element_type=f32)
            value_t[head] += jnp.dot(grads_t[cols, picked], probs_low, preferred_element_type=f32)
        out_ref[picked, place(0)] = jnp.concatenate(outs, axis=1).astype(bf16)
    out_ref[:, place(1)] = jnp.concatenate(key_t, axis=0).T.astype(bf16)
    out_ref[:, place(2)] = jnp.concatenate(value_t, axis=0).T.astype(bf16)


def attend_back(joined, mixed_grad, probs, head_size):
    seqs, heads, seq_len, _ = probs.shape
    tokens, width = joined.shape
    pair = min(heads, LANES // head_size)
    return pl.pallas_call(
        functools.partial(attend_back_kernel, head_size),
        grid=(seqs, heads // pair),
        in_specs=[
            pl.BlockSpec((seq_len, width), lambda s, h: (s, 0)),
            pl.BlockSpec((seq_len, pair * head_size), lambda s, h: (s, h)),
            pl.BlockSpec((1, pair, seq_len, seq_len), lambda s, h: (s, h, 0, 0)),
        ],
        out_specs=[
            pl.BlockSpec((seq_len, width), lambda s, h: (s, 0)),
            pl.BlockSpec((1, pair, seq_len, seq_len), lambda s, h: (s, h, 0, 0)),
        ],
        out_shape=[
            jax.ShapeDtypeStruct((tokens, width), bf16),
            pltpu.HBM((seqs, heads, seq_len, seq_len), bf16),
        ],
        compiler_params=pltpu.CompilerParams(vmem_limit_bytes=20 * MIB),
        cost_estimate=small_cost,
        name="attend_back",
    )(joined, mixed_grad, probs)


gelu_scale = float(np.sqrt(2.0 / np.pi))


def gelu_parts(pre):
    bent = jnp.tanh(gelu_scale * (pre + 0.044715 * pre * pre * pre))
    return 0.5 * pre * (1.0 + bent), bent


def gelu_slope(pre):
    _, bent = gelu_parts(pre)
    return 0.5 * (1.0 + bent) + 0.5 * pre * (1.0 - bent * bent) * gelu_scale * (1.0 + 0.134145 * pre * pre)


def expert_kernel(cuts, middle_step, members, *refs):
    block_refs = refs[:members]
    order_ref, first_ref, second_ref, *middle_refs, inner_ref, rows_out, keep_ref, send_ref = refs[members:-6]
    first_held, second_held, inner_held, rows_ref, arrived, left = refs[-6:]
    half = members // 2
    all_rows, piece = block_refs[0].shape
    experts, _, picked = order_ref.shape
    expert_rows = picked // cuts
    loads = []
    for expert in range(experts):
        for at, (source, held) in enumerate(((first_ref, first_held), (second_ref, second_held))):
            loads.append(pltpu.make_async_copy(source.at[expert], held.at[expert], arrived.at[2 * expert + at]))
    for load in loads[:2]:
        load.start()
    places = [
        (order_ref[expert] == lax.broadcasted_iota(jnp.int32, (all_rows, picked), 0)).astype(f32)
        for expert in range(experts)
    ]
    sorting = jnp.concatenate([place.T for place in places], axis=0).astype(bf16)
    for member in range(members):
        moved = jnp.dot(sorting, block_refs[member][...], preferred_element_type=f32).astype(bf16)
        for expert in range(experts):
            for cut in range(cuts):
                source = expert * picked + cut * expert_rows
                rows_ref[
                    expert, member * expert_rows : (member + 1) * expert_rows, cut * piece : (cut + 1) * piece
                ] = moved[source : source + expert_rows]
    stores = [pltpu.make_async_copy(rows_ref, rows_out, left.at[experts])]
    stores[0].start()
    results = []
    for expert in range(experts):
        loads[2 * expert].wait()
        if 2 * expert + 2 < len(loads):
            loads[2 * expert + 2].start()
            loads[2 * expert + 3].start()
        inner = lax.dot_general(
            rows_ref[expert], first_held[expert], (((1,), (1,)), ((), ())), preferred_element_type=f32
        )
        inner = middle_step(expert, inner, *middle_refs)
        inner_held[expert] = inner
        stores.append(pltpu.make_async_copy(inner_held.at[expert], inner_ref.at[expert], left.at[expert]))
        stores[-1].start()
        loads[2 * expert + 1].wait()
        results.append(jnp.dot(inner, second_held[expert], preferred_element_type=f32).astype(bf16))
    unsorting = jnp.concatenate([place.astype(bf16) for place in places], axis=1)
    for member in range(members):
        parts = [
            result[member * expert_rows : (member + 1) * expert_rows, cut * piece : (cut + 1) * piece]
            for result in results
            for cut in range(cuts)
        ]
        placed = jnp.dot(unsorting, jnp.concatenate(parts, axis=0), preferred_element_type=f32).astype(bf16)
        target, at = (keep_ref, member) if member < half else (send_ref, member - half)
        target[at] = placed
    for store in stores:
        store.wait()


def forward_step(expert, inner, pre_ref):
    pre_ref[expert] = inner
    return gelu_parts(inner)[0].astype(bf16)


def backward_step(expert, inner, pre_ref):
    return (inner.astype(bf16).astype(f32) * gelu_slope(pre_ref[expert])).astype(bf16)


def run_experts(blocks, order, first, second, cuts, pre=None):
    members = len(blocks)
    experts, units, width = first.shape
    picked = order.shape[1]
    rows = members * (picked // cuts)
    part = jax.ShapeDtypeStruct((members // 2,) + blocks[0].shape, bf16)
    inside = pl.BlockSpec(memory_space=pltpu.VMEM)
    outside = pl.BlockSpec(memory_space=pltpu.HBM)
    first, second = [pltpu.with_memory_space_constraint(item, pltpu.HBM) for item in (first, second)]
    out_specs = [outside, outside, inside, inside]
    in_specs = [inside] * (members + 1) + [outside, outside]
    operands = [*blocks, order[:, None, :], first, second]
    out_shape = [pltpu.HBM((experts, rows, units), bf16), pltpu.HBM((experts, rows, width), bf16), part, part]
    if pre is None:
        step, name = forward_step, "experts"
        out_shape.insert(0, jax.ShapeDtypeStruct((experts, rows, units), f32))
        out_specs.insert(0, inside)
    else:
        step, name = backward_step, "experts_back"
        in_specs.append(inside)
        operands.append(pre)
    return pl.pallas_call(
        functools.partial(expert_kernel, cuts, step, members),
        in_specs=in_specs,
        out_specs=out_specs,
        out_shape=out_shape,
        scratch_shapes=[
            pltpu.VMEM((experts, units, width), bf16),
            pltpu.VMEM((experts, units, width), bf16),
            pltpu.VMEM((experts, rows, units), bf16),
            pltpu.VMEM((experts, rows, width), bf16),
            pltpu.SemaphoreType.DMA((2 * experts,)),
            pltpu.SemaphoreType.DMA((experts + 1,)),
        ],
        compiler_params=pltpu.CompilerParams(vmem_limit_bytes=26 * MIB),
        cost_estimate=small_cost,
        name=name,
    )(*operands)


def root_inverse(values):
    return lax.rsqrt(jnp.mean(values * values, axis=-1, keepdims=True) + norm_eps)


def shards(
    tokens,
    gain_attn,
    w_query,
    w_key,
    w_value,
    w_output,
    rel_bias,
    bucket_table,
    gain_moe,
    router,
    w_in,
    w_out,
    routes,
    slots,
    cotangent,
):
    group_count = lax.axis_size("dp")
    member_count = lax.axis_size("mp")
    member = lax.axis_index("mp")
    tok_dev, width = tokens.shape
    expert_local = w_in.shape[0]
    expert_count = expert_local * group_count
    capacity = max(2, (5 * tok_dev + 4 * expert_count - 1) // (4 * expert_count))
    seq_len = bucket_table.shape[0]
    head_cols = w_query.shape[1]
    head_local = rel_bias.shape[1]
    head_size = head_cols // head_local
    group_tokens = tok_dev * member_count
    seq_members = seq_len // tok_dev

    bucket_rows = jnp.pad(rel_bias.T, ((0, 0), (0, LANES - rel_bias.shape[0])))
    shift = (member % seq_members).astype(jnp.int32)[None]
    bias, moved_table = make_bias(bucket_table, bucket_rows, shift, tok_dev)
    near_tokens, far_tokens, (bias, moved_table) = gather_members(tokens, (bias, moved_table))
    token_blocks = [item for pair in zip(near_tokens, far_tokens) for item in pair]
    sequences = [
        attend(token_blocks[at : at + seq_members], gain_attn[None], w_query, w_key, w_value, bias, head_size)
        for at in range(0, member_count, seq_members)
    ]
    normed_low, joined, mixed, probs = [
        parts[0] if len(parts) == 1 else jnp.concatenate(parts, axis=0) for parts in zip(*sequences)
    ]
    mixed_pairs = mixed.reshape(member_count // 2, 2, tok_dev, head_cols)

    def project(rows):
        return jnp.einsum("stc,cd->std", rows, w_output, preferred_element_type=f32)

    attn_got = swap(project(mixed_pairs[:, 1]).astype(bf16), "mp", 1)
    attn = scatter_rest(project(mixed_pairs[:, 0]), attn_got)
    middle = tokens.astype(f32) + attn

    middle_root = root_inverse(middle)
    unit_moe = middle * middle_root
    moe_low = (unit_moe * gain_moe).astype(bf16)
    moe_rows = moe_low.astype(f32)
    router_t = router.T
    logits = lax.dot_general(
        moe_rows, router_t, (((1,), (1,)), ((), ())), precision=highest, preferred_element_type=f32
    )
    router_probs = jax.nn.softmax(logits, axis=-1)
    route_hot = (routes[:, None] == jnp.arange(expert_count, dtype=jnp.int32)[None, :]).astype(f32)
    gate_prob = jnp.sum(router_probs * route_hot, axis=-1, keepdims=True)

    chunk_slots = expert_local * capacity
    cuts = 1
    while cuts * chunk_slots % 8 != 0:
        cuts *= 2
    piece = width // cuts
    chunk_rows = cuts * chunk_slots
    all_rows = group_count * chunk_rows
    row_index = jnp.arange(all_rows, dtype=jnp.int32)
    row_chunk, row_cut, row_slot = (
        row_index // chunk_rows,
        (row_index // chunk_slots) % cuts,
        row_index % chunk_slots,
    )
    target = jnp.where(slots < capacity, routes * capacity + slots, -1)
    wanted = row_chunk * chunk_slots + row_slot
    hit = (wanted[:, None, None] == target[None, None, :]) & (
        row_cut[:, None, None] == jnp.arange(cuts, dtype=jnp.int32)[None, :, None]
    )
    placement = hit.astype(bf16).reshape(all_rows, cuts * tok_dev)

    def cut_rows(rows):
        return jnp.concatenate([rows[:, c * piece : (c + 1) * piece] for c in range(cuts)], axis=0)

    def join_rows(rows):
        return jnp.concatenate([rows[c * tok_dev : (c + 1) * tok_dev] for c in range(cuts)], axis=1)

    def send_rows(rows):
        return exchange_groups(jnp.dot(placement, cut_rows(rows), preferred_element_type=f32).astype(bf16))

    def place_back(back):
        rows = lax.dot_general(placement, back, (((0,), (0,)), ((), ())), preferred_element_type=f32)
        return join_rows(rows)

    order = np.arange(all_rows).reshape(group_count, cuts, expert_local, capacity).transpose(2, 1, 0, 3)
    order = jnp.asarray(order.reshape(expert_local, -1), jnp.int32)
    w_in_t = jnp.swapaxes(w_in, 1, 2)

    upstream = cotangent.astype(f32)
    sent = send_rows(moe_low)
    grad_sent = send_rows((gate_prob * upstream).astype(bf16))
    w_joined = jnp.concatenate([w_query, w_key, w_value], axis=1)
    near_rows, far_rows, (grad_sent, w_joined) = gather_members(sent, (grad_sent, w_joined))

    pre, hidden, expert_in, value_keep, value_send = run_experts(near_rows + far_rows, order, w_in_t, w_out, cuts)
    near_rows, far_rows, (value_keep, value_send) = gather_members(grad_sent, (value_keep, value_send))
    value_hop = core_hop(value_keep, value_send)
    pre_grad, result_grad, *rows_blocks = run_experts(near_rows + far_rows, order, w_out, w_in_t, cuts, pre)
    value_sum, rows_blocks = scatter_rest(*value_hop, beside=rows_blocks)
    rows_hop = core_hop(*rows_blocks)
    value_back = exchange_groups(value_sum.astype(bf16))
    rows_sum, value_back = scatter_rest(*rows_hop, beside=value_back)
    rows_back = exchange_groups(rows_sum.astype(bf16))
    grad_w_out = jnp.einsum("jrf,jrd->jfd", hidden, result_grad, preferred_element_type=f32)
    rows_back, grad_w_out = lax.optimization_barrier((rows_back, grad_w_out))
    grad_w_in_t = jnp.einsum("jrf,jrd->jfd", pre_grad, expert_in, preferred_element_type=f32)
    combined = place_back(value_back)
    moe_grad = place_back(rows_back)

    block_out = (middle + gate_prob * combined).astype(bf16)
    gate_grad = jnp.sum(upstream * combined, axis=-1, keepdims=True)
    logit_grad = router_probs * (route_hot * gate_grad - gate_prob * gate_grad)
    grad_router_t = lax.dot_general(
        logit_grad, moe_rows, (((0,), (0,)), ((), ())), precision=highest, preferred_element_type=f32
    )
    moe_grad = moe_grad + jnp.dot(logit_grad, router_t, precision=highest, preferred_element_type=f32)
    grad_gain_moe = jnp.sum(moe_grad * unit_moe, axis=0, keepdims=True)
    scaled = moe_grad * gain_moe
    middle_grad = upstream + middle_root * (
        scaled - unit_moe * jnp.mean(scaled * unit_moe, axis=-1, keepdims=True)
    )

    near_grads, far_grads, grad_w_in_t = gather_members(middle_grad.astype(bf16), grad_w_in_t)
    grad_w_in = jnp.swapaxes(grad_w_in_t, 1, 2)
    grad_blocks = [item for pair in zip(near_grads, far_grads) for item in pair]
    mixed_grad, output_part = output_back(grad_blocks, mixed, w_output)
    output_near = halve(output_part, 0)
    joined_grad, score_grad = attend_back(joined, mixed_grad, probs, head_size)
    output_near, joined_grad, token_blocks = lax.optimization_barrier((output_near, joined_grad, token_blocks))
    locals_ = []
    for half in range(2):
        columns = normed_low[:, half * (width // 2) : (half + 1) * (width // 2)]
        locals_.append(jnp.einsum("td,tc->dc", columns, joined_grad, preferred_element_type=f32).astype(bf16))
    locals_, joined_grad, score_grad = lax.optimization_barrier((locals_, joined_grad, score_grad))
    first_near = halve(locals_[0], 0)
    second_near = halve(locals_[1], 0)
    attn_partial = jnp.einsum("tc,dc->td", joined_grad, w_joined, preferred_element_type=f32)
    attn_pairs = attn_partial.reshape(member_count // 2, 2, tok_dev, width)
    attn_hop = core_hop(attn_pairs[:, 0], attn_pairs[:, 1])
    all_tokens = jnp.concatenate(token_blocks, axis=0).astype(f32)
    gain_partial = jnp.sum(attn_partial * (all_tokens * root_inverse(all_tokens)), axis=0, keepdims=True)
    bucket_part = bucket_grad(moved_table, score_grad, rel_bias.shape[0])
    first_near, attn_hop, bucket_part, gain_partial, output_near = lax.optimization_barrier(
        (first_near, attn_hop, bucket_part, gain_partial, output_near)
    )
    bucket_row = lax.dynamic_update_slice(
        jnp.zeros((1, width), f32), bucket_part.reshape(1, -1), (0, member * bucket_part.size)
    )
    small = jnp.concatenate([grad_gain_moe, gain_partial, bucket_row, grad_router_t], axis=0)
    for axis in ("mp", "dp"):
        for bit in reversed(range(bit_count(axis))):
            small = small + swap(small, axis, 1 << bit)
    attn_grad = scatter_rest(*attn_hop)
    grad_w_output = last_step(sum_rest(output_near))
    grad_joined = jnp.concatenate([last_step(sum_rest_direct(first_near)), last_step(sum_rest_direct(second_near))], axis=0)
    grad_w_query, grad_w_key, grad_w_value = [
        grad_joined[:, part * head_cols : (part + 1) * head_cols] for part in range(3)
    ]
    own_tokens = tokens.astype(f32)
    own_root = root_inverse(own_tokens)
    own_unit = own_tokens * own_root
    scaled = attn_grad * gain_attn
    input_grad = (
        middle_grad + own_root * (scaled - own_unit * jnp.mean(scaled * own_unit, axis=-1, keepdims=True))
    ).astype(bf16)
    grad_rel_bias = lax.dynamic_slice(small[2:3], (0, member * bucket_part.size), (1, bucket_part.size))
    grad_rel_bias = grad_rel_bias.reshape(bucket_part.shape)
    return (
        block_out,
        input_grad,
        small[1],
        grad_w_query,
        grad_w_key,
        grad_w_value,
        grad_w_output,
        grad_rel_bias,
        small[0],
        small[3:].T,
        grad_w_in,
        grad_w_out,
    )


def solution(mesh):
    in_specs = (
        P(("dp", "mp"), None),
        P(),
        P(None, "mp"),
        P(None, "mp"),
        P(None, "mp"),
        P("mp", None),
        P(None, "mp"),
        P(),
        P(),
        P(),
        P("dp", None, "mp"),
        P("dp", "mp", None),
        P(("dp", "mp")),
        P(("dp", "mp")),
        P(("dp", "mp"), None),
    )
    out_specs = (
        P(("dp", "mp"), None),
        P(("dp", "mp"), None),
        P(),
        P(None, "mp"),
        P(None, "mp"),
        P(None, "mp"),
        P("mp", None),
        P(None, "mp"),
        P(),
        P(),
        P("dp", None, "mp"),
        P("dp", "mp", None),
    )
    return jax.shard_map(shards, mesh=mesh, in_specs=in_specs, out_specs=out_specs, check_vma=False)
```

```python
import functools

import jax
import jax.numpy as jnp
import numpy as np
from jax import lax
from jax.experimental import pallas as pl
from jax.experimental.pallas import tpu as pltpu
from jax.sharding import PartitionSpec as P

norm_eps = 1e-06
highest = lax.Precision.HIGHEST
bf16 = jnp.bfloat16
f32 = jnp.float32
LANES = 128
MIB = 1 << 20
small_cost = pl.CostEstimate(flops=0, bytes_accessed=2048, transcendentals=0)


def swap(block, axis, offset):
    size = lax.axis_size(axis)
    return lax.ppermute(block, axis, [(i, i ^ offset) for i in range(size)])


def bit_count(axis):
    return lax.axis_size(axis).bit_length() - 1


def gather_members(block, beside):
    held = [block]
    mirrored = [swap(block, "mp", 1)]
    bits = bit_count("mp")
    for bit in reversed(range(1, bits)):
        others = [swap(item, "mp", 1 << bit) for item in held]
        if bit == bits - 1:
            others, beside = lax.optimization_barrier((others, beside))
        held = [item for pair in zip(held, others) for item in pair]
    return held, mirrored + [swap(item, "mp", 1) for item in held[1:]], beside


def core_hop(keep, send):
    return keep, swap(send.astype(bf16), "mp", 1)


def scatter_rest(keep, received, beside=None):
    held = keep.astype(f32) + received.astype(f32)
    for bit in range(1, bit_count("mp")):
        halves = held.reshape((-1, 2) + held.shape[1:])
        got = swap(halves[:, 1].astype(bf16), "mp", 1 << bit)
        if beside is not None and bit == 1:
            got, beside = lax.optimization_barrier((got, beside))
        held = halves[:, 0] + got.astype(f32)
    return held[0] if beside is None else (held[0], beside)


def exchange_groups(buffer):
    return lax.all_to_all(buffer, "dp", split_axis=0, concat_axis=0, tiled=True)


def halve(held, bit):
    mine = (lax.axis_index("dp") >> bit) & 1
    halves = held.reshape(2, held.shape[0] // 2, held.shape[1])
    got = swap(lax.dynamic_index_in_dim(halves, 1 - mine, 0, keepdims=False), "dp", 1 << bit)
    return lax.dynamic_index_in_dim(halves, mine, 0, keepdims=False), got


def joined_halves(keep, got):
    return (keep.astype(f32) + got.astype(f32)).astype(bf16)


def sum_rest(near):
    held = joined_halves(*near)
    for bit in range(1, bit_count("dp")):
        held = joined_halves(*halve(held, bit))
    held = held[None]
    for bit in reversed(range(1, bit_count("dp"))):
        held = jnp.concatenate([held, swap(held, "dp", 1 << bit)], axis=0)
    return held


def sum_rest_direct(near):
    rest = lax.axis_size("dp") // 2
    bits = bit_count("dp")
    mine = lax.axis_index("dp") >> 1
    held = joined_halves(*near)
    blocks = held.reshape(rest, held.shape[0] // rest, held.shape[1])
    reverse = [sum(((q >> bit) & 1) << (bits - 2 - bit) for bit in range(bits - 1)) for q in range(rest)]
    place = jnp.int32(0)
    for bit in range(bits - 1):
        place = place | (((mine >> bit) & 1) << (bits - 2 - bit))
    total = lax.dynamic_index_in_dim(blocks, place, 0, keepdims=False).astype(f32)
    got = [
        swap(lax.dynamic_index_in_dim(blocks, place ^ reverse[offset], 0, keepdims=False), "dp", 2 * offset)
        for offset in range(1, rest)
    ]
    for item in got:
        total = total + item.astype(f32)
    own = total.astype(bf16)
    gathered = {0: own}
    for offset in range(1, rest):
        gathered[reverse[offset]] = swap(own, "dp", 2 * offset)
    return jnp.stack([gathered[at] for at in range(rest)])


def last_step(own_half):
    other = swap(own_half, "dp", 1)
    both = jnp.stack([own_half, other])
    bits = bit_count("dp")
    me = lax.axis_index("dp")
    rows = []
    for half in range(2):
        for block in range(1 << (bits - 1)):
            at = jnp.int32(0)
            for bit in range(1, bits):
                differs = ((block >> (bits - 1 - bit)) & 1) ^ ((me >> bit) & 1)
                at = at + (differs << (bits - 1 - bit))
            rows.append(both[half ^ (me & 1), at])
    return jnp.concatenate(rows, axis=0).astype(f32)


def bias_kernel(block, shift_ref, table_ref, bucket_ref, bias_ref, moved_ref):
    shift = shift_ref[0]
    for at in range(table_ref.shape[1] // block):
        source = pl.multiple_of((at ^ shift) * block, block)
        labels = table_ref[:, pl.ds(source, block)]
        columns = slice(at * block, (at + 1) * block)
        moved_ref[:, columns] = labels
        for head in range(bucket_ref.shape[0]):
            row = jnp.broadcast_to(bucket_ref[head : head + 1, :], labels.shape)
            bias_ref[head, :, columns] = jnp.take_along_axis(row, labels, axis=1, mode="promise_in_bounds")


def make_bias(table, bucket_rows, shift, block):
    seq_len = table.shape[0]
    heads = bucket_rows.shape[0]
    return pl.pallas_call(
        functools.partial(bias_kernel, block),
        grid_spec=pltpu.PrefetchScalarGridSpec(
            num_scalar_prefetch=1,
            grid=(seq_len // block,),
            in_specs=[
                pl.BlockSpec((block, seq_len), lambda i, s: (i ^ s[0], 0)),
                pl.BlockSpec((heads, LANES), lambda i, s: (0, 0)),
            ],
            out_specs=[
                pl.BlockSpec((heads, block, seq_len), lambda i, s: (0, i, 0)),
                pl.BlockSpec((block, seq_len), lambda i, s: (i, 0)),
            ],
        ),
        out_shape=[
            jax.ShapeDtypeStruct((heads, seq_len, seq_len), f32),
            pltpu.HBM((seq_len, seq_len), jnp.int32),
        ],
        compiler_params=pltpu.CompilerParams(vmem_limit_bytes=8 * MIB),
        cost_estimate=small_cost,
        name="bias_lookup",
    )(shift, table, bucket_rows)


def bucket_kernel(buckets, table_ref, grad_ref, out_ref):
    seqs, heads, rows, seq_len = grad_ref.shape

    @pl.when(pl.program_id(0) == 0)
    def _():
        out_ref[...] = jnp.zeros_like(out_ref)

    labels = lax.broadcasted_iota(jnp.int32, (buckets, seq_len), 0).astype(f32).astype(bf16)
    table = table_ref[...].astype(f32).astype(bf16)
    one, zero = jnp.ones((), bf16), jnp.zeros((), bf16)
    onehot = jnp.concatenate([jnp.where(table[row : row + 1, :] == labels, one, zero) for row in range(rows)], axis=0)
    total = jnp.zeros((rows * buckets, heads * rows), f32)
    for seq in range(seqs):
        grads = grad_ref[seq].reshape(heads * rows, seq_len)
        total += lax.dot_general(onehot, grads, (((1,), (1,)), ((), ())), preferred_element_type=f32)
    own_row = lax.broadcasted_iota(jnp.int32, (rows, buckets, heads * rows), 0)
    its_row = lax.broadcasted_iota(jnp.int32, (rows, buckets, heads * rows), 2) % rows
    kept = jnp.where(own_row == its_row, total.reshape(rows, buckets, heads * rows), 0.0)
    out_ref[...] += jnp.sum(kept, axis=0)


def bucket_grad(table, score_grad, buckets):
    seqs, heads, seq_len, _ = score_grad.shape
    rows = 32
    out = pl.pallas_call(
        functools.partial(bucket_kernel, buckets),
        grid=(seq_len // rows,),
        in_specs=[
            pl.BlockSpec((rows, seq_len), lambda i: (i, 0)),
            pl.BlockSpec((seqs, heads, rows, seq_len), lambda i: (0, 0, i, 0)),
        ],
        out_specs=pl.BlockSpec((buckets, heads * rows), lambda i: (0, 0)),
        out_shape=jax.ShapeDtypeStruct((buckets, heads * rows), f32),
        compiler_params=pltpu.CompilerParams(vmem_limit_bytes=16 * MIB),
        cost_estimate=small_cost,
        name="bucket_grad",
    )(table, score_grad)
    return jnp.sum(out.reshape(buckets, heads, rows), axis=2)


def attend_kernel(
    head_size,
    *refs,
):
    *token_refs, gain_ref, query_ref, key_ref, value_ref, bias_ref, normed_ref, joined_ref, mixed_ref, probs_ref = refs
    seq_len, width = joined_ref.shape
    head_cols = width // 3
    pair_heads = bias_ref.shape[0]
    pair_cols = pair_heads * head_size
    block = token_refs[0].shape[0]

    @pl.when(pl.program_id(0) == 0)
    def _():
        for at, token_ref in enumerate(token_refs):
            values = token_ref[...].astype(f32)
            root = lax.rsqrt(jnp.mean(values * values, axis=-1, keepdims=True) + norm_eps)
            normed_ref[at * block : (at + 1) * block, :] = (values * root * gain_ref[...]).astype(bf16)
        for part, weight_ref in enumerate((query_ref, key_ref, value_ref)):
            joined_ref[:, part * head_cols : (part + 1) * head_cols] = jnp.dot(
                normed_ref[...], weight_ref[...], preferred_element_type=f32
            ).astype(bf16)

    start = pl.program_id(0) * pair_cols
    columns = [
        joined_ref[:, pl.ds(pl.multiple_of(start + part * head_cols, pair_cols), pair_cols)] for part in range(3)
    ]
    rows = min(512, seq_len)
    for chunk in range(seq_len // rows):
        picked = slice(chunk * rows, (chunk + 1) * rows)
        outs = []
        for head in range(pair_heads):
            cols = slice(head * head_size, (head + 1) * head_size)
            scores = lax.dot_general(
                columns[0][picked, cols], columns[1][:, cols], (((1,), (1,)), ((), ())), preferred_element_type=f32
            )
            scores = scores + bias_ref[head, picked, :]
            expo = jnp.exp(scores - jnp.max(scores, axis=-1, keepdims=True))
            probs = (expo * (1.0 / jnp.sum(expo, axis=-1, keepdims=True))).astype(bf16)
            probs_ref[0, head, picked, :] = probs
            outs.append(jnp.dot(probs, columns[2][:, cols], preferred_element_type=f32))
        mixed_ref[picked, :] = jnp.concatenate(outs, axis=1).astype(bf16)


def attend(blocks, gain, w_query, w_key, w_value, bias, head_size):
    heads, seq_len, _ = bias.shape
    block, width = blocks[0].shape
    head_cols = w_query.shape[1]
    pair = min(heads, LANES // head_size)
    weight = pl.BlockSpec((width, head_cols), lambda h: (0, 0))
    gain, *weights = [pltpu.with_memory_space_constraint(item, pltpu.HBM) for item in (gain, w_query, w_key, w_value)]
    blocks = [pltpu.with_memory_space_constraint(blocks[0], pltpu.HBM)] + blocks[1:]
    return pl.pallas_call(
        functools.partial(attend_kernel, head_size),
        grid=(heads // pair,),
        in_specs=[pl.BlockSpec((block, width), lambda h: (0, 0))] * len(blocks)
        + [
            pl.BlockSpec((1, width), lambda h: (0, 0)),
            weight,
            weight,
            weight,
            pl.BlockSpec((pair, seq_len, seq_len), lambda h: (h, 0, 0)),
        ],
        out_specs=[
            pl.BlockSpec((seq_len, width), lambda h: (0, 0)),
            pl.BlockSpec((seq_len, 3 * head_cols), lambda h: (0, 0)),
            pl.BlockSpec((seq_len, pair * head_size), lambda h: (0, h)),
            pl.BlockSpec((1, pair, seq_len, seq_len), lambda h: (0, h, 0, 0)),
        ],
        out_shape=[
            pltpu.HBM((seq_len, width), bf16),
            pltpu.HBM((seq_len, 3 * head_cols), bf16),
            jax.ShapeDtypeStruct((seq_len, head_cols), bf16),
            pltpu.HBM((1, heads, seq_len, seq_len), bf16),
        ],
        compiler_params=pltpu.CompilerParams(vmem_limit_bytes=18 * MIB),
        cost_estimate=small_cost,
        name="attend",
    )(*blocks, gain, *weights, bias)


def output_back_kernel(*refs):
    *block_refs, mixed_ref, weight_ref, mixed_grad_ref, part_ref = refs
    rows = jnp.concatenate([block_ref[...] for block_ref in block_refs], axis=0)
    part_ref[...] = lax.dot_general(
        mixed_ref[...], rows, (((0,), (0,)), ((), ())), preferred_element_type=f32
    ).astype(bf16)
    mixed_grad_ref[...] = lax.dot_general(
        rows, weight_ref[...], (((1,), (1,)), ((), ())), preferred_element_type=f32
    ).astype(bf16)


def output_back(blocks, mixed, weight):
    tokens, head_cols = mixed.shape
    width = weight.shape[1]
    return pl.pallas_call(
        output_back_kernel,
        out_shape=[
            jax.ShapeDtypeStruct((tokens, head_cols), bf16),
            jax.ShapeDtypeStruct((head_cols, width), bf16),
        ],
        compiler_params=pltpu.CompilerParams(vmem_limit_bytes=16 * MIB),
        cost_estimate=small_cost,
        name="output_back",
    )(*blocks, mixed, weight)


def attend_back_kernel(head_size, joined_ref, grad_ref, probs_ref, out_ref, score_ref):
    seq_len, width = joined_ref.shape
    head_cols = width // 3
    pair_heads = probs_ref.shape[1]
    pair_cols = pair_heads * head_size
    start = pl.program_id(1) * pair_cols

    def place(part):
        return pl.ds(pl.multiple_of(start + part * head_cols, pair_cols), pair_cols)

    queries, keys, values = [joined_ref[:, place(part)] for part in range(3)]
    grads = grad_ref[...]
    queries_t, grads_t = queries.T, grads.T
    rows = min(512, seq_len)
    query_parts = []
    key_t = [jnp.zeros((head_size, seq_len), f32) for _ in range(pair_heads)]
    value_t = [jnp.zeros((head_size, seq_len), f32) for _ in range(pair_heads)]
    for chunk in range(seq_len // rows):
        picked = slice(chunk * rows, (chunk + 1) * rows)
        outs = []
        for head in range(pair_heads):
            cols = slice(head * head_size, (head + 1) * head_size)
            probs_low = probs_ref[0, head, picked, :]
            probs = probs_low.astype(f32)
            prob_grad = lax.dot_general(
                grads[picked, cols], values[:, cols], (((1,), (1,)), ((), ())), preferred_element_type=f32
            )
            weighted = jnp.sum(probs * prob_grad, axis=-1, keepdims=True)
            score_grad = (probs * (prob_grad - weighted)).astype(bf16)
            score_ref[0, head, picked, :] = score_grad
            outs.append(jnp.dot(score_grad, keys[:, cols], preferred_element_type=f32))
            key_t[head] += jnp.dot(queries_t[cols, picked], score_grad, preferred_element_type=f32)
            value_t[head] += jnp.dot(grads_t[cols, picked], probs_low, preferred_element_type=f32)
        out_ref[picked, place(0)] = jnp.concatenate(outs, axis=1).astype(bf16)
    out_ref[:, place(1)] = jnp.concatenate(key_t, axis=0).T.astype(bf16)
    out_ref[:, place(2)] = jnp.concatenate(value_t, axis=0).T.astype(bf16)


def attend_back(joined, mixed_grad, probs, head_size):
    seqs, heads, seq_len, _ = probs.shape
    tokens, width = joined.shape
    pair = min(heads, LANES // head_size)
    return pl.pallas_call(
        functools.partial(attend_back_kernel, head_size),
        grid=(seqs, heads // pair),
        in_specs=[
            pl.BlockSpec((seq_len, width), lambda s, h: (s, 0)),
            pl.BlockSpec((seq_len, pair * head_size), lambda s, h: (s, h)),
            pl.BlockSpec((1, pair, seq_len, seq_len), lambda s, h: (s, h, 0, 0)),
        ],
        out_specs=[
            pl.BlockSpec((seq_len, width), lambda s, h: (s, 0)),
            pl.BlockSpec((1, pair, seq_len, seq_len), lambda s, h: (s, h, 0, 0)),
        ],
        out_shape=[
            jax.ShapeDtypeStruct((tokens, width), bf16),
            pltpu.HBM((seqs, heads, seq_len, seq_len), bf16),
        ],
        compiler_params=pltpu.CompilerParams(vmem_limit_bytes=16 * MIB),
        cost_estimate=small_cost,
        name="attend_back",
    )(joined, mixed_grad, probs)


gelu_scale = float(np.sqrt(2.0 / np.pi))


def gelu_parts(pre):
    bent = jnp.tanh(gelu_scale * (pre + 0.044715 * pre * pre * pre))
    return 0.5 * pre * (1.0 + bent), bent


def gelu_slope(pre):
    _, bent = gelu_parts(pre)
    return 0.5 * (1.0 + bent) + 0.5 * pre * (1.0 - bent * bent) * gelu_scale * (1.0 + 0.134145 * pre * pre)


def expert_kernel(cuts, middle_step, members, *refs):
    block_refs = refs[:members]
    order_ref, first_ref, second_ref, *middle_refs, inner_ref, rows_out, keep_ref, send_ref = refs[members:-6]
    first_held, second_held, inner_held, rows_ref, arrived, left = refs[-6:]
    half = members // 2
    all_rows, piece = block_refs[0].shape
    experts, _, picked = order_ref.shape
    expert_rows = picked // cuts
    loads = []
    for expert in range(experts):
        for at, (source, held) in enumerate(((first_ref, first_held), (second_ref, second_held))):
            loads.append(pltpu.make_async_copy(source.at[expert], held.at[expert], arrived.at[2 * expert + at]))
    for load in loads[:2]:
        load.start()
    places = [
        (order_ref[expert] == lax.broadcasted_iota(jnp.int32, (all_rows, picked), 0)).astype(f32)
        for expert in range(experts)
    ]
    sorting = jnp.concatenate([place.T for place in places], axis=0).astype(bf16)
    for member in range(members):
        moved = jnp.dot(sorting, block_refs[member][...], preferred_element_type=f32).astype(bf16)
        for expert in range(experts):
            for cut in range(cuts):
                source = expert * picked + cut * expert_rows
                rows_ref[
                    expert, member * expert_rows : (member + 1) * expert_rows, cut * piece : (cut + 1) * piece
                ] = moved[source : source + expert_rows]
    stores = [pltpu.make_async_copy(rows_ref, rows_out, left.at[experts])]
    stores[0].start()
    results = []
    for expert in range(experts):
        loads[2 * expert].wait()
        if 2 * expert + 2 < len(loads):
            loads[2 * expert + 2].start()
            loads[2 * expert + 3].start()
        inner = lax.dot_general(
            rows_ref[expert], first_held[expert], (((1,), (1,)), ((), ())), preferred_element_type=f32
        )
        inner = middle_step(expert, inner, *middle_refs)
        inner_held[expert] = inner
        stores.append(pltpu.make_async_copy(inner_held.at[expert], inner_ref.at[expert], left.at[expert]))
        stores[-1].start()
        loads[2 * expert + 1].wait()
        results.append(jnp.dot(inner, second_held[expert], preferred_element_type=f32).astype(bf16))
    unsorting = jnp.concatenate([place.astype(bf16) for place in places], axis=1)
    for member in range(members):
        parts = [
            result[member * expert_rows : (member + 1) * expert_rows, cut * piece : (cut + 1) * piece]
            for result in results
            for cut in range(cuts)
        ]
        placed = jnp.dot(unsorting, jnp.concatenate(parts, axis=0), preferred_element_type=f32).astype(bf16)
        target, at = (keep_ref, member) if member < half else (send_ref, member - half)
        target[at] = placed
    for store in stores:
        store.wait()


def forward_step(expert, inner, pre_ref):
    pre_ref[expert] = inner
    return gelu_parts(inner)[0].astype(bf16)


def backward_step(expert, inner, pre_ref):
    return (inner.astype(bf16).astype(f32) * gelu_slope(pre_ref[expert])).astype(bf16)


def run_experts(blocks, order, first, second, cuts, pre=None):
    members = len(blocks)
    experts, units, width = first.shape
    picked = order.shape[1]
    rows = members * (picked // cuts)
    part = jax.ShapeDtypeStruct((members // 2,) + blocks[0].shape, bf16)
    inside = pl.BlockSpec(memory_space=pltpu.VMEM)
    outside = pl.BlockSpec(memory_space=pltpu.HBM)
    first, second = [pltpu.with_memory_space_constraint(item, pltpu.HBM) for item in (first, second)]
    out_specs = [outside, outside, inside, inside]
    in_specs = [inside] * (members + 1) + [outside, outside]
    operands = [*blocks, order[:, None, :], first, second]
    out_shape = [pltpu.HBM((experts, rows, units), bf16), pltpu.HBM((experts, rows, width), bf16), part, part]
    if pre is None:
        step, name = forward_step, "experts"
        out_shape.insert(0, jax.ShapeDtypeStruct((experts, rows, units), f32))
        out_specs.insert(0, inside)
    else:
        step, name = backward_step, "experts_back"
        in_specs.append(inside)
        operands.append(pre)
    return pl.pallas_call(
        functools.partial(expert_kernel, cuts, step, members),
        in_specs=in_specs,
        out_specs=out_specs,
        out_shape=out_shape,
        scratch_shapes=[
            pltpu.VMEM((experts, units, width), bf16),
            pltpu.VMEM((experts, units, width), bf16),
            pltpu.VMEM((experts, rows, units), bf16),
            pltpu.VMEM((experts, rows, width), bf16),
            pltpu.SemaphoreType.DMA((2 * experts,)),
            pltpu.SemaphoreType.DMA((experts + 1,)),
        ],
        compiler_params=pltpu.CompilerParams(vmem_limit_bytes=22 * MIB),
        cost_estimate=small_cost,
        name=name,
    )(*operands)


def root_inverse(values):
    return lax.rsqrt(jnp.mean(values * values, axis=-1, keepdims=True) + norm_eps)


def shards(
    tokens,
    gain_attn,
    w_query,
    w_key,
    w_value,
    w_output,
    rel_bias,
    bucket_table,
    gain_moe,
    router,
    w_in,
    w_out,
    routes,
    slots,
    cotangent,
):
    group_count = lax.axis_size("dp")
    member_count = lax.axis_size("mp")
    member = lax.axis_index("mp")
    tok_dev, width = tokens.shape
    expert_local = w_in.shape[0]
    expert_count = expert_local * group_count
    capacity = max(2, (5 * tok_dev + 4 * expert_count - 1) // (4 * expert_count))
    seq_len = bucket_table.shape[0]
    head_cols = w_query.shape[1]
    head_local = rel_bias.shape[1]
    head_size = head_cols // head_local
    group_tokens = tok_dev * member_count
    seq_members = seq_len // tok_dev

    bucket_rows = jnp.pad(rel_bias.T, ((0, 0), (0, LANES - rel_bias.shape[0])))
    shift = (member % seq_members).astype(jnp.int32)[None]
    bias, moved_table = make_bias(bucket_table, bucket_rows, shift, tok_dev)
    near_tokens, far_tokens, (bias, moved_table) = gather_members(tokens, (bias, moved_table))
    token_blocks = [item for pair in zip(near_tokens, far_tokens) for item in pair]
    sequences = [
        attend(token_blocks[at : at + seq_members], gain_attn[None], w_query, w_key, w_value, bias, head_size)
        for at in range(0, member_count, seq_members)
    ]
    normed_low, joined, mixed, probs = [
        parts[0] if len(parts) == 1 else jnp.concatenate(parts, axis=0) for parts in zip(*sequences)
    ]
    mixed_pairs = mixed.reshape(member_count // 2, 2, tok_dev, head_cols)

    def project(rows):
        return jnp.einsum("stc,cd->std", rows, w_output, preferred_element_type=f32)

    attn_got = swap(project(mixed_pairs[:, 1]).astype(bf16), "mp", 1)
    attn = scatter_rest(project(mixed_pairs[:, 0]), attn_got)
    middle = tokens.astype(f32) + attn

    middle_root = root_inverse(middle)
    unit_moe = middle * middle_root
    moe_low = (unit_moe * gain_moe).astype(bf16)
    moe_rows = moe_low.astype(f32)
    router_t = router.T
    logits = lax.dot_general(
        moe_rows, router_t, (((1,), (1,)), ((), ())), precision=highest, preferred_element_type=f32
    )
    router_probs = jax.nn.softmax(logits, axis=-1)
    route_hot = (routes[:, None] == jnp.arange(expert_count, dtype=jnp.int32)[None, :]).astype(f32)
    gate_prob = jnp.sum(router_probs * route_hot, axis=-1, keepdims=True)

    chunk_slots = expert_local * capacity
    cuts = 1
    while cuts * chunk_slots % 8 != 0:
        cuts *= 2
    piece = width // cuts
    chunk_rows = cuts * chunk_slots
    all_rows = group_count * chunk_rows
    row_index = jnp.arange(all_rows, dtype=jnp.int32)
    row_chunk, row_cut, row_slot = (
        row_index // chunk_rows,
        (row_index // chunk_slots) % cuts,
        row_index % chunk_slots,
    )
    target = jnp.where(slots < capacity, routes * capacity + slots, -1)
    wanted = row_chunk * chunk_slots + row_slot
    hit = (wanted[:, None, None] == target[None, None, :]) & (
        row_cut[:, None, None] == jnp.arange(cuts, dtype=jnp.int32)[None, :, None]
    )
    placement = hit.astype(bf16).reshape(all_rows, cuts * tok_dev)

    def cut_rows(rows):
        return jnp.concatenate([rows[:, c * piece : (c + 1) * piece] for c in range(cuts)], axis=0)

    def join_rows(rows):
        return jnp.concatenate([rows[c * tok_dev : (c + 1) * tok_dev] for c in range(cuts)], axis=1)

    def send_rows(rows):
        return exchange_groups(jnp.dot(placement, cut_rows(rows), preferred_element_type=f32).astype(bf16))

    def place_back(back):
        rows = lax.dot_general(placement, back, (((0,), (0,)), ((), ())), preferred_element_type=f32)
        return join_rows(rows)

    order = np.arange(all_rows).reshape(group_count, cuts, expert_local, capacity).transpose(2, 1, 0, 3)
    order = jnp.asarray(order.reshape(expert_local, -1), jnp.int32)
    w_in_t = jnp.swapaxes(w_in, 1, 2)

    upstream = cotangent.astype(f32)
    sent = send_rows(moe_low)
    grad_sent = send_rows((gate_prob * upstream).astype(bf16))
    w_joined = jnp.concatenate([w_query, w_key, w_value], axis=1)
    near_rows, far_rows, (grad_sent, w_joined) = gather_members(sent, (grad_sent, w_joined))

    pre, hidden, expert_in, value_keep, value_send = run_experts(near_rows + far_rows, order, w_in_t, w_out, cuts)
    near_rows, far_rows, (value_keep, value_send) = gather_members(grad_sent, (value_keep, value_send))
    value_hop = core_hop(value_keep, value_send)
    pre_grad, result_grad, *rows_blocks = run_experts(near_rows + far_rows, order, w_out, w_in_t, cuts, pre)
    value_sum, rows_blocks = scatter_rest(*value_hop, beside=rows_blocks)
    rows_hop = core_hop(*rows_blocks)
    value_back = exchange_groups(value_sum.astype(bf16))
    rows_sum, value_back = scatter_rest(*rows_hop, beside=value_back)
    rows_back = exchange_groups(rows_sum.astype(bf16))
    grad_w_out = jnp.einsum("jrf,jrd->jfd", hidden, result_grad, preferred_element_type=f32)
    rows_back, grad_w_out = lax.optimization_barrier((rows_back, grad_w_out))
    grad_w_in_t = jnp.einsum("jrf,jrd->jfd", pre_grad, expert_in, preferred_element_type=f32)
    combined = place_back(value_back)
    moe_grad = place_back(rows_back)

    block_out = (middle + gate_prob * combined).astype(bf16)
    gate_grad = jnp.sum(upstream * combined, axis=-1, keepdims=True)
    logit_grad = router_probs * (route_hot * gate_grad - gate_prob * gate_grad)
    grad_router_t = lax.dot_general(
        logit_grad, moe_rows, (((0,), (0,)), ((), ())), precision=highest, preferred_element_type=f32
    )
    moe_grad = moe_grad + jnp.dot(logit_grad, router_t, precision=highest, preferred_element_type=f32)
    grad_gain_moe = jnp.sum(moe_grad * unit_moe, axis=0, keepdims=True)
    scaled = moe_grad * gain_moe
    middle_grad = upstream + middle_root * (
        scaled - unit_moe * jnp.mean(scaled * unit_moe, axis=-1, keepdims=True)
    )

    near_grads, far_grads, grad_w_in_t = gather_members(middle_grad.astype(bf16), grad_w_in_t)
    grad_w_in = jnp.swapaxes(grad_w_in_t, 1, 2)
    grad_blocks = [item for pair in zip(near_grads, far_grads) for item in pair]
    mixed_grad, output_part = output_back(grad_blocks, mixed, w_output)
    output_near = halve(output_part, 0)
    joined_grad, score_grad = attend_back(joined, mixed_grad, probs, head_size)
    output_near, joined_grad, token_blocks = lax.optimization_barrier((output_near, joined_grad, token_blocks))
    locals_ = []
    for half in range(2):
        columns = normed_low[:, half * (width // 2) : (half + 1) * (width // 2)]
        locals_.append(jnp.einsum("td,tc->dc", columns, joined_grad, preferred_element_type=f32).astype(bf16))
    locals_, joined_grad, score_grad = lax.optimization_barrier((locals_, joined_grad, score_grad))
    first_near = halve(locals_[0], 0)
    second_near = halve(locals_[1], 0)
    attn_partial = jnp.einsum("tc,dc->td", joined_grad, w_joined, preferred_element_type=f32)
    attn_pairs = attn_partial.reshape(member_count // 2, 2, tok_dev, width)
    attn_hop = core_hop(attn_pairs[:, 0], attn_pairs[:, 1])
    all_tokens = jnp.concatenate(token_blocks, axis=0).astype(f32)
    gain_partial = jnp.sum(attn_partial * (all_tokens * root_inverse(all_tokens)), axis=0, keepdims=True)
    bucket_part = bucket_grad(moved_table, score_grad, rel_bias.shape[0])
    first_near, attn_hop, bucket_part, output_near = lax.optimization_barrier(
        (first_near, attn_hop, bucket_part, output_near)
    )
    bucket_row = lax.dynamic_update_slice(
        jnp.zeros((1, width), f32), bucket_part.reshape(1, -1), (0, member * bucket_part.size)
    )
    small = jnp.concatenate([grad_gain_moe, gain_partial, bucket_row, grad_router_t], axis=0)
    for axis in ("mp", "dp"):
        for bit in reversed(range(bit_count(axis))):
            small = small + swap(small, axis, 1 << bit)
    attn_grad = scatter_rest(*attn_hop)
    grad_w_output = last_step(sum_rest(output_near))
    grad_joined = jnp.concatenate([last_step(sum_rest_direct(first_near)), last_step(sum_rest_direct(second_near))], axis=0)
    grad_w_query, grad_w_key, grad_w_value = [
        grad_joined[:, part * head_cols : (part + 1) * head_cols] for part in range(3)
    ]
    own_tokens = tokens.astype(f32)
    own_root = root_inverse(own_tokens)
    own_unit = own_tokens * own_root
    scaled = attn_grad * gain_attn
    input_grad = (
        middle_grad + own_root * (scaled - own_unit * jnp.mean(scaled * own_unit, axis=-1, keepdims=True))
    ).astype(bf16)
    grad_rel_bias = lax.dynamic_slice(small[2:3], (0, member * bucket_part.size), (1, bucket_part.size))
    grad_rel_bias = grad_rel_bias.reshape(bucket_part.shape)
    return (
        block_out,
        input_grad,
        small[1],
        grad_w_query,
        grad_w_key,
        grad_w_value,
        grad_w_output,
        grad_rel_bias,
        small[0],
        small[3:].T,
        grad_w_in,
        grad_w_out,
    )


def solution(mesh):
    in_specs = (
        P(("dp", "mp"), None),
        P(),
        P(None, "mp"),
        P(None, "mp"),
        P(None, "mp"),
        P("mp", None),
        P(None, "mp"),
        P(),
        P(),
        P(),
        P("dp", None, "mp"),
        P("dp", "mp", None),
        P(("dp", "mp")),
        P(("dp", "mp")),
        P(("dp", "mp"), None),
    )
    out_specs = (
        P(("dp", "mp"), None),
        P(("dp", "mp"), None),
        P(),
        P(None, "mp"),
        P(None, "mp"),
        P(None, "mp"),
        P("mp", None),
        P(None, "mp"),
        P(),
        P(),
        P("dp", None, "mp"),
        P("dp", "mp", None),
    )
    return jax.shard_map(shards, mesh=mesh, in_specs=in_specs, out_specs=out_specs, check_vma=False)
```
